32 devices in a mesh: dp: 8 (over y, x, core), tensor: 4 (over z).
Axes of the slice: x: 2, y: 2, z: 4, core: 2. Of those that a mesh axis runs over, the one named last changes fastest.
Arguments:
- tokens: bfloat16 [64, 256, 1152], P('dp', 'tensor'), may hold values from -8 to 8
- timesteps: int32 [64], P('dp'), may hold values from 0 to 999
- labels: int32 [64], P('dp'), may hold values from 0 to 999
- patch_cells: int32 [64, 256], P('dp'), may hold values from 0 to 255, each once within a row
- class_table: bfloat16 [1000, 1152], P(None, 'tensor'), may hold values from -6 to 6
- ada_weight: bfloat16 [1152, 6, 1152], P('tensor', None, 'dp'), may hold values from -0.1875 to 0.1875
- ada_bias: bfloat16 [6, 1152], replicated, may hold values from -4 to 4
- qkv_weight: bfloat16 [1152, 3, 1152], P('dp', None, 'tensor'), may hold values from -0.1875 to 0.1875
- qkv_bias: bfloat16 [3, 1152], P(None, 'tensor'), may hold values from -3 to 3
- q_gain: bfloat16 [72], replicated, may hold values from 0.796875 to 2
- k_gain: bfloat16 [72], replicated, may hold values from 0.796875 to 2
- out_weight: bfloat16 [1152, 1152], P('tensor', 'dp'), may hold values from -0.75 to 0.75
- out_bias: bfloat16 [1152], replicated, may hold values from -3 to 3
- gate_up_weight: bfloat16 [1152, 2, 3072], P('dp', None, 'tensor'), may hold values from -0.1875 to 0.1875
- gate_up_bias: bfloat16 [2, 3072], P(None, 'tensor'), may hold values from -3 to 3
- down_weight: bfloat16 [3072, 1152], P('tensor', 'dp'), may hold values from -0.109375 to 0.109375
- down_bias: bfloat16 [1152], replicated, may hold values from -3 to 3
- cotangent: bfloat16 [64, 256, 1152], P('dp', 'tensor'), may hold values from -8 to 8
Outputs:
- output: bfloat16 [64, 256, 1152], P('dp', 'tensor')
- tokens_grad: float32 [64, 256, 1152], P('dp', 'tensor')
- class_table_grad: float32 [1000, 1152], P(None, 'tensor')
- ada_weight_grad: float32 [1152, 6, 1152], P('tensor', None, 'dp')
- ada_bias_grad: float32 [6, 1152], replicated
- qkv_weight_grad: float32 [1152, 3, 1152], P('dp', None, 'tensor')
- qkv_bias_grad: float32 [3, 1152], P(None, 'tensor')
- q_gain_grad: float32 [72], replicated
- k_gain_grad: float32 [72], replicated
- out_weight_grad: float32 [1152, 1152], P('tensor', 'dp')
- out_bias_grad: float32 [1152], replicated
- gate_up_weight_grad: float32 [1152, 2, 3072], P('dp', None, 'tensor')
- gate_up_bias_grad: float32 [2, 3072], P(None, 'tensor')
- down_weight_grad: float32 [3072, 1152], P('tensor', 'dp')
- down_bias_grad: float32 [1152], replicated
The draws below stay inside these ranges and needn't reach their ends.
Inputs may be any that keep to these rules, and one draw needn't show every extreme that they name: `patch_cells`: each image's row holds every cell of the 16 x 16 patch grid once.
All inputs are finite; a program needn't handle non-finite values.
Results may differ from the reference program's by a relative error of at most 0.02.
Values may be sent and summed in bfloat16 or wider, within the bound.
No kernel may reach another device: no remote copies, remote signals or barrier semaphores. Data moves between devices by JAX's collectives and lax.ppermute only.
A program may use at most 112 MiB of HBM per device.

```python
import math
import jax
import jax.numpy as jnp
from jax import lax

D = 1152
HEAD_DIM = 72
FF = 3072
CLASSES = 1000
GRID = 16
PATCHES = 256
IMAGES = 64


def plant(entries, rng, least, largest):
    longest = entries.shape.index(max(entries.shape))
    spots = []
    for shift in (0, 1):
        where = [jax.random.randint(jax.random.fold_in(rng, axis), (), 0, length) for axis, length in enumerate(entries.shape)]
        where[longest] = (where[longest] + shift) % entries.shape[longest]
        spots.append(tuple(where))
    return entries.at[spots[0]].set(least).at[spots[1]].set(largest)


def spiked(values, stream_key, source, target, blocks, factor):
    owner, partner = [(jnp.arange(values.shape[position]) // (values.shape[position] // blocks)).reshape([-1 if axis == position else 1 for axis in range(values.ndim)]) for position in (source, target)]
    chosen = jax.random.permutation(stream_key, blocks)[partner]
    strong = (owner == chosen) | (owner == (partner + blocks // 2) % blocks)
    return jnp.where(strong, factor * values, values)


def levels(stream_key, dims, pieces, least, high):
    factor_of, own = 1.0, jax.random.fold_in(stream_key, 6)
    for dim, parts in pieces:
        heights = jnp.exp(jax.random.uniform(jax.random.fold_in(own, dim), (parts,), jnp.float32, least / len(pieces), high / len(pieces)))
        factor_of = factor_of * jnp.repeat(heights, dims[dim] // parts).reshape([-1 if axis == dim else 1 for axis in range(len(dims))])
    return factor_of


def bell_draw(own_key, dims, spread, bound, cuts=(), kind=jnp.bfloat16):
    factor_of = levels(own_key, dims, cuts, -0.22, 0.18) if cuts else 1.0
    values = jax.random.normal(own_key, dims, jnp.float32) * spread * factor_of
    return jnp.minimum(jnp.maximum(values, -bound), bound).astype(kind)


def heavy_noise(key, shape, scale, most, cuts, heavy, held_as=jnp.bfloat16):
    values = scale * jax.random.normal(key, shape, jnp.float32)
    if cuts:
        values = values * levels(key, shape, cuts, -0.22, 0.18)
    return jnp.clip(spiked(values, jax.random.fold_in(key, 3), *heavy), -most, most).astype(held_as)


def setup_inputs(seed: int = 0) -> dict:
    key_of = jax.random.split(jax.random.key(seed), 19)
    return {
        "tokens": heavy_noise(key_of[0], (IMAGES, PATCHES, D), 1.0, 8.0, ((0, 8), (1, 4)), (0, 2, 8, 2.0)),
        "timesteps": plant(jax.random.randint(key_of[1], (IMAGES,), 0, 1000), jax.random.fold_in(key_of[1], 1), 0, 999).astype(jnp.int32),
        "labels": plant(jax.random.randint(key_of[2], (IMAGES,), 0, CLASSES), jax.random.fold_in(key_of[2], 1), 0, CLASSES - 1).astype(jnp.int32),
        "patch_cells": jax.vmap(lambda own: jax.random.permutation(own, PATCHES))(jax.random.split(key_of[3], IMAGES)).reshape((IMAGES, PATCHES)).astype(jnp.int32),
        "class_table": bell_draw(key_of[4], (CLASSES, D), 1.0, 6.0, ((1, 4),)),
        "ada_weight": bell_draw(key_of[5], (D, 6, D), D ** -0.5, 0.1875, ((0, 4), (2, 8))),
        "ada_bias": bell_draw(key_of[6], (6, D), 1.0, 4.0),
        "qkv_weight": bell_draw(key_of[7], (D, 3, D), D ** -0.5, 0.1875, ((0, 8), (2, 4))),
        "qkv_bias": bell_draw(key_of[8], (3, D), 0.5, 3.0, ((1, 4),)),
        "q_gain": jnp.clip(jax.random.uniform(key_of[9], (HEAD_DIM,), jnp.float32, 0.796875, 2.0), 0.796875, 2.0).astype(jnp.bfloat16),
        "k_gain": jnp.clip(jax.random.uniform(key_of[10], (HEAD_DIM,), jnp.float32, 0.796875, 2.0), 0.796875, 2.0).astype(jnp.bfloat16),
        "out_weight": bell_draw(key_of[11], (D, D), (D // 16) ** -0.5, 0.75, ((0, 4), (1, 8))),
        "out_bias": bell_draw(key_of[12], (D,), 0.5, 3.0),
        "gate_up_weight": bell_draw(key_of[13], (D, 2, FF), D ** -0.5, 0.1875, ((0, 8), (2, 4))),
        "gate_up_bias": bell_draw(key_of[14], (2, FF), 0.5, 3.0, ((1, 4),)),
        "down_weight": bell_draw(key_of[15], (FF, D), FF ** -0.5, 0.109375, ((0, 4), (1, 8))),
        "down_bias": bell_draw(key_of[16], (D,), 0.5, 3.0),
        "cotangent": heavy_noise(key_of[17], (IMAGES, PATCHES, D), 1.0, 8.0, ((0, 8), (1, 4)), (0, 2, 8, 2.0)),
    }


@jax.custom_vjp
def low(v):
    return lax.optimization_barrier(v.astype(jnp.bfloat16)).astype(jnp.float32)

@jax.custom_vjp
def low_back(v):
    return v

def low_keep(v):
    return (low(v), None)

def low_pass(kept, grad):
    return (grad,)

def back_keep(v):
    return (v, None)

def back_low(kept, grad):
    return (low(grad),)
low.defvjp(low_keep, low_pass)
low_back.defvjp(back_keep, back_low)

def product(form, left, right):
    return jnp.einsum(form, left, right, precision=lax.Precision.HIGHEST)

def rms_rows(values):
    return values * lax.rsqrt(lax.optimization_barrier(jnp.mean(values * values, axis=-1, keepdims=True)) + 1e-06)

def modulate(values, shift_rows, scale_rows):
    return rms_rows(values) * (1.0 + scale_rows) + shift_rows

def rotate_pairs(values):
    paired = values.reshape(values.shape[:-1] + (values.shape[-1] // 2, 2))
    return jnp.stack((-paired[..., 1], paired[..., 0]), axis=-1).reshape(values.shape)

def rotary_tables(patch_cells):
    row_place = (patch_cells // GRID).astype(jnp.float32)
    col_place = (patch_cells % GRID).astype(jnp.float32)
    rates = 10000.0 ** (-4.0 * jnp.arange(HEAD_DIM // 4, dtype=jnp.float32) / HEAD_DIM)
    rates = jnp.repeat(rates, 2)
    angles = jnp.concatenate((row_place[..., None] * rates, col_place[..., None] * rates), axis=-1)
    return (jnp.cos(angles)[..., None, :], jnp.sin(angles)[..., None, :])

def timestep_wave(timesteps):
    half_width = D // 2
    rates = jnp.exp(-math.log(10000.0) * jnp.arange(half_width, dtype=jnp.float32) / half_width)
    phases = timesteps.astype(jnp.float32)[:, None] * rates[None, :]
    return jnp.concatenate((jnp.cos(phases), jnp.sin(phases)), axis=-1)

def prepare_heads(q_cols, k_cols, q_gain, k_gain, cosines, sines):
    head_shape = q_cols.shape[:-1] + (q_cols.shape[-1] // HEAD_DIM, HEAD_DIM)
    q_normed = rms_rows(q_cols.reshape(head_shape)) * q_gain
    k_normed = rms_rows(k_cols.reshape(head_shape)) * k_gain
    q_turned = q_normed * cosines + rotate_pairs(q_normed) * sines
    k_turned = k_normed * cosines + rotate_pairs(k_normed) * sines
    return (q_turned, k_turned)

def block_forward(params, image_rows, label_rows, wave_rows, cosines, sines):
    class_table, ada_weight, ada_bias, qkv_weight, qkv_bias, q_gain, k_gain, out_weight, out_bias, gate_up_weight, gate_up_bias, down_weight, down_bias = params
    cond = class_table[label_rows] + wave_rows
    cond_act = low(jax.nn.silu(cond))
    mod_values = low_back(product('gc,cke->gke', cond_act, ada_weight)) + ada_bias
    shift_a = mod_values[:, 0:1]
    scale_a = mod_values[:, 1:2]
    gate_a = mod_values[:, 2:3]
    shift_f = mod_values[:, 3:4]
    scale_f = mod_values[:, 4:5]
    gate_f = mod_values[:, 5:6]
    attn_in = low(modulate(image_rows, shift_a, scale_a))
    qkv = low_back(product('gpd,dke->gpke', attn_in, qkv_weight) + qkv_bias)
    q_rot, k_rot = prepare_heads(qkv[:, :, 0], qkv[:, :, 1], q_gain, k_gain, cosines, sines)
    q_rot = low(q_rot)
    k_rot = low(k_rot)
    v_low = low(qkv[:, :, 2].reshape(q_rot.shape))
    scores = low_back(product('gqhe,gkhe->ghqk', q_rot, k_rot) / math.sqrt(HEAD_DIM))
    probs = low(jax.nn.softmax(scores, axis=-1))
    heads_out = low_back(low(product('ghqk,gkhe->gqhe', probs, v_low))).reshape(image_rows.shape)
    attn = low_back(product('gpc,cd->gpd', heads_out, out_weight)) + out_bias
    mid = image_rows + gate_a * attn
    ffn_in = low(modulate(mid, shift_f, scale_f))
    gate_up = low_back(product('gpd,dkf->gpkf', ffn_in, gate_up_weight) + gate_up_bias)
    hidden = low(jax.nn.silu(gate_up[:, :, 0]) * gate_up[:, :, 1])
    ffn = low_back(product('gpf,fd->gpd', hidden, down_weight)) + down_bias
    return mid + gate_f * ffn

def reference(tokens, timesteps, labels, patch_cells, class_table, ada_weight, ada_bias, qkv_weight, qkv_bias, q_gain, k_gain, out_weight, out_bias, gate_up_weight, gate_up_bias, down_weight, down_bias, cotangent):
    params = tuple((weight.astype(jnp.float32) for weight in (class_table, ada_weight, ada_bias, qkv_weight, qkv_bias, q_gain, k_gain, out_weight, out_bias, gate_up_weight, gate_up_bias, down_weight, down_bias)))
    group_size = math.gcd(IMAGES, 16)
    group_count = IMAGES // group_size
    wave_all = timestep_wave(timesteps)
    cos_all, sin_all = rotary_tables(patch_cells)

    def one_group(totals, group_index):
        first = (group_index * group_size).astype(jnp.int32)

        def pick_rows(values):
            return lax.dynamic_slice_in_dim(values, first, group_size, 0)
        image_rows = pick_rows(tokens).astype(jnp.float32)
        label_rows = pick_rows(labels)
        wave_rows = pick_rows(wave_all)
        cosines = pick_rows(cos_all)
        sines = pick_rows(sin_all)

        def forward_only(weights, rows_in):
            return block_forward(weights, rows_in, label_rows, wave_rows, cosines, sines)
        result, backward = jax.vjp(forward_only, params, image_rows)
        weight_grads, rows_grad = backward(pick_rows(cotangent).astype(jnp.float32))
        totals = jax.tree.map(jnp.add, totals, weight_grads)
        return (totals, (result.astype(jnp.bfloat16), rows_grad))
    zeros = tuple((jnp.zeros_like(weight) for weight in params))
    totals, (results, row_grads) = lax.scan(one_group, zeros, jnp.arange(group_count, dtype=jnp.int32))
    output = results.reshape(IMAGES, PATCHES, D)
    tokens_grad = row_grads.reshape(IMAGES, PATCHES, D)
    return (output, tokens_grad, totals[0], totals[1], totals[2], totals[3], totals[4], totals[5], totals[6], totals[7], totals[8], totals[9], totals[10], totals[11], totals[12])
```

```python
import math

import jax
import jax.numpy as jnp
from jax import lax
from jax.sharding import Mesh
from jax.sharding import PartitionSpec as P

D = 1152
HEAD_DIM = 72
CLASSES = 1000
GRID = 16
F32 = jnp.float32
BF16 = jnp.bfloat16
CHIPS = "p"
CORES = "c"
LINE = "t"
EVERY = (CHIPS, CORES, LINE)
DATA = (CHIPS, CORES)


def rms_rows(values):
    return values * lax.rsqrt(jnp.mean(values * values, axis=-1, keepdims=True) + 1e-06)


def modulate(values, shift_rows, scale_rows):
    return rms_rows(values) * (1.0 + scale_rows) + shift_rows


def rotate_pairs(values):
    paired = values.reshape(values.shape[:-1] + (values.shape[-1] // 2, 2))
    return jnp.stack((-paired[..., 1], paired[..., 0]), axis=-1).reshape(values.shape)


def rotary_tables(patch_cells):
    row_place = (patch_cells // GRID).astype(F32)
    col_place = (patch_cells % GRID).astype(F32)
    rates = 10000.0 ** (-4.0 * jnp.arange(HEAD_DIM // 4, dtype=F32) / HEAD_DIM)
    rates = jnp.repeat(rates, 2)
    angles = jnp.concatenate((row_place[..., None] * rates, col_place[..., None] * rates), axis=-1)
    return (jnp.cos(angles)[..., None, :], jnp.sin(angles)[..., None, :])


def wave_columns(timesteps, first, width):
    half_width = D // 2
    columns = first + jnp.arange(width, dtype=jnp.int32)
    is_cos = columns < half_width
    spot = jnp.where(is_cos, columns, columns - half_width).astype(F32)
    rates = jnp.exp(-math.log(10000.0) * spot / half_width)
    phases = timesteps.astype(F32)[:, None] * rates[None, :]
    return jnp.where(is_cos[None, :], jnp.cos(phases), jnp.sin(phases))


def prepare_heads(q_cols, k_cols, q_gain, k_gain, cosines, sines):
    q_normed = rms_rows(q_cols) * q_gain
    k_normed = rms_rows(k_cols) * k_gain
    q_turned = q_normed * cosines + rotate_pairs(q_normed) * sines
    k_turned = k_normed * cosines + rotate_pairs(k_normed) * sines
    return (q_turned, k_turned)


def swiglu(gate_vals, up_vals):
    return jax.nn.silu(gate_vals) * up_vals


def axis_len(name):
    return lax.axis_size(name)


def swap(values, name, bit=1):
    count = axis_len(name)
    return lax.ppermute(values, name, [(i, i ^ bit) for i in range(count)])


def sum_by_swaps(values, name):
    count = axis_len(name)
    bit = 1
    while bit < count:
        values = values + swap(values, name, bit)
        bit *= 2
    return values


def gather_weight(piece):
    held = lax.all_gather(piece, LINE, axis=0)
    line, rows, cols = held.shape
    chips = axis_len(CHIPS)
    if chips != 4:
        return lax.all_gather(held, CHIPS, axis=1, tiled=True)
    me = lax.axis_index(CHIPS)
    half = line // 2
    from_x = swap(held, CHIPS, 1)
    from_y = swap(held, CHIPS, 2)
    diag_a = swap(from_x[:half], CHIPS, 2)
    diag_b = swap(from_y[half:], CHIPS, 1)
    whole = jnp.zeros((line, chips * rows, cols), piece.dtype)
    for part, flip, top in (
        (held, 0, 0),
        (from_x, 1, 0),
        (from_y, 2, 0),
        (diag_a, 3, 0),
        (diag_b, 3, half),
    ):
        whole = lax.dynamic_update_slice(whole, part, (top, (me ^ flip) * rows, 0))
    return whole


def scatter_grad(grad):
    line, all_rows, cols = grad.shape
    chips = axis_len(CHIPS)
    if chips != 4:
        grad = lax.psum_scatter(grad, CHIPS, scatter_dimension=1, tiled=True)
        return lax.psum_scatter(grad, LINE, scatter_dimension=0, tiled=False)
    rows = all_rows // chips
    me = lax.axis_index(CHIPS)
    half = line // 2

    def part(flip, top, count):
        return lax.dynamic_slice(grad, (top, (me ^ flip) * rows, 0), (count, rows, cols))

    got_x = swap(part(3, 0, half), CHIPS, 1)
    got_y = swap(part(3, half, line - half), CHIPS, 2)
    to_y = jnp.concatenate((part(2, 0, half) + got_x, part(2, half, line - half)), axis=0)
    to_x = jnp.concatenate((part(1, 0, half), part(1, half, line - half) + got_y), axis=0)
    from_y = swap(to_y, CHIPS, 2)
    from_x = swap(to_x, CHIPS, 1)
    own = (part(0, 0, line).astype(F32) + from_x.astype(F32) + from_y.astype(F32)).astype(BF16)
    return lax.psum_scatter(own, LINE, scatter_dimension=0, tiled=False)


def with_peer(values):
    return jnp.concatenate((values, swap(values, CORES)), axis=0)


def fold_peer(values):
    own = values.shape[0] // 2
    sent = swap(values[own:].astype(BF16), CORES)
    return values[:own] + sent.astype(F32)


def on_device(
    tokens,
    timesteps,
    labels,
    patch_cells,
    class_table,
    ada_weight,
    ada_bias,
    qkv_weight,
    qkv_bias,
    q_gain,
    k_gain,
    out_weight,
    out_bias,
    gate_up_weight,
    gate_up_bias,
    down_weight,
    down_bias,
    cotangent,
):
    core = lax.axis_index(CORES)
    line_at = lax.axis_index(LINE)
    line = axis_len(LINE)
    data = axis_len(CHIPS) * axis_len(CORES)
    devices = data * line
    images = tokens.shape[0]
    own_images = images // line
    width = class_table.shape[1]
    chunk = ada_weight.shape[2]
    inv_root = 1.0 / math.sqrt(HEAD_DIM)
    highest = lax.Precision.HIGHEST

    rows_w = qkv_weight.shape[0]
    head_cols = qkv_weight.shape[2] // 2
    ff_cols = gate_up_weight.shape[2] // 2

    def column_halves(which):
        qkv_half = lax.dynamic_slice_in_dim(qkv_weight, which * head_cols, head_cols, 2)
        out_half = lax.dynamic_slice_in_dim(out_weight, which * head_cols, head_cols, 0)
        gu_half = lax.dynamic_slice_in_dim(gate_up_weight, which * ff_cols, ff_cols, 2)
        down_half = lax.dynamic_slice_in_dim(down_weight, which * ff_cols, ff_cols, 0)
        return jnp.concatenate(
            (
                qkv_half.reshape(rows_w, 3 * head_cols),
                out_half.T,
                gu_half.reshape(rows_w, 2 * ff_cols),
                down_half.T,
            ),
            axis=1,
        )

    kept = column_halves(core)
    got = swap(column_halves(1 - core), CORES)
    both = jnp.concatenate(
        (jnp.where(core == 0, kept, got), jnp.where(core == 0, got, kept)), axis=0
    )
    attn_cols = 4 * head_cols
    w_attn = gather_weight(both[:, :attn_cols])
    w_ffn = gather_weight(both[:, attn_cols:])
    w_qkv = w_attn[:, :, : 3 * head_cols]
    w_out = w_attn[:, :, 3 * head_cols :]
    w_gu = w_ffn[:, :, : 2 * ff_cols]
    w_down = w_ffn[:, :, 2 * ff_cols :]

    small_in = lax.all_gather(jnp.stack((labels, timesteps)), DATA, axis=0)
    labels_all = small_in[:, 0].reshape(data * images)
    steps_all = small_in[:, 1].reshape(data * images)
    bias_in = jnp.concatenate((qkv_bias.reshape(-1), gate_up_bias.reshape(-1)))
    bias_all = lax.all_gather(bias_in, LINE, axis=0).astype(F32)
    qkv_b = bias_all[:, : 6 * head_cols].reshape(line, 3, 2, head_cols)
    qkv_b = lax.dynamic_index_in_dim(qkv_b, core, 2, keepdims=False).reshape(line, 3 * head_cols)
    gu_b = bias_all[:, 6 * head_cols :].reshape(line, 2, 2, ff_cols)
    gu_b = lax.dynamic_index_in_dim(gu_b, core, 2, keepdims=False).reshape(line, 2 * ff_cols)

    one_hot = (labels_all[:, None] == jnp.arange(CLASSES, dtype=jnp.int32)[None, :]).astype(BF16)
    cond = jnp.dot(one_hot, class_table, preferred_element_type=F32)
    cond = cond + wave_columns(steps_all, line_at * width, width)
    cond_low = jax.nn.silu(cond).astype(BF16)
    ada_flat = ada_weight.reshape(width, 6 * chunk)
    mod_part = jnp.dot(cond_low, ada_flat, preferred_element_type=F32)
    mod_part = lax.all_to_all(
        mod_part.reshape(devices, own_images * 6 * chunk), EVERY, 0, 0, tiled=True
    )
    mod = jnp.sum(mod_part.reshape(data, line, own_images, 6, chunk), axis=1)
    mod = mod.transpose(1, 2, 0, 3).reshape(own_images, 6, D) + ada_bias.astype(F32)
    shift_a, scale_a, gate_a, shift_f, scale_f, gate_f = (mod[:, k : k + 1] for k in range(6))

    cells = lax.dynamic_slice_in_dim(patch_cells, line_at * own_images, own_images, 0)
    cosines, sines = rotary_tables(with_peer(cells))
    cosines, sines = cosines[:, :, None], sines[:, :, None]
    q_gain_f = q_gain.astype(F32)
    k_gain_f = k_gain.astype(F32)

    x_rows = lax.all_to_all(tokens, LINE, 0, 1, tiled=True).astype(F32)
    attn_in = with_peer(modulate(x_rows, shift_a, scale_a).astype(BF16))
    qkv = jnp.einsum("bpd,zdn->bpzn", attn_in, w_qkv, preferred_element_type=F32) + qkv_b
    pair, patches = qkv.shape[:2]
    qkv = qkv.reshape(pair, patches, line, 3, head_cols // HEAD_DIM, HEAD_DIM)
    q_cols, k_cols = qkv[:, :, :, 0], qkv[:, :, :, 1]
    q_rot, k_rot = prepare_heads(q_cols, k_cols, q_gain_f, k_gain_f, cosines, sines)
    q_low, k_low = q_rot.astype(BF16), k_rot.astype(BF16)
    v_low = qkv[:, :, :, 2].astype(BF16)
    scores = (
        jnp.einsum("bqzhe,bkzhe->bzhqk", q_low, k_low, preferred_element_type=F32) * inv_root
    )
    peak = jnp.max(scores, axis=-1, keepdims=True)
    expo = jnp.exp(scores - peak)
    totals_row = jnp.sum(expo, axis=-1, keepdims=True)
    log_total = peak + jnp.log(totals_row)
    probs_low = (expo / totals_row).astype(BF16)
    heads_out = jnp.einsum("bzhqk,bkzhe->bqzhe", probs_low, v_low, preferred_element_type=F32)
    heads_out = heads_out.astype(BF16).reshape(pair, patches, line, head_cols)
    attn = fold_peer(
        jnp.einsum("bpzc,zdc->bpd", heads_out, w_out, preferred_element_type=F32)
    ) + out_bias.astype(F32)
    mid = x_rows + gate_a * attn
    ffn_in = with_peer(modulate(mid, shift_f, scale_f).astype(BF16))
    gate_up = jnp.einsum("bpd,zdn->bpzn", ffn_in, w_gu, preferred_element_type=F32) + gu_b
    gate_vals, up_vals = gate_up[..., :ff_cols], gate_up[..., ff_cols:]
    hidden = swiglu(gate_vals, up_vals).astype(BF16)
    ffn = fold_peer(
        jnp.einsum("bpzf,zdf->bpd", hidden, w_down, preferred_element_type=F32)
    ) + down_bias.astype(F32)
    output = lax.all_to_all((mid + gate_f * ffn).astype(BF16), LINE, 1, 0, tiled=True)

    grad_out = lax.all_to_all(cotangent, LINE, 0, 1, tiled=True).astype(F32)
    d_ffn_f = gate_f * grad_out
    down_bias_part = jnp.sum(d_ffn_f, axis=(0, 1))
    d_gate_f = jnp.sum(grad_out * ffn, axis=1, keepdims=True)
    d_ffn = with_peer(d_ffn_f.astype(BF16))
    g_down = jnp.einsum("bpd,bpzf->zdf", d_ffn, hidden, preferred_element_type=F32)
    d_hidden = jnp.einsum("bpd,zdf->bpzf", d_ffn, w_down, preferred_element_type=F32)
    d_gate, d_up = jax.vjp(swiglu, gate_vals, up_vals)[1](d_hidden)
    d_gu = jnp.concatenate((d_gate, d_up), axis=-1).astype(BF16)
    gu_bias_part = jnp.sum(d_gu, axis=(0, 1), dtype=F32)
    g_gu = jnp.einsum("bpd,bpzn->zdn", ffn_in, d_gu, preferred_element_type=F32)
    g_ffn = scatter_grad(jnp.concatenate((g_gu.astype(BF16), g_down.astype(BF16)), axis=-1))
    d_ffn_in = fold_peer(jnp.einsum("bpzn,zdn->bpd", d_gu, w_gu, preferred_element_type=F32))
    mid_grad, d_shift_f, d_scale_f = jax.vjp(modulate, mid, shift_f, scale_f)[1](d_ffn_in)
    d_mid = grad_out + mid_grad
    d_attn_f = gate_a * d_mid
    out_bias_part = jnp.sum(d_attn_f, axis=(0, 1))
    d_gate_a = jnp.sum(d_mid * attn, axis=1, keepdims=True)
    d_attn = with_peer(d_attn_f.astype(BF16))
    g_out = jnp.einsum("bpd,bpzc->zdc", d_attn, heads_out, preferred_element_type=F32)
    d_heads = jnp.einsum("bpd,zdc->bpzc", d_attn, w_out, preferred_element_type=F32)
    d_heads = d_heads.astype(BF16).reshape(q_low.shape)
    scores = (
        jnp.einsum("bqzhe,bkzhe->bzhqk", q_low, k_low, preferred_element_type=F32) * inv_root
    )
    probs_f = jnp.exp(scores - log_total)
    d_probs = jnp.einsum("bqzhe,bkzhe->bzhqk", d_heads, v_low, preferred_element_type=F32)
    d_vals = jnp.einsum(
        "bzhqk,bqzhe->bkzhe", probs_f.astype(BF16), d_heads, preferred_element_type=F32
    )
    d_scores = probs_f * (d_probs - jnp.sum(d_probs * probs_f, axis=-1, keepdims=True))
    d_scores = d_scores.astype(BF16)
    d_qrot = (
        jnp.einsum("bzhqk,bkzhe->bqzhe", d_scores, k_low, preferred_element_type=F32) * inv_root
    )
    d_krot = (
        jnp.einsum("bzhqk,bqzhe->bkzhe", d_scores, q_low, preferred_element_type=F32) * inv_root
    )
    prepare_back = jax.vjp(prepare_heads, q_cols, k_cols, q_gain_f, k_gain_f, cosines, sines)[1]
    d_q, d_k, q_gain_part, k_gain_part = prepare_back((d_qrot, d_krot))[:4]
    d_qkv = jnp.stack((d_q, d_k, d_vals), axis=3).astype(BF16)
    d_qkv = d_qkv.reshape(pair, patches, line, 3 * head_cols)
    qkv_bias_part = jnp.sum(d_qkv, axis=(0, 1), dtype=F32)
    g_qkv = jnp.einsum("bpd,bpzn->zdn", attn_in, d_qkv, preferred_element_type=F32)
    g_attn = scatter_grad(jnp.concatenate((g_qkv.astype(BF16), g_out.astype(BF16)), axis=-1))
    d_attn_in = fold_peer(jnp.einsum("bpzn,zdn->bpd", d_qkv, w_qkv, preferred_element_type=F32))
    row_grad, d_shift_a, d_scale_a = jax.vjp(modulate, x_rows, shift_a, scale_a)[1](d_attn_in)
    tokens_grad = lax.all_to_all(
        (d_mid + row_grad).astype(BF16), LINE, 1, 0, tiled=True
    ).astype(F32)

    d_mod = jnp.concatenate(
        (d_shift_a, d_scale_a, d_gate_a, d_shift_f, d_scale_f, d_gate_f), axis=1
    )
    ada_bias_part = jnp.sum(d_mod, axis=0)
    d_mod_low = d_mod.astype(BF16).reshape(own_images, 6, data, chunk).transpose(2, 0, 1, 3)
    d_mod_low = jnp.broadcast_to(
        d_mod_low[:, None], (data, line, own_images, 6, chunk)
    ).reshape(devices, own_images * 6 * chunk)
    d_mod_all = lax.all_to_all(d_mod_low, EVERY, 0, 0, tiled=True)
    d_mod_all = d_mod_all.reshape(data * images, 6 * chunk)
    g_ada = jnp.einsum("bc,be->ce", cond_low, d_mod_all, preferred_element_type=F32)
    g_ada = g_ada.reshape(width, 6, chunk)
    d_silu = jnp.einsum("be,ce->bc", d_mod_all, ada_flat, preferred_element_type=F32)
    d_cond = jax.vjp(jax.nn.silu, cond)[1](d_silu)[0]

    def by_core(part, groups, cols):
        spread = jnp.zeros((line, groups, 2, cols), F32)
        return lax.dynamic_update_slice(
            spread, part.reshape(line, groups, 1, cols), (0, 0, core, 0)
        )

    parts = (
        by_core(qkv_bias_part, 3, head_cols),
        by_core(gu_bias_part, 2, ff_cols),
        ada_bias_part,
        out_bias_part,
        down_bias_part,
        q_gain_part,
        k_gain_part,
    )
    flat = jnp.concatenate([part.reshape(-1) for part in parts])
    count = flat.shape[0]
    flat = jnp.concatenate((flat, d_cond.reshape(-1)))
    flat = sum_by_swaps(sum_by_swaps(flat, CORES), CHIPS)
    d_cond = flat[count:].reshape(d_cond.shape)
    flat = sum_by_swaps(flat[:count], LINE)
    sums = []
    at = 0
    for part in parts:
        sums.append(flat[at : at + part.size].reshape(part.shape))
        at += part.size
    qkv_bias_grad = lax.dynamic_index_in_dim(sums[0], line_at, 0, keepdims=False)
    gu_bias_grad = lax.dynamic_index_in_dim(sums[1], line_at, 0, keepdims=False)
    table_grad = jnp.dot(one_hot.astype(F32).T, d_cond, precision=highest)

    g_both = jnp.concatenate((g_attn, g_ffn), axis=1)
    kept = lax.dynamic_slice_in_dim(g_both, core * rows_w, rows_w, 0)
    got = swap(lax.dynamic_slice_in_dim(g_both, (1 - core) * rows_w, rows_w, 0), CORES)
    low_half = jnp.where(core == 0, kept, got).astype(F32)
    high_half = jnp.where(core == 0, got, kept).astype(F32)

    def joined(first, groups, cols):
        last = first + groups * cols
        return jnp.concatenate(
            (
                low_half[:, first:last].reshape(rows_w, groups, cols),
                high_half[:, first:last].reshape(rows_w, groups, cols),
            ),
            axis=2,
        )

    g_qkv = joined(0, 3, head_cols)
    g_out = joined(3 * head_cols, 1, head_cols)[:, 0].T
    g_gu = joined(attn_cols, 2, ff_cols)
    g_down = joined(attn_cols + 2 * ff_cols, 1, ff_cols)[:, 0].T
    return (
        output,
        tokens_grad,
        table_grad,
        g_ada,
        sums[2],
        g_qkv,
        qkv_bias_grad.reshape(qkv_bias.shape),
        sums[5],
        sums[6],
        g_out,
        sums[3],
        g_gu,
        gu_bias_grad.reshape(gate_up_bias.shape),
        g_down,
        sums[4],
    )


def solution(mesh):
    chips = mesh.shape["dp"] // 2
    finer = Mesh(mesh.devices.reshape(chips, 2, mesh.shape["tensor"]), EVERY)
    in_specs = (
        P(DATA, LINE, None),
        P(DATA),
        P(DATA),
        P(DATA, None),
        P(None, LINE),
        P(LINE, None, DATA),
        P(),
        P(DATA, None, LINE),
        P(None, LINE),
        P(),
        P(),
        P(LINE, DATA),
        P(),
        P(DATA, None, LINE),
        P(None, LINE),
        P(LINE, DATA),
        P(),
        P(DATA, LINE, None),
    )
    out_specs = (
        P(DATA, LINE, None),
        P(DATA, LINE, None),
        P(None, LINE),
        P(LINE, None, DATA),
        P(),
        P(DATA, None, LINE),
        P(None, LINE),
        P(),
        P(),
        P(LINE, DATA),
        P(),
        P(DATA, None, LINE),
        P(None, LINE),
        P(LINE, DATA),
        P(),
    )
    return jax.shard_map(
        on_device, mesh=finer, in_specs=in_specs, out_specs=out_specs, check_vma=False
    )
```

```python
import functools
import math

import jax
import jax.numpy as jnp
from jax import lax
from jax.experimental import pallas as pl
from jax.experimental.pallas import tpu as pltpu
from jax.sharding import Mesh
from jax.sharding import PartitionSpec as P

D = 1152
HEAD_DIM = 72
CLASSES = 1000
GRID = 16
F32 = jnp.float32
BF16 = jnp.bfloat16
INV_ROOT = 1.0 / math.sqrt(HEAD_DIM)
CHIPS = "p"
CORES = "c"
LINE = "t"
PAD = 128
EVERY = (CHIPS, CORES, LINE)
DATA = (CHIPS, CORES)


def rms_rows(values):
    return values * lax.rsqrt(jnp.mean(values * values, axis=-1, keepdims=True) + 1e-06)


def modulate(values, shift_rows, scale_rows):
    return rms_rows(values) * (1.0 + scale_rows) + shift_rows


def rotary_tables(patch_cells, repeat):
    entry = jnp.arange(repeat * HEAD_DIM, dtype=jnp.int32) % HEAD_DIM
    half = HEAD_DIM // 2
    step = (entry % half // 2).astype(F32)
    rates = 10000.0 ** (-4.0 * step / HEAD_DIM)
    cells = patch_cells[..., None]
    place = jnp.where(entry < half, cells // GRID, cells % GRID).astype(F32)
    angles = place * rates
    return jnp.cos(angles), jnp.sin(angles)


def wave_columns(timesteps, first, width):
    half_width = D // 2
    columns = first + jnp.arange(width, dtype=jnp.int32)
    is_cos = columns < half_width
    spot = jnp.where(is_cos, columns, columns - half_width).astype(F32)
    rates = jnp.exp(-math.log(10000.0) * spot / half_width)
    phases = timesteps.astype(F32)[:, None] * rates[None, :]
    return jnp.where(is_cos[None, :], jnp.cos(phases), jnp.sin(phases))


def dot_rows(a, b):
    return lax.dot_general(a, b, (((1,), (0,)), ((), ())), preferred_element_type=F32)


def dot_last(a, b):
    return lax.dot_general(a, b, (((1,), (1,)), ((), ())), preferred_element_type=F32)


def dot_first(a, b):
    return lax.dot_general(a, b, (((0,), (0,)), ((), ())), preferred_element_type=F32)


def head_tables(cols):
    lane = lax.broadcasted_iota(jnp.int32, (cols, cols), 0)
    other = lax.broadcasted_iota(jnp.int32, (cols, cols), 1)
    same = jnp.where(lane // HEAD_DIM == other // HEAD_DIM, 1.0, 0.0).astype(BF16)
    even = other % 2 == 0
    turn = jnp.where(even & (lane == other + 1), -1.0, 0.0)
    turn = jnp.where(jnp.logical_not(even) & (lane == other - 1), 1.0, turn).astype(BF16)
    return same, turn


def unit_heads(values, same):
    mean_sq = dot_rows((values * values).astype(BF16), same) * (1.0 / HEAD_DIM)
    scale = lax.rsqrt(mean_sq + 1e-06)
    return values * scale, scale


def turn_heads(values, cosines, sines, turn):
    return values * cosines + dot_rows(values.astype(BF16), turn) * sines


def head_masks(cols):
    lane = lax.broadcasted_iota(jnp.int32, (1, cols), 1)
    return [
        (lane >= h * HEAD_DIM) & (lane < (h + 1) * HEAD_DIM) for h in range(cols // HEAD_DIM)
    ]


def attn_forward_kernel(
    own_ref, peer_ref, w_ref, b_ref, g_ref, cos_ref, sin_ref, same_ref, turn_ref,
    qkv_ref, heads_ref, own_out, peer_out, total,
):
    _, chips, rows, cols = w_ref.shape
    hc = cols // 4
    images, patches, width = own_ref.shape
    same, turn = same_ref[...], turn_ref[...]
    masks = head_masks(hc)
    at = pl.program_id(0)
    w = w_ref[0].reshape(chips * rows, cols)
    for side, x_ref in enumerate((own_ref, peer_ref)):
        x = x_ref[...].reshape(images * patches, width)
        qkv = dot_rows(x, w[:, : 3 * hc]) + b_ref[0]
        first = side * images * patches
        qkv_ref[0, first : first + images * patches] = qkv.astype(BF16)
        tables = [
            ref[side * images : (side + 1) * images].reshape(images * patches, hc)
            for ref in (cos_ref, sin_ref)
        ]
        q_rot = unit_heads(qkv[:, :hc], same)[0] * g_ref[0]
        q_rot = turn_heads(q_rot, *tables, turn).astype(BF16)
        k_rot = unit_heads(qkv[:, hc : 2 * hc], same)[0] * g_ref[1]
        k_rot = turn_heads(k_rot, *tables, turn).astype(BF16)
        v_all = qkv[:, 2 * hc :].astype(BF16)
        outs = []
        for image in range(images):
            rows_at = slice(image * patches, (image + 1) * patches)
            q, k, v = q_rot[rows_at], k_rot[rows_at], v_all[rows_at]
            heads = None
            for mine in masks:
                scores = dot_last(jnp.where(mine, q, jnp.zeros_like(q)), k)
                expo = jnp.exp(scores * INV_ROOT)
                probs = expo * (1.0 / jnp.sum(expo, axis=1, keepdims=True))
                part = dot_rows(probs.astype(BF16), v)
                heads = part if heads is None else jnp.where(mine, part, heads)
            outs.append(heads.astype(BF16))
        heads = jnp.concatenate(outs, axis=0)
        heads_ref[0, first : first + images * patches] = heads
        step = dot_last(heads, w[:, 3 * hc :])

        @pl.when(at == 0)
        def _():
            total[side] = step

        @pl.when(at > 0)
        def _():
            total[side] += step

    @pl.when(at == pl.num_programs(0) - 1)
    def _():
        own_out[...] = total[0].reshape(images, patches, width).astype(BF16)
        peer_out[...] = total[1].reshape(images, patches, width).astype(BF16)


def attn_backward_kernel(
    own_ref, peer_ref, w_ref, qkv_in_ref, g_ref, cos_ref, sin_ref, same_ref, turn_ref,
    dqkv_ref, own_out, peer_out, bias_ref, gain_ref, total,
):
    _, chips, rows, cols = w_ref.shape
    hc = cols // 4
    images, patches, width = own_ref.shape
    same, turn = same_ref[...], turn_ref[...]
    masks = head_masks(hc)
    at = pl.program_id(0)

    @pl.when(at == 0)
    def _():
        gain_ref[...] = jnp.zeros_like(gain_ref)

    w = w_ref[0].reshape(chips * rows, cols)
    bias = None
    for side, dy_ref in enumerate((own_ref, peer_ref)):
        first = side * images * patches
        rows_here = slice(first, first + images * patches)
        tables = [
            ref[side * images : (side + 1) * images].reshape(images * patches, hc)
            for ref in (cos_ref, sin_ref)
        ]
        dy = dy_ref[...].reshape(images * patches, width)
        d_heads_all = dot_rows(dy, w[:, 3 * hc :]).astype(BF16)
        qkv = qkv_in_ref[0, rows_here]
        v_all = qkv[:, 2 * hc :]
        uq, rq = unit_heads(qkv[:, :hc].astype(F32), same)
        uk, rk = unit_heads(qkv[:, hc : 2 * hc].astype(F32), same)
        q_rot = turn_heads(uq * g_ref[0], *tables, turn).astype(BF16)
        k_rot = turn_heads(uk * g_ref[1], *tables, turn).astype(BF16)
        grads = ([], [], [])
        for image in range(images):
            rows_at = slice(image * patches, (image + 1) * patches)
            q, k, v, d_heads = q_rot[rows_at], k_rot[rows_at], v_all[rows_at], d_heads_all[rows_at]
            zero = jnp.zeros_like(q)
            here = [None, None, None]
            for mine in masks:
                scores = dot_last(jnp.where(mine, q, zero), k)
                expo = jnp.exp(scores * INV_ROOT)
                probs = expo * (1.0 / jnp.sum(expo, axis=1, keepdims=True))
                d_probs = dot_last(jnp.where(mine, d_heads, zero), v)
                mean = jnp.sum(d_probs * probs, axis=1, keepdims=True)
                d_scores = (probs * (d_probs - mean)).astype(BF16)
                parts = (
                    dot_rows(d_scores, k),
                    dot_first(d_scores, q),
                    dot_first(probs.astype(BF16), d_heads),
                )
                here = [
                    new if old is None else jnp.where(mine, new, old)
                    for new, old in zip(parts, here)
                ]
            for which in range(3):
                grads[which].append(here[which])
        d_q, d_k, d_v = (jnp.concatenate(part, axis=0) for part in grads)
        sides = []
        for which, (grad, unit, scale) in enumerate(((d_q, uq, rq), (d_k, uk, rk))):
            grad = grad * INV_ROOT
            back = grad * tables[0] + dot_last((grad * tables[1]).astype(BF16), turn)
            gain_ref[which : which + 1] += jnp.sum(back * unit, axis=0, keepdims=True)
            back = back * g_ref[which]
            mean = dot_rows((back * unit).astype(BF16), same) * (1.0 / HEAD_DIM)
            sides.append((back - unit * mean) * scale)
        d_qkv = jnp.concatenate((sides[0], sides[1], d_v), axis=1)
        part = jnp.sum(d_qkv, axis=0, keepdims=True)
        bias = part if bias is None else bias + part
        d_qkv = d_qkv.astype(BF16)
        dqkv_ref[0, rows_here] = d_qkv
        step = dot_last(d_qkv, w[:, : 3 * hc])

        @pl.when(at == 0)
        def _():
            total[side] = step

        @pl.when(at > 0)
        def _():
            total[side] += step

    bias_ref[0] = bias

    @pl.when(at == pl.num_programs(0) - 1)
    def _():
        own_out[...] = total[0].reshape(images, patches, width).astype(BF16)
        peer_out[...] = total[1].reshape(images, patches, width).astype(BF16)


def resident(shape):
    return pl.BlockSpec(shape, lambda i: (0,) * len(shape))


def by_line(shape):
    return pl.BlockSpec((1,) + shape, lambda i: (i,) + (0,) * len(shape))


def attn_cost(x, w, products):
    images, patches, width = x.shape
    line, _, _, cols = w.shape
    pairs = 2 * images * line * (cols // (4 * HEAD_DIM)) * patches * patches
    return pl.CostEstimate(
        flops=4 * images * patches * width * line * cols + products * 2 * pairs * 256,
        bytes_accessed=w.size * 2 + x.size * 16,
        transcendentals=pairs,
    )


def attn_forward(own, peer, w, b, *tables):
    images, patches, width = own.shape
    line, _, _, cols = w.shape
    hc = cols // 4
    rows = 2 * images * patches
    return pl.pallas_call(
        attn_forward_kernel,
        grid=(line,),
        in_specs=[resident(own.shape)] * 2
        + [by_line(w.shape[1:]), by_line(b.shape[1:])]
        + [resident(table.shape) for table in tables],
        out_specs=[by_line((rows, 3 * hc)), by_line((rows, hc))] + [resident(own.shape)] * 2,
        out_shape=[
            jax.ShapeDtypeStruct((line, rows, 3 * hc), BF16),
            jax.ShapeDtypeStruct((line, rows, hc), BF16),
        ]
        + [jax.ShapeDtypeStruct(own.shape, BF16)] * 2,
        scratch_shapes=[pltpu.VMEM((2, images * patches, width), F32)],
        compiler_params=pltpu.CompilerParams(vmem_limit_bytes=50 << 20),
        cost_estimate=attn_cost(own, w, 2),
    )(own, peer, w, b, *tables)


def attn_backward(own, peer, w, qkv, *tables):
    images, patches, width = own.shape
    line, _, _, cols = w.shape
    hc = cols // 4
    rows = 2 * images * patches
    return pl.pallas_call(
        attn_backward_kernel,
        grid=(line,),
        in_specs=[resident(own.shape)] * 2
        + [by_line(w.shape[1:]), by_line(qkv.shape[1:])]
        + [resident(table.shape) for table in tables],
        out_specs=[by_line((rows, 3 * hc))]
        + [resident(own.shape)] * 2
        + [by_line((1, 3 * hc)), resident((2, hc))],
        out_shape=[jax.ShapeDtypeStruct((line, rows, 3 * hc), BF16)]
        + [jax.ShapeDtypeStruct(own.shape, BF16)] * 2
        + [jax.ShapeDtypeStruct((line, 1, 3 * hc), F32), jax.ShapeDtypeStruct((2, hc), F32)],
        scratch_shapes=[pltpu.VMEM((2, images * patches, width), F32)],
        compiler_params=pltpu.CompilerParams(vmem_limit_bytes=50 << 20),
        cost_estimate=attn_cost(own, w, 5),
    )(own, peer, w, qkv, *tables)


def swiglu(gate_vals, up_vals):
    return jax.nn.silu(gate_vals) * up_vals


def after(values, *others):
    return lax.optimization_barrier((values, others))[0]


def axis_len(name):
    return lax.axis_size(name)


def swap(values, name, bit=1):
    count = axis_len(name)
    return lax.ppermute(values, name, [(i, i ^ bit) for i in range(count)])


def sum_by_swaps(values, name):
    count = axis_len(name)
    bit = 1
    while bit < count:
        values = values + swap(values, name, bit)
        bit *= 2
    return values


def place_kernel(half, spot_ref, own_ref, x_ref, y_ref, da_ref, db_ref, out_ref):
    at = pl.program_id(0)
    out_ref[0, spot_ref[0]] = own_ref[0]
    out_ref[0, spot_ref[1]] = x_ref[0]
    out_ref[0, spot_ref[2]] = y_ref[0]

    @pl.when(at < half)
    def _():
        out_ref[0, spot_ref[3]] = da_ref[0]

    @pl.when(at >= half)
    def _():
        out_ref[0, spot_ref[3]] = db_ref[0]


def place_parts(own, from_x, from_y, diag_a, diag_b):
    line, rows, cols = own.shape
    half = diag_a.shape[0]
    spots = lax.axis_index(CHIPS) ^ jnp.arange(4, dtype=jnp.int32)
    straight = pl.BlockSpec((1, rows, cols), lambda i: (i, 0, 0))
    early = pl.BlockSpec((1, rows, cols), lambda i: (jnp.minimum(i, half - 1), 0, 0))
    late = pl.BlockSpec((1, rows, cols), lambda i: (jnp.maximum(i - half, 0), 0, 0))
    return pl.pallas_call(
        functools.partial(place_kernel, half),
        grid=(line,),
        in_specs=[pl.BlockSpec(memory_space=pltpu.SMEM)] + [straight] * 3 + [early, late],
        out_specs=pl.BlockSpec((1, 4, rows, cols), lambda i: (i, 0, 0, 0)),
        out_shape=jax.ShapeDtypeStruct((line, 4, rows, cols), own.dtype),
        compiler_params=pltpu.CompilerParams(vmem_limit_bytes=40 << 20),
        cost_estimate=pl.CostEstimate(flops=0, bytes_accessed=16 * own.size, transcendentals=0),
    )(spots, own, from_x, from_y, diag_a, diag_b)


def gather_line(piece):
    return lax.all_gather(piece, LINE, axis=0)


def first_hop(held):
    if axis_len(CHIPS) != 4:
        return (held,)
    return swap(held, CHIPS, 1), swap(held, CHIPS, 2)


def second_hop(arrived):
    if len(arrived) == 1:
        return arrived, arrived
    half = arrived[0].shape[0] // 2
    low, high = arrived[0][:half], arrived[1][half:]
    return (low, high), (swap(low, CHIPS, 2), swap(high, CHIPS, 1))


def whole_weight(held, arrived, last):
    if len(arrived) == 1:
        return lax.all_gather(held, CHIPS, axis=1, tiled=True)[:, None]
    return place_parts(held, *arrived, *last)


def weight_product(lefts, right):
    left = jnp.concatenate(lefts, axis=0)
    return jnp.einsum("rd,zrn->zdn", left, right, preferred_element_type=F32).astype(BF16)


def grad_kernel(counts, spot_ref, *refs):
    lefts, refs = refs[: sum(counts)], refs[sum(counts) :]
    rights, refs = refs[: len(counts)], refs[len(counts) :]
    outs, scratch = refs[:5], refs[5:]
    plain, turned = scratch[0], scratch[1:]
    rows = outs[4].shape[1]
    half = rows // 2

    @pl.when(pl.program_id(0) == 0)
    def _():
        for pair, count in enumerate(counts):
            at = 0
            for left in lefts[sum(counts[:pair]) : sum(counts[:pair]) + count]:
                plain[:, at : at + left.shape[0]] = left[...].T
                at += left.shape[0]
            for place in range(4):
                turned[pair][place * rows : (place + 1) * rows] = plain[
                    pl.ds(pl.multiple_of(spot_ref[place] * rows, rows), rows)
                ]

    first = 0
    for pair, right in enumerate(rights):
        last = first + right.shape[-1]
        made = dot_rows(turned[pair][...], right[0]).astype(BF16)
        top = 0
        for out, count in zip(outs, (half, rows - half, rows, rows, rows)):
            out[0, :, first:last] = made[top : top + count]
            top += count
        first = last


def chip_products(pairs):
    line, total_rows, _ = pairs[0][1].shape
    width = pairs[0][0][0].shape[1]
    cols = sum(right.shape[-1] for _, right in pairs)
    rows = width // 4
    half = rows // 2
    spots = lax.axis_index(CHIPS) ^ jnp.array((3, 2, 1, 0), dtype=jnp.int32)
    lefts = [left for group, _ in pairs for left in group]
    rights = [right for _, right in pairs]
    cut = (half, rows - half, rows, rows, rows)
    return pl.pallas_call(
        functools.partial(grad_kernel, tuple(len(group) for group, _ in pairs)),
        grid=(line,),
        in_specs=[pl.BlockSpec(memory_space=pltpu.SMEM)]
        + [resident(left.shape) for left in lefts]
        + [by_line(right.shape[1:]) for right in rights],
        out_specs=[by_line((count, cols)) for count in cut],
        out_shape=[jax.ShapeDtypeStruct((line, count, cols), BF16) for count in cut],
        scratch_shapes=[pltpu.VMEM((width, total_rows), BF16)] * (1 + len(pairs)),
        compiler_params=pltpu.CompilerParams(vmem_limit_bytes=50 << 20),
        cost_estimate=pl.CostEstimate(
            flops=2 * line * width * total_rows * cols,
            bytes_accessed=2 * line * (width + total_rows) * cols,
            transcendentals=0,
        ),
    )(spots, *lefts, *rights)


def send_diagonal(pairs):
    if axis_len(CHIPS) != 4:
        grad = jnp.concatenate([weight_product(*pair) for pair in pairs], axis=-1)
        return (grad,), None
    parts = chip_products(pairs)
    return parts, (swap(parts[0], CHIPS, 1), swap(parts[1], CHIPS, 2))


def send_blocks(parts, got):
    if got is None:
        return parts, None
    _, _, to_y, to_x, _ = parts
    half = got[0].shape[1]
    to_y = jnp.concatenate((to_y[:, :half] + got[0], to_y[:, half:]), axis=1)
    to_x = jnp.concatenate((to_x[:, :half], to_x[:, half:] + got[1]), axis=1)
    return (to_y, to_x), (swap(to_y, CHIPS, 2), swap(to_x, CHIPS, 1))


def add_blocks(parts, got):
    if got is None:
        return lax.psum_scatter(parts[0], CHIPS, scatter_dimension=1, tiled=True)
    return (parts[4].astype(F32) + got[0].astype(F32) + got[1].astype(F32)).astype(BF16)


def scatter_line(part):
    return lax.psum_scatter(part, LINE, scatter_dimension=0, tiled=False)


def with_peer(values):
    return jnp.concatenate((values, swap(values, CORES)), axis=0)


def fold_peer(values):
    own = values.shape[0] // 2
    sent = swap(values[own:].astype(BF16), CORES)
    return values[:own] + sent.astype(F32)


def on_device(
    tokens,
    timesteps,
    labels,
    patch_cells,
    class_table,
    ada_weight,
    ada_bias,
    qkv_weight,
    qkv_bias,
    q_gain,
    k_gain,
    out_weight,
    out_bias,
    gate_up_weight,
    gate_up_bias,
    down_weight,
    down_bias,
    cotangent,
):
    core = lax.axis_index(CORES)
    line_at = lax.axis_index(LINE)
    line = axis_len(LINE)
    data = axis_len(CHIPS) * axis_len(CORES)
    devices = data * line
    images = tokens.shape[0]
    own_images = images // line
    width = class_table.shape[1]
    chunk = ada_weight.shape[2]
    highest = lax.Precision.HIGHEST

    rows_w = qkv_weight.shape[0]
    head_cols = qkv_weight.shape[2] // 2
    ff_cols = gate_up_weight.shape[2] // 2

    def column_halves(which):
        qkv_half = lax.dynamic_slice_in_dim(qkv_weight, which * head_cols, head_cols, 2)
        out_half = lax.dynamic_slice_in_dim(out_weight, which * head_cols, head_cols, 0)
        gu_half = lax.dynamic_slice_in_dim(gate_up_weight, which * ff_cols, ff_cols, 2)
        down_half = lax.dynamic_slice_in_dim(down_weight, which * ff_cols, ff_cols, 0)
        return jnp.concatenate(
            (
                qkv_half.reshape(rows_w, 3 * head_cols),
                out_half.T,
                gu_half.reshape(rows_w, 2 * ff_cols),
                down_half.T,
            ),
            axis=1,
        )

    kept = column_halves(core)
    got = swap(column_halves(1 - core), CORES)
    both = jnp.concatenate(
        (jnp.where(core == 0, kept, got), jnp.where(core == 0, got, kept)), axis=0
    )
    attn_cols = 4 * head_cols
    held_attn = gather_line(both[:, :attn_cols])
    held_gu = gather_line(both[:, attn_cols : attn_cols + 2 * ff_cols])
    down_piece = both[:, attn_cols + 2 * ff_cols :]
    held_down = gather_line(jnp.pad(down_piece, ((0, 0), (0, PAD))))

    small_in = jnp.stack((labels, timesteps))
    small_in = lax.all_to_all(
        jnp.broadcast_to(small_in, (data,) + small_in.shape), DATA, 0, 0, tiled=True
    )
    labels_all = small_in[:, 0].reshape(data * images)
    steps_all = small_in[:, 1].reshape(data * images)
    one_hot = (labels_all[:, None] == jnp.arange(CLASSES, dtype=jnp.int32)[None, :]).astype(BF16)
    cond = jnp.dot(one_hot, class_table, preferred_element_type=F32)
    cond = cond + wave_columns(steps_all, line_at * width, width)
    cond_low = jax.nn.silu(cond).astype(BF16)
    ada_flat = ada_weight.reshape(width, 6 * chunk)
    mod_part = jnp.dot(cond_low, ada_flat, preferred_element_type=F32)
    bias_in = jnp.concatenate((qkv_bias.reshape(-1), gate_up_bias.reshape(-1))).astype(F32)
    bias_len = bias_in.shape[0]
    share = -(-bias_len // data)
    bias_in = jnp.pad(bias_in, (0, share * data - bias_len)).reshape(data, share)
    data_at = lax.axis_index(CHIPS) * axis_len(CORES) + core
    bias_in = lax.dynamic_index_in_dim(bias_in, data_at, 0, keepdims=True)
    mod_part = mod_part.reshape(devices, own_images * 6 * chunk)
    mod_part = jnp.concatenate((mod_part, jnp.broadcast_to(bias_in, (devices, share))), axis=1)
    mod_part = lax.all_to_all(mod_part, EVERY, 0, 0, tiled=True)
    bias_all = mod_part[:, own_images * 6 * chunk :].reshape(data, line, share)
    bias_all = bias_all.transpose(1, 0, 2).reshape(line, data * share)[:, :bias_len]
    mod_part = mod_part[:, : own_images * 6 * chunk]
    mod = jnp.sum(mod_part.reshape(data, line, own_images, 6, chunk), axis=1)
    mod = mod.transpose(1, 2, 0, 3).reshape(own_images, 6, D) + ada_bias.astype(F32)
    shift_a, scale_a, gate_a, shift_f, scale_f, gate_f = (mod[:, k : k + 1] for k in range(6))

    cells = lax.dynamic_slice_in_dim(patch_cells, line_at * own_images, own_images, 0)
    repeat = head_cols // HEAD_DIM
    cosines, sines = rotary_tables(with_peer(cells), repeat)
    gains = jnp.tile(jnp.stack((q_gain, k_gain)).astype(F32)[:, None], (1, 1, repeat))
    same, turn = head_tables(head_cols)

    x_rows = lax.all_to_all(after(tokens, held_attn), LINE, 0, 1, tiled=True)
    attn_arrived = after(first_hop(held_attn), cosines, sines)
    _, attn_last = second_hop(attn_arrived)
    x_rows = after(x_rows, attn_last).astype(F32)
    held_gu = after(held_gu, attn_last)
    gu_arrived = first_hop(held_gu)
    qkv_b = bias_all[:, : 6 * head_cols].reshape(line, 3, 2, head_cols)
    qkv_b = lax.dynamic_index_in_dim(qkv_b, core, 2, keepdims=False).reshape(line, 1, 3 * head_cols)
    gu_b = bias_all[:, 6 * head_cols :].reshape(line, 2, 2, ff_cols)
    gu_b = lax.dynamic_index_in_dim(gu_b, core, 2, keepdims=False).reshape(line, 2 * ff_cols)
    attn_own = modulate(x_rows, shift_a, scale_a).astype(BF16)
    attn_peer = swap(attn_own, CORES)
    w_attn = whole_weight(held_attn, attn_arrived, attn_last)
    tables = (gains, cosines, sines, same, turn)
    qkv, heads_out, part_own, part_peer = attn_forward(
        after(attn_own, held_gu), attn_peer, w_attn, qkv_b, *tables
    )
    part_peer = swap(part_peer, CORES)
    gu_passed, gu_last = second_hop(gu_arrived)
    part_own = after(part_own, gu_passed)
    held_down = after(held_down[:, :, :ff_cols], gu_last)
    down_arrived = first_hop(held_down)
    attn = part_own.astype(F32) + part_peer.astype(F32) + out_bias.astype(F32)
    patches = x_rows.shape[1]
    rows_all = 2 * own_images * patches

    def as_rows(*values):
        return [value.reshape(own_images * patches, D) for value in values]

    mid = x_rows + gate_a * attn
    ffn_in = with_peer(modulate(mid, shift_f, scale_f).astype(BF16))
    ffn_in = ffn_in.reshape(rows_all, D)
    w_gu = whole_weight(held_gu, gu_arrived, after(gu_last, ffn_in)).reshape(line, D, 2 * ff_cols)
    gate_up = jnp.einsum("rd,zdn->zrn", ffn_in, w_gu, preferred_element_type=F32) + gu_b[:, None]
    down_passed, down_last = second_hop(after(down_arrived, gate_up))
    gate_up = after(gate_up, down_passed)
    gate_vals, up_vals = gate_up[..., :ff_cols], gate_up[..., ff_cols:]
    hidden = swiglu(gate_vals, up_vals).astype(BF16)
    grad_out = lax.all_to_all(after(cotangent, heads_out), LINE, 0, 1, tiled=True).astype(F32)
    d_ffn_f = gate_f * grad_out
    d_ffn_own = d_ffn_f.astype(BF16)
    d_ffn = jnp.concatenate(as_rows(d_ffn_own, swap(d_ffn_own, CORES)), axis=0)
    down_parts, down_got = send_diagonal([([d_ffn], hidden)])
    hidden, d_ffn = after((hidden, d_ffn), down_parts)
    w_down = whole_weight(held_down, down_arrived, down_last).reshape(line, D, ff_cols)
    ffn = jnp.einsum("zrf,zdf->rd", hidden, w_down, preferred_element_type=F32)
    ffn = fold_peer(ffn.reshape(2 * own_images, patches, D)) + down_bias.astype(F32)
    output = lax.all_to_all((mid + gate_f * ffn).astype(BF16), LINE, 1, 0, tiled=True)

    down_bias_part = jnp.sum(d_ffn_f, axis=(0, 1))
    d_gate_f = jnp.sum(grad_out * ffn, axis=1, keepdims=True)
    d_hidden = jnp.einsum("rd,zdf->zrf", d_ffn, w_down, preferred_element_type=F32)
    d_gate, d_up = jax.vjp(swiglu, gate_vals, up_vals)[1](d_hidden)
    d_gu = jnp.concatenate((d_gate, d_up), axis=-1).astype(BF16)
    gu_bias_part = jnp.sum(d_gu, axis=1, dtype=F32)
    down_sent, down_blocks = send_blocks(down_parts, down_got)
    gu_parts, gu_got = send_diagonal([([ffn_in], after(d_gu, down_sent))])
    d_gu = after(d_gu, gu_parts)
    d_ffn_in = jnp.einsum("zrn,zdn->rd", d_gu, w_gu, preferred_element_type=F32)
    d_ffn_in = fold_peer(d_ffn_in.reshape(2 * own_images, patches, D))
    d_ffn_in = after(d_ffn_in, down_blocks)
    g_down = add_blocks(down_parts if down_blocks is not None else down_sent, down_blocks)
    g_down = scatter_line(g_down)
    mid_grad, d_shift_f, d_scale_f = jax.vjp(modulate, mid, shift_f, scale_f)[1](d_ffn_in)
    d_mid = grad_out + mid_grad
    d_attn_f = gate_a * d_mid
    out_bias_part = jnp.sum(d_attn_f, axis=(0, 1))
    d_gate_a = jnp.sum(d_mid * attn, axis=1, keepdims=True)
    d_attn_own = d_attn_f.astype(BF16)
    d_attn_peer = swap(d_attn_own, CORES)
    gu_sent, gu_blocks = send_blocks(gu_parts, gu_got)
    d_qkv, d_in_own, d_in_peer, qkv_bias_part, gain_part = attn_backward(
        after(d_attn_own, gu_sent), d_attn_peer, w_attn, qkv, *tables
    )
    d_in_peer = swap(d_in_peer, CORES)
    g_gu = add_blocks(gu_parts if gu_blocks is not None else gu_sent, after(gu_blocks, d_qkv))
    attn_parts, attn_got = send_diagonal(
        [
            (as_rows(attn_own, attn_peer), after(d_qkv, g_gu, output)),
            (as_rows(d_attn_own, d_attn_peer), heads_out),
        ]
    )
    g_gu = scatter_line(after(g_gu, g_down))
    gain_part = gain_part.reshape(2, repeat, HEAD_DIM).sum(axis=1)
    d_attn_in = d_in_own.astype(F32) + d_in_peer.astype(F32)
    row_grad, d_shift_a, d_scale_a = jax.vjp(modulate, x_rows, shift_a, scale_a)[1](d_attn_in)
    tokens_sent = (d_mid + row_grad).astype(BF16)

    d_mod = jnp.concatenate(
        (d_shift_a, d_scale_a, d_gate_a, d_shift_f, d_scale_f, d_gate_f), axis=1
    )
    ada_bias_part = jnp.sum(d_mod, axis=0)
    d_mod_low = d_mod.astype(BF16).reshape(own_images, 6, data, chunk).transpose(2, 0, 1, 3)
    d_mod_low = jnp.broadcast_to(
        d_mod_low[:, None], (data, line, own_images, 6, chunk)
    ).reshape(devices, own_images * 6 * chunk)
    attn_got, tokens_sent = lax.optimization_barrier((attn_got, tokens_sent))
    tokens_grad = lax.all_to_all(tokens_sent, LINE, 1, 0, tiled=True)
    attn_sent, attn_blocks = send_blocks(attn_parts, attn_got)
    d_mod_all = lax.all_to_all(d_mod_low, EVERY, 0, 0, tiled=True)
    d_mod_all = d_mod_all.reshape(data * images, 6 * chunk)
    g_ada = jnp.einsum("bc,be->ce", cond_low, d_mod_all, preferred_element_type=F32)
    g_ada = g_ada.reshape(width, 6, chunk)
    d_silu = jnp.einsum("be,ce->bc", d_mod_all, ada_flat, preferred_element_type=F32)
    d_cond = jax.vjp(jax.nn.silu, cond)[1](d_silu)[0]

    def by_core(part, groups, cols):
        spread = jnp.zeros((line, groups, 2, cols), F32)
        return lax.dynamic_update_slice(
            spread, part.reshape(line, groups, 1, cols), (0, 0, core, 0)
        )

    parts = (
        by_core(qkv_bias_part, 3, head_cols),
        by_core(gu_bias_part, 2, ff_cols),
        ada_bias_part,
        out_bias_part,
        down_bias_part,
        gain_part[0],
        gain_part[1],
    )
    flat = jnp.concatenate([part.reshape(-1) for part in parts])
    count = flat.shape[0]
    flat = jnp.concatenate((flat, d_cond.reshape(-1)))
    flat = sum_by_swaps(sum_by_swaps(flat, CORES), CHIPS)
    g_attn = add_blocks(attn_parts, after(attn_blocks, flat))
    g_attn, tokens_grad = lax.optimization_barrier((after(g_attn, g_gu), tokens_grad))
    g_attn = scatter_line(g_attn)
    d_cond = flat[count:].reshape(d_cond.shape)
    flat = sum_by_swaps(flat[:count], LINE)
    sums = []
    at = 0
    for part in parts:
        sums.append(flat[at : at + part.size].reshape(part.shape))
        at += part.size
    qkv_bias_grad = lax.dynamic_index_in_dim(sums[0], line_at, 0, keepdims=False)
    gu_bias_grad = lax.dynamic_index_in_dim(sums[1], line_at, 0, keepdims=False)
    tokens_grad = tokens_grad.astype(F32)
    table_grad = jnp.dot(one_hot.astype(F32).T, d_cond, precision=highest)

    def own_rows(part):
        kept = lax.dynamic_slice_in_dim(part, core * rows_w, rows_w, 0)
        got = swap(lax.dynamic_slice_in_dim(part, (1 - core) * rows_w, rows_w, 0), CORES)
        low_half = jnp.where(core == 0, kept, got).astype(F32)
        high_half = jnp.where(core == 0, got, kept).astype(F32)

        def joined(first, groups, cols):
            halves = [
                half[:, first : first + groups * cols].reshape(rows_w, groups, cols)
                for half in (low_half, high_half)
            ]
            return jnp.concatenate(halves, axis=2)

        return joined

    joined = own_rows(g_gu)
    g_gu = joined(0, 2, ff_cols)
    joined = own_rows(g_down)
    g_down = joined(0, 1, ff_cols)[:, 0].T
    joined = own_rows(g_attn)
    g_qkv = joined(0, 3, head_cols)
    g_out = joined(3 * head_cols, 1, head_cols)[:, 0].T
    return (
        output,
        tokens_grad,
        table_grad,
        g_ada,
        sums[2],
        g_qkv,
        qkv_bias_grad.reshape(qkv_bias.shape),
        sums[5],
        sums[6],
        g_out,
        sums[3],
        g_gu,
        gu_bias_grad.reshape(gate_up_bias.shape),
        g_down,
        sums[4],
    )


def solution(mesh):
    chips = mesh.shape["dp"] // 2
    finer = Mesh(mesh.devices.reshape(chips, 2, mesh.shape["tensor"]), EVERY)
    in_specs = (
        P(DATA, LINE, None),
        P(DATA),
        P(DATA),
        P(DATA, None),
        P(None, LINE),
        P(LINE, None, DATA),
        P(),
        P(DATA, None, LINE),
        P(None, LINE),
        P(),
        P(),
        P(LINE, DATA),
        P(),
        P(DATA, None, LINE),
        P(None, LINE),
        P(LINE, DATA),
        P(),
        P(DATA, LINE, None),
    )
    out_specs = (
        P(DATA, LINE, None),
        P(DATA, LINE, None),
        P(None, LINE),
        P(LINE, None, DATA),
        P(),
        P(DATA, None, LINE),
        P(None, LINE),
        P(),
        P(),
        P(LINE, DATA),
        P(),
        P(DATA, None, LINE),
        P(None, LINE),
        P(LINE, DATA),
        P(),
    )
    return jax.shard_map(
        on_device, mesh=finer, in_specs=in_specs, out_specs=out_specs, check_vma=False
    )
```

```python
import functools
import math

import jax
import jax.numpy as jnp
from jax import lax
from jax.experimental import pallas as pl
from jax.experimental.pallas import tpu as pltpu
from jax.sharding import Mesh
from jax.sharding import PartitionSpec as P

D = 1152
HEAD_DIM = 72
CLASSES = 1000
GRID = 16
F32 = jnp.float32
BF16 = jnp.bfloat16
INV_ROOT = 1.0 / math.sqrt(HEAD_DIM)
CHIPS = "p"
CORES = "c"
LINE = "t"
PAD = 128
EVERY = (CHIPS, CORES, LINE)
DATA = (CHIPS, CORES)


def rms_rows(values):
    return values * lax.rsqrt(jnp.mean(values * values, axis=-1, keepdims=True) + 1e-06)


def modulate(values, shift_rows, scale_rows):
    return rms_rows(values) * (1.0 + scale_rows) + shift_rows


def rotary_tables(patch_cells, repeat):
    entry = jnp.arange(repeat * HEAD_DIM, dtype=jnp.int32) % HEAD_DIM
    half = HEAD_DIM // 2
    step = (entry % half // 2).astype(F32)
    rates = 10000.0 ** (-4.0 * step / HEAD_DIM)
    cells = patch_cells[..., None]
    place = jnp.where(entry < half, cells // GRID, cells % GRID).astype(F32)
    angles = place * rates
    return jnp.cos(angles), jnp.sin(angles)


def wave_columns(timesteps, first, width):
    half_width = D // 2
    columns = first + jnp.arange(width, dtype=jnp.int32)
    is_cos = columns < half_width
    spot = jnp.where(is_cos, columns, columns - half_width).astype(F32)
    rates = jnp.exp(-math.log(10000.0) * spot / half_width)
    phases = timesteps.astype(F32)[:, None] * rates[None, :]
    return jnp.where(is_cos[None, :], jnp.cos(phases), jnp.sin(phases))


def dot_rows(a, b):
    return lax.dot_general(a, b, (((1,), (0,)), ((), ())), preferred_element_type=F32)


def dot_last(a, b):
    return lax.dot_general(a, b, (((1,), (1,)), ((), ())), preferred_element_type=F32)


def dot_first(a, b):
    return lax.dot_general(a, b, (((0,), (0,)), ((), ())), preferred_element_type=F32)


def head_tables(cols):
    lane = lax.broadcasted_iota(jnp.int32, (cols, cols), 0)
    other = lax.broadcasted_iota(jnp.int32, (cols, cols), 1)
    same = jnp.where(lane // HEAD_DIM == other // HEAD_DIM, 1.0, 0.0).astype(BF16)
    even = other % 2 == 0
    turn = jnp.where(even & (lane == other + 1), -1.0, 0.0)
    turn = jnp.where(jnp.logical_not(even) & (lane == other - 1), 1.0, turn).astype(BF16)
    return same, turn


def unit_heads(values, same):
    mean_sq = dot_rows((values * values).astype(BF16), same) * (1.0 / HEAD_DIM)
    scale = lax.rsqrt(mean_sq + 1e-06)
    return values * scale, scale


def turn_heads(values, cosines, sines, turn):
    return values * cosines + dot_rows(values.astype(BF16), turn) * sines


def head_masks(cols):
    lane = lax.broadcasted_iota(jnp.int32, (1, cols), 1)
    return [
        (lane >= h * HEAD_DIM) & (lane < (h + 1) * HEAD_DIM) for h in range(cols // HEAD_DIM)
    ]


def attn_forward_kernel(
    own_ref, peer_ref, w_ref, b_ref, g_ref, cos_ref, sin_ref, same_ref, turn_ref,
    qkv_ref, heads_ref, own_out, peer_out, x_all, total,
):
    hc = w_ref.shape[2] // 4
    images, patches, width = own_ref.shape
    side = images * patches
    same, turn = same_ref[...], turn_ref[...]
    masks = head_masks(hc)
    at = pl.program_id(0)

    @pl.when(at == 0)
    def _():
        x_all[:side] = own_ref[...].reshape(side, width)
        x_all[side:] = peer_ref[...].reshape(side, width)

    qkv = dot_rows(x_all[...], w_ref[0, :, : 3 * hc]) + b_ref[0]
    qkv_ref[0] = qkv.astype(BF16)
    tables = (cos_ref[...], sin_ref[...])
    q_rot = unit_heads(qkv[:, :hc], same)[0] * (g_ref[0] * INV_ROOT)
    q_rot = turn_heads(q_rot, *tables, turn).astype(BF16)
    k_rot = unit_heads(qkv[:, hc : 2 * hc], same)[0] * g_ref[1]
    k_rot = turn_heads(k_rot, *tables, turn).astype(BF16)
    v_all = qkv[:, 2 * hc :].astype(BF16)
    v_all = jnp.concatenate((v_all, jnp.ones((2 * side, 256 - hc), BF16)), axis=1)
    q_heads = [jnp.where(mine, q_rot, jnp.zeros_like(q_rot)) for mine in masks]
    outs = []
    for image in range(2 * images):
        rows_at = slice(image * patches, (image + 1) * patches)
        k, v = k_rot[rows_at], v_all[rows_at]
        heads = None
        for q, mine in zip(q_heads, masks):
            expo = jnp.exp(dot_last(q[rows_at], k)).astype(BF16)
            part = dot_rows(expo, v)
            part = part[:, :hc] * (1.0 / part[:, hc : hc + 1])
            heads = part if heads is None else jnp.where(mine, part, heads)
        outs.append(heads.astype(BF16))
    heads = jnp.concatenate(outs, axis=0)
    heads_ref[0] = heads
    step = dot_last(heads, w_ref[0, :, 3 * hc :])

    @pl.when(at == 0)
    def _():
        total[...] = step

    @pl.when(at > 0)
    def _():
        total[...] += step

    @pl.when(at == pl.num_programs(0) - 1)
    def _():
        own_out[...] = total[:side].reshape(images, patches, width).astype(BF16)
        peer_out[...] = total[side:].reshape(images, patches, width).astype(BF16)


def attn_backward_kernel(
    own_ref, peer_ref, w_ref, qkv_in_ref, g_ref, cos_ref, sin_ref, same_ref, turn_ref,
    dqkv_ref, own_out, peer_out, bias_ref, gain_ref, x_all, total,
):
    hc = w_ref.shape[2] // 4
    images, patches, width = own_ref.shape
    side = images * patches
    same, turn = same_ref[...], turn_ref[...]
    masks = head_masks(hc)
    at = pl.program_id(0)

    @pl.when(at == 0)
    def _():
        gain_ref[...] = jnp.zeros_like(gain_ref)
        x_all[:side] = own_ref[...].reshape(side, width)
        x_all[side:] = peer_ref[...].reshape(side, width)

    tables = (cos_ref[...], sin_ref[...])
    d_heads_all = dot_rows(x_all[...], w_ref[0, :, 3 * hc :]).astype(BF16)
    qkv = qkv_in_ref[0]
    v_all = qkv[:, 2 * hc :]
    uq, rq = unit_heads(qkv[:, :hc].astype(F32), same)
    uk, rk = unit_heads(qkv[:, hc : 2 * hc].astype(F32), same)
    q_rot = turn_heads(uq * (g_ref[0] * INV_ROOT), *tables, turn).astype(BF16)
    k_rot = turn_heads(uk * g_ref[1], *tables, turn).astype(BF16)
    zero = jnp.zeros_like(q_rot)
    q_heads = [jnp.where(mine, q_rot, zero) for mine in masks]
    v_heads = [jnp.where(mine, v_all, zero) for mine in masks]
    grads = ([], [], [])
    for image in range(2 * images):
        rows_at = slice(image * patches, (image + 1) * patches)
        q, k, d_heads = q_rot[rows_at], k_rot[rows_at], d_heads_all[rows_at]
        here = [None, None, None]
        for head, mine in enumerate(masks):
            expo = jnp.exp(dot_last(k, q_heads[head][rows_at]))
            probs = expo * (1.0 / jnp.sum(expo, axis=0, keepdims=True))
            d_probs = dot_last(v_heads[head][rows_at], d_heads)
            mean = jnp.sum(d_probs * probs, axis=0, keepdims=True)
            d_scores = (probs * (d_probs - mean)).astype(BF16)
            parts = (
                dot_first(d_scores, k),
                dot_rows(d_scores, q),
                dot_rows(probs.astype(BF16), d_heads),
            )
            here = [
                new if old is None else jnp.where(mine, new, old)
                for new, old in zip(parts, here)
            ]
        for which in range(3):
            grads[which].append(here[which])
    d_q, d_k, d_v = (jnp.concatenate(part, axis=0) for part in grads)
    sides = []
    for which, (grad, unit, scale) in enumerate(((d_q * INV_ROOT, uq, rq), (d_k, uk, rk))):
        back = grad * tables[0] + dot_last((grad * tables[1]).astype(BF16), turn)
        gain_ref[which : which + 1] += jnp.sum(back * unit, axis=0, keepdims=True)
        back = back * g_ref[which]
        mean = dot_rows((back * unit).astype(BF16), same) * (1.0 / HEAD_DIM)
        sides.append((back - unit * mean) * scale)
    d_qkv = jnp.concatenate((sides[0], sides[1], d_v), axis=1)
    bias_ref[0] = jnp.sum(d_qkv, axis=0, keepdims=True)
    d_qkv = d_qkv.astype(BF16)
    dqkv_ref[0] = d_qkv
    step = dot_last(d_qkv, w_ref[0, :, : 3 * hc])

    @pl.when(at == 0)
    def _():
        total[...] = step

    @pl.when(at > 0)
    def _():
        total[...] += step

    @pl.when(at == pl.num_programs(0) - 1)
    def _():
        own_out[...] = total[:side].reshape(images, patches, width).astype(BF16)
        peer_out[...] = total[side:].reshape(images, patches, width).astype(BF16)


def resident(shape):
    return pl.BlockSpec(shape, lambda i: (0,) * len(shape))


def by_line(shape):
    return pl.BlockSpec((1,) + shape, lambda i: (i,) + (0,) * len(shape))


def attn_cost(x, w, products):
    images, patches, width = x.shape
    line, _, cols = w.shape
    pairs = 2 * images * line * (cols // (4 * HEAD_DIM)) * patches * patches
    return pl.CostEstimate(
        flops=4 * images * patches * width * line * cols + products * 2 * pairs * 256,
        bytes_accessed=w.size * 2 + x.size * 16,
        transcendentals=pairs,
    )


def attn_forward(own, peer, w, b, *tables):
    images, patches, width = own.shape
    line, _, cols = w.shape
    hc = cols // 4
    rows = 2 * images * patches
    return pl.pallas_call(
        attn_forward_kernel,
        grid=(line,),
        in_specs=[resident(own.shape)] * 2
        + [by_line(w.shape[1:]), by_line(b.shape[1:])]
        + [resident(table.shape) for table in tables],
        out_specs=[by_line((rows, 3 * hc)), by_line((rows, hc))]
        + [resident(own.shape)] * 2,
        out_shape=[
            jax.ShapeDtypeStruct((line, rows, 3 * hc), BF16),
            jax.ShapeDtypeStruct((line, rows, hc), BF16),
        ]
        + [jax.ShapeDtypeStruct(own.shape, BF16)] * 2,
        scratch_shapes=[pltpu.VMEM((rows, width), BF16), pltpu.VMEM((rows, width), F32)],
        compiler_params=pltpu.CompilerParams(vmem_limit_bytes=50 << 20),
        cost_estimate=attn_cost(own, w, 2),
    )(own, peer, w, b, *tables)


def attn_backward(own, peer, w, qkv, *tables):
    images, patches, width = own.shape
    line, _, cols = w.shape
    hc = cols // 4
    rows = 2 * images * patches
    return pl.pallas_call(
        attn_backward_kernel,
        grid=(line,),
        in_specs=[resident(own.shape)] * 2
        + [by_line(w.shape[1:]), by_line(qkv.shape[1:])]
        + [resident(table.shape) for table in tables],
        out_specs=[by_line((rows, 3 * hc))]
        + [resident(own.shape)] * 2
        + [by_line((1, 3 * hc)), resident((2, hc))],
        out_shape=[jax.ShapeDtypeStruct((line, rows, 3 * hc), BF16)]
        + [jax.ShapeDtypeStruct(own.shape, BF16)] * 2
        + [jax.ShapeDtypeStruct((line, 1, 3 * hc), F32), jax.ShapeDtypeStruct((2, hc), F32)],
        scratch_shapes=[pltpu.VMEM((rows, width), BF16), pltpu.VMEM((rows, width), F32)],
        compiler_params=pltpu.CompilerParams(vmem_limit_bytes=50 << 20),
        cost_estimate=attn_cost(own, w, 5),
    )(own, peer, w, qkv, *tables)


def ffn_forward_kernel(
    own_ref, peer_ref, w_ref, b_ref, gu_ref, hidden_ref, x_all,
):
    ff = hidden_ref.shape[2]
    images, patches, width = own_ref.shape
    side = images * patches

    @pl.when(pl.program_id(0) == 0)
    def _():
        x_all[:side] = own_ref[...].reshape(side, width)
        x_all[side:] = peer_ref[...].reshape(side, width)

    made = dot_rows(x_all[...], w_ref[0]) + b_ref[0]
    gu_ref[0] = made.astype(BF16)
    gate, up = made[:, :ff], made[:, ff:]
    hidden_ref[0] = (gate * up / (1.0 + jnp.exp(-gate))).astype(BF16)


def ffn_forward(own, peer, w, b):
    images, patches, width = own.shape
    line, _, cols = w.shape
    rows = 2 * images * patches
    return pl.pallas_call(
        ffn_forward_kernel,
        grid=(line,),
        in_specs=[resident(own.shape)] * 2
        + [by_line(w.shape[1:]), by_line(b.shape[1:])],
        out_specs=[by_line((rows, cols)), by_line((rows, cols // 2))],
        out_shape=[
            jax.ShapeDtypeStruct((line, rows, cols), BF16),
            jax.ShapeDtypeStruct((line, rows, cols // 2), BF16),
        ],
        scratch_shapes=[pltpu.VMEM((rows, width), BF16)],
        compiler_params=pltpu.CompilerParams(vmem_limit_bytes=50 << 20),
        cost_estimate=pl.CostEstimate(
            flops=2 * rows * width * line * cols,
            bytes_accessed=2 * line * cols * (width + 2 * rows),
            transcendentals=line * rows * cols // 2,
        ),
    )(own, peer, w, b)


def ffn_backward_kernel(
    own_ref, peer_ref, down_ref, w_ref, gu_ref,
    d_gu_ref, own_out, peer_out, bias_ref, x_all, total,
):
    ff = down_ref.shape[2]
    images, patches, width = own_ref.shape
    side = images * patches
    at = pl.program_id(0)

    @pl.when(at == 0)
    def _():
        x_all[:side] = own_ref[...].reshape(side, width)
        x_all[side:] = peer_ref[...].reshape(side, width)

    d_hidden = dot_rows(x_all[...], down_ref[0])
    gate, up = gu_ref[0, :, :ff].astype(F32), gu_ref[0, :, ff:].astype(F32)
    sig = 1.0 / (1.0 + jnp.exp(-gate))
    silu = gate * sig
    d_up = d_hidden * silu
    d_gate = d_hidden * up * (sig + silu * (1.0 - sig))
    bias_ref[0, :, :ff] = jnp.sum(d_gate, axis=0, keepdims=True)
    bias_ref[0, :, ff:] = jnp.sum(d_up, axis=0, keepdims=True)
    d_gu_ref[0, :, :ff] = d_gate.astype(BF16)
    d_gu_ref[0, :, ff:] = d_up.astype(BF16)
    step = dot_last(d_gu_ref[0], w_ref[0])

    @pl.when(at == 0)
    def _():
        total[...] = step

    @pl.when(at > 0)
    def _():
        total[...] += step

    @pl.when(at == pl.num_programs(0) - 1)
    def _():
        own_out[...] = total[:side].reshape(images, patches, width).astype(BF16)
        peer_out[...] = total[side:].reshape(images, patches, width).astype(BF16)


def ffn_backward(own, peer, w_down, w_gu, gate_up):
    images, patches, width = own.shape
    line, rows, cols = gate_up.shape
    return pl.pallas_call(
        ffn_backward_kernel,
        grid=(line,),
        in_specs=[resident(own.shape)] * 2
        + [by_line(w_down.shape[1:]), by_line(w_gu.shape[1:]), by_line((rows, cols))],
        out_specs=[by_line((rows, cols))] + [resident(own.shape)] * 2 + [by_line((1, cols))],
        out_shape=[jax.ShapeDtypeStruct((line, rows, cols), BF16)]
        + [jax.ShapeDtypeStruct(own.shape, BF16)] * 2
        + [jax.ShapeDtypeStruct((line, 1, cols), F32)],
        scratch_shapes=[pltpu.VMEM((rows, width), BF16), pltpu.VMEM((rows, width), F32)],
        compiler_params=pltpu.CompilerParams(vmem_limit_bytes=50 << 20),
        cost_estimate=pl.CostEstimate(
            flops=3 * rows * width * line * cols,
            bytes_accessed=2 * line * cols * (2 * width + 2 * rows),
            transcendentals=line * rows * cols // 2,
        ),
    )(own, peer, w_down, w_gu, gate_up)


def after(values, *others):
    return lax.optimization_barrier((values, others))[0]


def axis_len(name):
    return lax.axis_size(name)


def swap(values, name, bit=1):
    count = axis_len(name)
    return lax.ppermute(values, name, [(i, i ^ bit) for i in range(count)])


def sum_by_swaps(values, name):
    count = axis_len(name)
    bit = 1
    while bit < count:
        values = values + swap(values, name, bit)
        bit *= 2
    return values


def place_kernel(half, spot_ref, own_ref, x_ref, y_ref, da_ref, db_ref, out_ref):
    at = pl.program_id(0)
    out_ref[0, spot_ref[0]] = own_ref[0]
    out_ref[0, spot_ref[1]] = x_ref[0]
    out_ref[0, spot_ref[2]] = y_ref[0]

    @pl.when(at < half)
    def _():
        out_ref[0, spot_ref[3]] = da_ref[0]

    @pl.when(at >= half)
    def _():
        out_ref[0, spot_ref[3]] = db_ref[0]


def place_parts(own, from_x, from_y, diag_a, diag_b):
    line, rows, cols = own.shape
    half = diag_a.shape[0]
    spots = lax.axis_index(CHIPS) ^ jnp.arange(4, dtype=jnp.int32)
    straight = pl.BlockSpec((1, rows, cols), lambda i: (i, 0, 0))
    early = pl.BlockSpec((1, rows, cols), lambda i: (jnp.minimum(i, half - 1), 0, 0))
    late = pl.BlockSpec((1, rows, cols), lambda i: (jnp.maximum(i - half, 0), 0, 0))
    return pl.pallas_call(
        functools.partial(place_kernel, half),
        grid=(line,),
        in_specs=[pl.BlockSpec(memory_space=pltpu.SMEM)] + [straight] * 3 + [early, late],
        out_specs=pl.BlockSpec((1, 4, rows, cols), lambda i: (i, 0, 0, 0)),
        out_shape=jax.ShapeDtypeStruct((line, 4, rows, cols), own.dtype),
        compiler_params=pltpu.CompilerParams(vmem_limit_bytes=40 << 20),
        cost_estimate=pl.CostEstimate(flops=0, bytes_accessed=16 * own.size, transcendentals=0),
    )(spots, own, from_x, from_y, diag_a, diag_b)


def to_whole(values):
    line = axis_len(LINE)
    images, patches, width = values.shape
    moved = values.reshape(line, images // line, patches, width)
    moved = lax.all_to_all(moved, LINE, 0, 0, tiled=True)
    return moved.transpose(1, 0, 2, 3).reshape(images // line, line * patches, width)


def to_parts(values):
    line = axis_len(LINE)
    images, patches, width = values.shape
    moved = values.reshape(images, line, patches // line, width).transpose(1, 0, 2, 3)
    moved = lax.all_to_all(moved, LINE, 0, 0, tiled=True)
    return moved.reshape(images * line, patches // line, width)


def gather_line(piece):
    return lax.all_gather(piece, LINE, axis=0)


def first_hop(held):
    if axis_len(CHIPS) != 4:
        return (held,)
    return swap(held, CHIPS, 1), swap(held, CHIPS, 2)


def second_hop(arrived):
    if len(arrived) == 1:
        return arrived, arrived
    half = arrived[0].shape[0] // 2
    low, high = arrived[0][:half], arrived[1][half:]
    return (low, high), (swap(low, CHIPS, 2), swap(high, CHIPS, 1))


def whole_weight(held, arrived, last):
    if len(arrived) == 1:
        return lax.all_gather(held, CHIPS, axis=1, tiled=True)[:, None]
    return place_parts(held, *arrived, *last)


def weight_product(lefts, right):
    left = jnp.concatenate(lefts, axis=0)
    return jnp.einsum("rd,zrn->zdn", left, right, preferred_element_type=F32).astype(BF16)


def grad_kernel(counts, spot_ref, *refs):
    lefts, refs = refs[: sum(counts)], refs[sum(counts) :]
    rights, refs = refs[: len(counts)], refs[len(counts) :]
    outs, scratch = refs[:5], refs[5:]
    plain, turned = scratch[0], scratch[1:]
    rows = outs[4].shape[1]
    half = rows // 2

    @pl.when(pl.program_id(0) == 0)
    def _():
        for pair, count in enumerate(counts):
            at = 0
            for left in lefts[sum(counts[:pair]) : sum(counts[:pair]) + count]:
                plain[:, at : at + left.shape[0]] = left[...].T
                at += left.shape[0]
            for place in range(4):
                turned[pair][place * rows : (place + 1) * rows] = plain[
                    pl.ds(pl.multiple_of(spot_ref[place] * rows, rows), rows)
                ]

    first = 0
    for pair, right in enumerate(rights):
        last = first + right.shape[-1]
        made = dot_rows(turned[pair][...], right[0]).astype(BF16)
        top = 0
        for out, count in zip(outs, (half, rows - half, rows, rows, rows)):
            out[0, :, first:last] = made[top : top + count]
            top += count
        first = last


def chip_products(pairs):
    line, total_rows, _ = pairs[0][1].shape
    width = pairs[0][0][0].shape[1]
    cols = sum(right.shape[-1] for _, right in pairs)
    rows = width // 4
    half = rows // 2
    spots = lax.axis_index(CHIPS) ^ jnp.array((3, 2, 1, 0), dtype=jnp.int32)
    lefts = [left for group, _ in pairs for left in group]
    rights = [right for _, right in pairs]
    cut = (half, rows - half, rows, rows, rows)
    return pl.pallas_call(
        functools.partial(grad_kernel, tuple(len(group) for group, _ in pairs)),
        grid=(line,),
        in_specs=[pl.BlockSpec(memory_space=pltpu.SMEM)]
        + [resident(left.shape) for left in lefts]
        + [by_line(right.shape[1:]) for right in rights],
        out_specs=[by_line((count, cols)) for count in cut],
        out_shape=[jax.ShapeDtypeStruct((line, count, cols), BF16) for count in cut],
        scratch_shapes=[pltpu.VMEM((width, total_rows), BF16)] * (1 + len(pairs)),
        compiler_params=pltpu.CompilerParams(vmem_limit_bytes=50 << 20),
        cost_estimate=pl.CostEstimate(
            flops=2 * line * width * total_rows * cols,
            bytes_accessed=2 * line * (width + total_rows) * cols,
            transcendentals=0,
        ),
    )(spots, *lefts, *rights)


def send_diagonal(pairs):
    if axis_len(CHIPS) != 4:
        grad = jnp.concatenate([weight_product(*pair) for pair in pairs], axis=-1)
        return (grad,), None
    parts = chip_products(pairs)
    return parts, (swap(parts[0], CHIPS, 1), swap(parts[1], CHIPS, 2))


def send_blocks(parts, got):
    if got is None:
        return parts, None
    _, _, to_y, to_x, _ = parts
    half = got[0].shape[1]
    to_y = jnp.concatenate((to_y[:, :half] + got[0], to_y[:, half:]), axis=1)
    to_x = jnp.concatenate((to_x[:, :half], to_x[:, half:] + got[1]), axis=1)
    return (to_y, to_x), (swap(to_y, CHIPS, 2), swap(to_x, CHIPS, 1))


def add_blocks(parts, got):
    if got is None:
        return lax.psum_scatter(parts[0], CHIPS, scatter_dimension=1, tiled=True)
    return (parts[4].astype(F32) + got[0].astype(F32) + got[1].astype(F32)).astype(BF16)


def scatter_line(part):
    return lax.psum_scatter(part, LINE, scatter_dimension=0, tiled=False)


def with_peer(values):
    return jnp.concatenate((values, swap(values, CORES)), axis=0)


def fold_peer(values):
    own = values.shape[0] // 2
    sent = swap(values[own:].astype(BF16), CORES)
    return values[:own] + sent.astype(F32)


def on_device(
    tokens,
    timesteps,
    labels,
    patch_cells,
    class_table,
    ada_weight,
    ada_bias,
    qkv_weight,
    qkv_bias,
    q_gain,
    k_gain,
    out_weight,
    out_bias,
    gate_up_weight,
    gate_up_bias,
    down_weight,
    down_bias,
    cotangent,
):
    core = lax.axis_index(CORES)
    line_at = lax.axis_index(LINE)
    line = axis_len(LINE)
    data = axis_len(CHIPS) * axis_len(CORES)
    devices = data * line
    images = tokens.shape[0]
    own_images = images // line
    width = class_table.shape[1]
    chunk = ada_weight.shape[2]
    highest = lax.Precision.HIGHEST

    rows_w = qkv_weight.shape[0]
    head_cols = qkv_weight.shape[2] // 2
    ff_cols = gate_up_weight.shape[2] // 2

    def column_halves(which):
        qkv_half = lax.dynamic_slice_in_dim(qkv_weight, which * head_cols, head_cols, 2)
        out_half = lax.dynamic_slice_in_dim(out_weight, which * head_cols, head_cols, 0)
        gu_half = lax.dynamic_slice_in_dim(gate_up_weight, which * ff_cols, ff_cols, 2)
        down_half = lax.dynamic_slice_in_dim(down_weight, which * ff_cols, ff_cols, 0)
        return jnp.concatenate(
            (
                qkv_half.reshape(rows_w, 3 * head_cols),
                out_half.T,
                gu_half.reshape(rows_w, 2 * ff_cols),
                down_half.T,
            ),
            axis=1,
        )

    kept = column_halves(core)
    got = swap(column_halves(1 - core), CORES)
    both = jnp.concatenate(
        (jnp.where(core == 0, kept, got), jnp.where(core == 0, got, kept)), axis=0
    )
    attn_cols = 4 * head_cols
    held_attn = gather_line(both[:, :attn_cols])
    held_gu = gather_line(both[:, attn_cols : attn_cols + 2 * ff_cols])
    down_piece = both[:, attn_cols + 2 * ff_cols :]
    held_down = gather_line(jnp.pad(down_piece, ((0, 0), (0, PAD))))

    small_in = jnp.stack((labels, timesteps))
    small_in = lax.all_to_all(
        jnp.broadcast_to(small_in, (data,) + small_in.shape), DATA, 0, 0, tiled=True
    )
    labels_all = small_in[:, 0].reshape(data * images)
    steps_all = small_in[:, 1].reshape(data * images)
    one_hot = (labels_all[:, None] == jnp.arange(CLASSES, dtype=jnp.int32)[None, :]).astype(BF16)
    cond = jnp.dot(one_hot, class_table, preferred_element_type=F32)
    cond = cond + wave_columns(steps_all, line_at * width, width)
    cond_low = jax.nn.silu(cond).astype(BF16)
    ada_flat = ada_weight.reshape(width, 6 * chunk)
    mod_part = jnp.dot(cond_low, ada_flat, preferred_element_type=F32)
    bias_in = jnp.concatenate((qkv_bias.reshape(-1), gate_up_bias.reshape(-1))).astype(F32)
    bias_len = bias_in.shape[0]
    share = -(-bias_len // data)
    bias_in = jnp.pad(bias_in, (0, share * data - bias_len)).reshape(data, share)
    data_at = lax.axis_index(CHIPS) * axis_len(CORES) + core
    bias_in = lax.dynamic_index_in_dim(bias_in, data_at, 0, keepdims=True)
    mod_part = mod_part.reshape(devices, own_images * 6 * chunk)
    mod_part = jnp.concatenate((mod_part, jnp.broadcast_to(bias_in, (devices, share))), axis=1)
    mod_part = lax.all_to_all(mod_part, EVERY, 0, 0, tiled=True)
    bias_all = mod_part[:, own_images * 6 * chunk :].reshape(data, line, share)
    bias_all = bias_all.transpose(1, 0, 2).reshape(line, data * share)[:, :bias_len]
    mod_part = mod_part[:, : own_images * 6 * chunk]
    mod = jnp.sum(mod_part.reshape(data, line, own_images, 6, chunk), axis=1)
    mod = mod.transpose(1, 2, 0, 3).reshape(own_images, 6, D) + ada_bias.astype(F32)
    shift_a, scale_a, gate_a, shift_f, scale_f, gate_f = (mod[:, k : k + 1] for k in range(6))

    cells = lax.dynamic_slice_in_dim(patch_cells, line_at * own_images, own_images, 0)
    repeat = head_cols // HEAD_DIM
    cosines, sines = rotary_tables(with_peer(cells), repeat)
    gains = jnp.tile(jnp.stack((q_gain, k_gain)).astype(F32)[:, None], (1, 1, repeat))
    same, turn = head_tables(head_cols)

    x_rows = to_whole(after(tokens, cond_low))
    attn_arrived, cosines, sines = lax.optimization_barrier(
        (first_hop(held_attn), cosines, sines)
    )
    _, attn_last = second_hop(attn_arrived)
    x_rows = after(x_rows, attn_last).astype(F32)
    held_gu = after(held_gu, attn_last)
    gu_arrived = first_hop(held_gu)
    qkv_b = bias_all[:, : 6 * head_cols].reshape(line, 3, 2, head_cols)
    qkv_b = lax.dynamic_index_in_dim(qkv_b, core, 2, keepdims=False).reshape(line, 1, 3 * head_cols)
    gu_b = bias_all[:, 6 * head_cols :].reshape(line, 2, 2, ff_cols)
    gu_b = lax.dynamic_index_in_dim(gu_b, core, 2, keepdims=False).reshape(line, 1, 2 * ff_cols)
    attn_own = modulate(x_rows, shift_a, scale_a).astype(BF16)
    attn_peer = swap(attn_own, CORES)
    w_attn = whole_weight(held_attn, attn_arrived, attn_last)
    w_attn = w_attn.reshape(line, D, attn_cols)
    patches = x_rows.shape[1]
    rows_all = 2 * own_images * patches
    tables = (gains, cosines.reshape(rows_all, -1), sines.reshape(rows_all, -1), same, turn)
    qkv, heads_out, part_own, part_peer = attn_forward(
        after(attn_own, held_gu), attn_peer, w_attn, qkv_b, *tables
    )
    part_peer = swap(part_peer, CORES)
    gu_passed, gu_last = second_hop(gu_arrived)
    part_own = after(part_own, gu_passed, held_down)
    held_down = after(held_down[:, :, :ff_cols], gu_last)
    down_arrived = first_hop(held_down)
    attn = part_own.astype(F32) + part_peer.astype(F32) + out_bias.astype(F32)

    def as_rows(*values):
        return [value.reshape(own_images * patches, D) for value in values]

    mid = x_rows + gate_a * attn
    ffn_own = modulate(mid, shift_f, scale_f).astype(BF16)
    ffn_peer = swap(ffn_own, CORES)
    grad_out = to_whole(after(cotangent, heads_out)).astype(F32)
    d_ffn_f = gate_f * grad_out
    d_ffn_own = d_ffn_f.astype(BF16)
    d_ffn_peer = swap(d_ffn_own, CORES)
    w_gu = whole_weight(held_gu, gu_arrived, gu_last).reshape(line, D, 2 * ff_cols)
    down_passed, down_last = second_hop(after(down_arrived, w_gu))
    gate_up, hidden = ffn_forward(after(ffn_own, down_passed), ffn_peer, w_gu, gu_b)
    down_parts, down_got = send_diagonal(
        [(as_rows(d_ffn_own, d_ffn_peer), after(hidden, down_last))]
    )
    w_down = whole_weight(held_down, down_arrived, down_last).reshape(line, D, ff_cols)
    d_gu, d_in_own, d_in_peer, gu_bias_part = ffn_backward(
        after(d_ffn_own, down_parts), d_ffn_peer, w_down, w_gu, gate_up
    )
    d_in_peer = swap(d_in_peer, CORES)
    down_sent, down_blocks = send_blocks(down_parts, after(down_got, d_gu))
    gu_parts, gu_got = send_diagonal(
        [(as_rows(ffn_own, ffn_peer), after(d_gu, down_sent))]
    )
    ffn = jnp.einsum("zrf,zdf->rd", after(hidden, gu_parts), w_down, preferred_element_type=F32)
    ffn = fold_peer(ffn.reshape(2 * own_images, patches, D)) + down_bias.astype(F32)
    output = to_parts((mid + gate_f * ffn).astype(BF16))

    down_bias_part = jnp.sum(d_ffn_f, axis=(0, 1))
    d_gate_f = jnp.sum(grad_out * ffn, axis=1, keepdims=True)
    d_ffn_in = after(d_in_own.astype(F32) + d_in_peer.astype(F32), down_blocks)
    g_down = add_blocks(down_parts if down_blocks is not None else down_sent, down_blocks)
    g_down = scatter_line(g_down)
    mid_grad, d_shift_f, d_scale_f = jax.vjp(modulate, mid, shift_f, scale_f)[1](d_ffn_in)
    d_mid = grad_out + mid_grad
    d_attn_f = gate_a * d_mid
    out_bias_part = jnp.sum(d_attn_f, axis=(0, 1))
    d_gate_a = jnp.sum(d_mid * attn, axis=1, keepdims=True)
    d_attn_own = d_attn_f.astype(BF16)
    d_attn_peer = swap(d_attn_own, CORES)
    gu_sent, gu_blocks = send_blocks(gu_parts, gu_got)
    d_qkv, d_in_own, d_in_peer, qkv_bias_part, gain_part = attn_backward(
        after(d_attn_own, gu_sent), d_attn_peer, w_attn, qkv, *tables
    )
    d_in_peer = swap(d_in_peer, CORES)
    attn_parts, attn_got = send_diagonal(
        [
            (as_rows(attn_own, attn_peer), after(d_qkv, output)),
            (as_rows(d_attn_own, d_attn_peer), heads_out),
        ]
    )
    g_gu = add_blocks(gu_parts if gu_blocks is not None else gu_sent, after(gu_blocks, attn_parts))
    g_gu = scatter_line(after(g_gu, g_down))
    gain_part = gain_part.reshape(2, repeat, HEAD_DIM).sum(axis=1)
    d_attn_in = d_in_own.astype(F32) + d_in_peer.astype(F32)
    row_grad, d_shift_a, d_scale_a = jax.vjp(modulate, x_rows, shift_a, scale_a)[1](d_attn_in)
    tokens_sent = (d_mid + row_grad).astype(BF16)

    d_mod = jnp.concatenate(
        (d_shift_a, d_scale_a, d_gate_a, d_shift_f, d_scale_f, d_gate_f), axis=1
    )
    ada_bias_part = jnp.sum(d_mod, axis=0)
    d_mod_low = d_mod.astype(BF16).reshape(own_images, 6, data, chunk).transpose(2, 0, 1, 3)
    d_mod_low = jnp.broadcast_to(
        d_mod_low[:, None], (data, line, own_images, 6, chunk)
    ).reshape(devices, own_images * 6 * chunk)
    attn_got, tokens_sent = lax.optimization_barrier((attn_got, tokens_sent))
    tokens_grad = to_parts(tokens_sent)
    attn_sent, attn_blocks = send_blocks(attn_parts, attn_got)
    d_mod_all = lax.all_to_all(d_mod_low, EVERY, 0, 0, tiled=True)
    d_mod_all = d_mod_all.reshape(data * images, 6 * chunk)
    g_ada = jnp.einsum("bc,be->ce", cond_low, d_mod_all, preferred_element_type=F32)
    g_ada = g_ada.reshape(width, 6, chunk)
    d_silu = jnp.einsum("be,ce->bc", d_mod_all, ada_flat, preferred_element_type=F32)
    d_cond = jax.vjp(jax.nn.silu, cond)[1](d_silu)[0]

    def by_core(part, groups, cols):
        spread = jnp.zeros((line, groups, 2, cols), F32)
        return lax.dynamic_update_slice(
            spread, part.reshape(line, groups, 1, cols), (0, 0, core, 0)
        )

    parts = (
        by_core(qkv_bias_part, 3, head_cols),
        by_core(gu_bias_part, 2, ff_cols),
        ada_bias_part,
        out_bias_part,
        down_bias_part,
        gain_part[0],
        gain_part[1],
    )
    flat = jnp.concatenate([part.reshape(-1) for part in parts])
    count = flat.shape[0]
    flat = jnp.concatenate((flat, d_cond.reshape(-1)))
    flat = sum_by_swaps(sum_by_swaps(flat, CORES), CHIPS)
    g_attn = add_blocks(attn_parts, attn_blocks)
    g_attn, tokens_grad = lax.optimization_barrier((after(g_attn, g_gu), tokens_grad))
    g_attn = scatter_line(g_attn)
    d_cond = flat[count:].reshape(d_cond.shape)
    flat = sum_by_swaps(flat[:count], LINE)
    sums = []
    at = 0
    for part in parts:
        sums.append(flat[at : at + part.size].reshape(part.shape))
        at += part.size
    qkv_bias_grad = lax.dynamic_index_in_dim(sums[0], line_at, 0, keepdims=False)
    gu_bias_grad = lax.dynamic_index_in_dim(sums[1], line_at, 0, keepdims=False)
    tokens_grad = tokens_grad.astype(F32)
    table_grad = jnp.dot(one_hot.astype(F32).T, d_cond, precision=highest)

    def own_rows(part):
        kept = lax.dynamic_slice_in_dim(part, core * rows_w, rows_w, 0)
        got = swap(lax.dynamic_slice_in_dim(part, (1 - core) * rows_w, rows_w, 0), CORES)
        low_half = jnp.where(core == 0, kept, got).astype(F32)
        high_half = jnp.where(core == 0, got, kept).astype(F32)

        def joined(first, groups, cols):
            halves = [
                half[:, first : first + groups * cols].reshape(rows_w, groups, cols)
                for half in (low_half, high_half)
            ]
            return jnp.concatenate(halves, axis=2)

        return joined

    joined = own_rows(g_gu)
    g_gu = joined(0, 2, ff_cols)
    joined = own_rows(g_down)
    g_down = joined(0, 1, ff_cols)[:, 0].T
    joined = own_rows(g_attn)
    g_qkv = joined(0, 3, head_cols)
    g_out = joined(3 * head_cols, 1, head_cols)[:, 0].T
    return (
        output,
        tokens_grad,
        table_grad,
        g_ada,
        sums[2],
        g_qkv,
        qkv_bias_grad.reshape(qkv_bias.shape),
        sums[5],
        sums[6],
        g_out,
        sums[3],
        g_gu,
        gu_bias_grad.reshape(gate_up_bias.shape),
        g_down,
        sums[4],
    )


def solution(mesh):
    chips = mesh.shape["dp"] // 2
    finer = Mesh(mesh.devices.reshape(chips, 2, mesh.shape["tensor"]), EVERY)
    in_specs = (
        P(DATA, LINE, None),
        P(DATA),
        P(DATA),
        P(DATA, None),
        P(None, LINE),
        P(LINE, None, DATA),
        P(),
        P(DATA, None, LINE),
        P(None, LINE),
        P(),
        P(),
        P(LINE, DATA),
        P(),
        P(DATA, None, LINE),
        P(None, LINE),
        P(LINE, DATA),
        P(),
        P(DATA, LINE, None),
    )
    out_specs = (
        P(DATA, LINE, None),
        P(DATA, LINE, None),
        P(None, LINE),
        P(LINE, None, DATA),
        P(),
        P(DATA, None, LINE),
        P(None, LINE),
        P(),
        P(),
        P(LINE, DATA),
        P(),
        P(DATA, None, LINE),
        P(None, LINE),
        P(LINE, DATA),
        P(),
    )
    return jax.shard_map(
        on_device, mesh=finer, in_specs=in_specs, out_specs=out_specs, check_vma=False
    )
```

```python
import functools
import math

import jax
import jax.numpy as jnp
from jax import lax
from jax.experimental import pallas as pl
from jax.experimental.pallas import tpu as pltpu
from jax.sharding import Mesh
from jax.sharding import PartitionSpec as P

D = 1152
HEAD_DIM = 72
CLASSES = 1000
GRID = 16
F32 = jnp.float32
BF16 = jnp.bfloat16
INV_ROOT = 1.0 / math.sqrt(HEAD_DIM)
CHIPS = "p"
CORES = "c"
LINE = "t"
PAD = 128
EVERY = (CHIPS, CORES, LINE)
DATA = (CHIPS, CORES)


def rms_rows(values):
    return values * lax.rsqrt(jnp.mean(values * values, axis=-1, keepdims=True) + 1e-06)


def modulate(values, shift_rows, scale_rows):
    return rms_rows(values) * (1.0 + scale_rows) + shift_rows


def rotary_tables(patch_cells, repeat):
    entry = jnp.arange(repeat * HEAD_DIM, dtype=jnp.int32) % HEAD_DIM
    half = HEAD_DIM // 2
    step = (entry % half // 2).astype(F32)
    rates = 10000.0 ** (-4.0 * step / HEAD_DIM)
    cells = patch_cells[..., None]
    place = jnp.where(entry < half, cells // GRID, cells % GRID).astype(F32)
    angles = place * rates
    return jnp.cos(angles), jnp.sin(angles)


def wave_columns(timesteps, first, width):
    half_width = D // 2
    columns = first + jnp.arange(width, dtype=jnp.int32)
    is_cos = columns < half_width
    spot = jnp.where(is_cos, columns, columns - half_width).astype(F32)
    rates = jnp.exp(-math.log(10000.0) * spot / half_width)
    phases = timesteps.astype(F32)[:, None] * rates[None, :]
    return jnp.where(is_cos[None, :], jnp.cos(phases), jnp.sin(phases))


def dot_rows(a, b):
    return lax.dot_general(a, b, (((1,), (0,)), ((), ())), preferred_element_type=F32)


def dot_last(a, b):
    return lax.dot_general(a, b, (((1,), (1,)), ((), ())), preferred_element_type=F32)


def dot_first(a, b):
    return lax.dot_general(a, b, (((0,), (0,)), ((), ())), preferred_element_type=F32)


def head_tables(cols):
    lane = lax.broadcasted_iota(jnp.int32, (cols, cols), 0)
    other = lax.broadcasted_iota(jnp.int32, (cols, cols), 1)
    same = jnp.where(lane // HEAD_DIM == other // HEAD_DIM, 1.0, 0.0).astype(BF16)
    even = other % 2 == 0
    turn = jnp.where(even & (lane == other + 1), -1.0, 0.0)
    turn = jnp.where(jnp.logical_not(even) & (lane == other - 1), 1.0, turn).astype(BF16)
    return same, turn


def unit_heads(values, same):
    mean_sq = dot_rows((values * values).astype(BF16), same) * (1.0 / HEAD_DIM)
    scale = lax.rsqrt(mean_sq + 1e-06)
    return values * scale, scale


def turn_heads(values, cosines, sines, turn):
    return values * cosines + dot_rows(values.astype(BF16), turn) * sines


def head_masks(cols):
    lane = lax.broadcasted_iota(jnp.int32, (1, cols), 1)
    return [
        (lane >= h * HEAD_DIM) & (lane < (h + 1) * HEAD_DIM) for h in range(cols // HEAD_DIM)
    ]


def attn_forward_kernel(
    own_ref, peer_ref, w_ref, b_ref, g_ref, cos_ref, sin_ref, same_ref, turn_ref,
    qkv_ref, heads_ref, own_out, peer_out, x_all, total,
):
    hc = w_ref.shape[2] // 4
    images, patches, width = own_ref.shape
    side = images * patches
    same, turn = same_ref[...], turn_ref[...]
    masks = head_masks(hc)
    at = pl.program_id(0)

    @pl.when(at == 0)
    def _():
        x_all[:side] = own_ref[...].reshape(side, width)
        x_all[side:] = peer_ref[...].reshape(side, width)

    qkv = dot_rows(x_all[...], w_ref[0, :, : 3 * hc]) + b_ref[0]
    qkv_ref[0] = qkv.astype(BF16)
    tables = (cos_ref[...], sin_ref[...])
    q_rot = unit_heads(qkv[:, :hc], same)[0] * (g_ref[0] * INV_ROOT)
    q_rot = turn_heads(q_rot, *tables, turn).astype(BF16)
    k_rot = unit_heads(qkv[:, hc : 2 * hc], same)[0] * g_ref[1]
    k_rot = turn_heads(k_rot, *tables, turn).astype(BF16)
    v_all = qkv[:, 2 * hc :].astype(BF16)
    v_all = jnp.concatenate((v_all, jnp.ones((2 * side, 256 - hc), BF16)), axis=1)
    q_heads = [jnp.where(mine, q_rot, jnp.zeros_like(q_rot)) for mine in masks]
    outs = []
    for image in range(2 * images):
        rows_at = slice(image * patches, (image + 1) * patches)
        k, v = k_rot[rows_at], v_all[rows_at]
        heads = None
        for q, mine in zip(q_heads, masks):
            expo = jnp.exp(dot_last(q[rows_at], k)).astype(BF16)
            part = dot_rows(expo, v)
            part = part[:, :hc] * (1.0 / part[:, hc : hc + 1])
            heads = part if heads is None else jnp.where(mine, part, heads)
        outs.append(heads.astype(BF16))
    heads = jnp.concatenate(outs, axis=0)
    heads_ref[0] = heads
    @pl.when(at == 0)
    def _():
        total[...] = dot_last(heads, w_ref[0, :, 3 * hc :])

    @pl.when(at > 0)
    def _():
        total[...] += dot_last(heads, w_ref[0, :, 3 * hc :])

    @pl.when(at == pl.num_programs(0) - 1)
    def _():
        own_out[...] = total[:side].reshape(images, patches, width).astype(BF16)
        peer_out[...] = total[side:].reshape(images, patches, width).astype(BF16)


def attn_backward_kernel(
    own_ref, peer_ref, w_ref, qkv_in_ref, g_ref, cos_ref, sin_ref, same_ref, turn_ref,
    dqkv_ref, own_out, peer_out, bias_ref, gain_ref, x_all, total,
):
    hc = w_ref.shape[2] // 4
    images, patches, width = own_ref.shape
    side = images * patches
    same, turn = same_ref[...], turn_ref[...]
    masks = head_masks(hc)
    at = pl.program_id(0)

    @pl.when(at == 0)
    def _():
        gain_ref[...] = jnp.zeros_like(gain_ref)
        x_all[:side] = own_ref[...].reshape(side, width)
        x_all[side:] = peer_ref[...].reshape(side, width)

    tables = (cos_ref[...], sin_ref[...])
    d_heads_all = dot_rows(x_all[...], w_ref[0, :, 3 * hc :]).astype(BF16)
    qkv = qkv_in_ref[0]
    v_all = qkv[:, 2 * hc :]
    uq, rq = unit_heads(qkv[:, :hc].astype(F32), same)
    uk, rk = unit_heads(qkv[:, hc : 2 * hc].astype(F32), same)
    q_rot = turn_heads(uq * (g_ref[0] * INV_ROOT), *tables, turn).astype(BF16)
    k_rot = turn_heads(uk * g_ref[1], *tables, turn).astype(BF16)
    zero = jnp.zeros_like(q_rot)
    q_heads = [jnp.where(mine, q_rot, zero) for mine in masks]
    v_heads = [jnp.where(mine, v_all, zero) for mine in masks]
    grads = ([], [], [])
    for image in range(2 * images):
        rows_at = slice(image * patches, (image + 1) * patches)
        q, k, d_heads = q_rot[rows_at], k_rot[rows_at], d_heads_all[rows_at]
        here = [None, None, None]
        for head, mine in enumerate(masks):
            expo = jnp.exp(dot_last(k, q_heads[head][rows_at]))
            probs = expo * (1.0 / jnp.sum(expo, axis=0, keepdims=True))
            d_probs = dot_last(v_heads[head][rows_at], d_heads)
            mean = jnp.sum(d_probs * probs, axis=0, keepdims=True)
            d_scores = (probs * (d_probs - mean)).astype(BF16)
            parts = (
                dot_first(d_scores, k),
                dot_rows(d_scores, q),
                dot_rows(probs.astype(BF16), d_heads),
            )
            here = [
                new if old is None else jnp.where(mine, new, old)
                for new, old in zip(parts, here)
            ]
        for which in range(3):
            grads[which].append(here[which])
    d_q, d_k, d_v = (jnp.concatenate(part, axis=0) for part in grads)
    sides = []
    for which, (grad, unit, scale) in enumerate(((d_q * INV_ROOT, uq, rq), (d_k, uk, rk))):
        back = grad * tables[0] + dot_last((grad * tables[1]).astype(BF16), turn)
        gain_ref[which : which + 1] += jnp.sum(back * unit, axis=0, keepdims=True)
        back = back * g_ref[which]
        mean = dot_rows((back * unit).astype(BF16), same) * (1.0 / HEAD_DIM)
        sides.append((back - unit * mean) * scale)
    d_qkv = jnp.concatenate((sides[0], sides[1], d_v), axis=1)
    bias_ref[0] = jnp.sum(d_qkv, axis=0, keepdims=True)
    d_qkv = d_qkv.astype(BF16)
    dqkv_ref[0] = d_qkv
    @pl.when(at == 0)
    def _():
        total[...] = dot_last(d_qkv, w_ref[0, :, : 3 * hc])

    @pl.when(at > 0)
    def _():
        total[...] += dot_last(d_qkv, w_ref[0, :, : 3 * hc])

    @pl.when(at == pl.num_programs(0) - 1)
    def _():
        own_out[...] = total[:side].reshape(images, patches, width).astype(BF16)
        peer_out[...] = total[side:].reshape(images, patches, width).astype(BF16)


def resident(shape):
    return pl.BlockSpec(shape, lambda i: (0,) * len(shape))


def by_line(shape):
    return pl.BlockSpec((1,) + shape, lambda i: (i,) + (0,) * len(shape))


def attn_cost(x, w, products):
    images, patches, width = x.shape
    line, _, cols = w.shape
    pairs = 2 * images * line * (cols // (4 * HEAD_DIM)) * patches * patches
    return pl.CostEstimate(
        flops=4 * images * patches * width * line * cols + products * 2 * pairs * 256,
        bytes_accessed=w.size * 2 + x.size * 16,
        transcendentals=pairs,
    )


def attn_forward(own, peer, w, b, *tables):
    images, patches, width = own.shape
    line, _, cols = w.shape
    hc = cols // 4
    rows = 2 * images * patches
    return pl.pallas_call(
        attn_forward_kernel,
        grid=(line,),
        in_specs=[resident(own.shape)] * 2
        + [by_line(w.shape[1:]), by_line(b.shape[1:])]
        + [resident(table.shape) for table in tables],
        out_specs=[by_line((rows, 3 * hc)), by_line((rows, hc))]
        + [resident(own.shape)] * 2,
        out_shape=[
            jax.ShapeDtypeStruct((line, rows, 3 * hc), BF16),
            jax.ShapeDtypeStruct((line, rows, hc), BF16),
        ]
        + [jax.ShapeDtypeStruct(own.shape, BF16)] * 2,
        scratch_shapes=[pltpu.VMEM((rows, width), BF16), pltpu.VMEM((rows, width), F32)],
        compiler_params=pltpu.CompilerParams(vmem_limit_bytes=50 << 20),
        cost_estimate=attn_cost(own, w, 2),
    )(own, peer, w, b, *tables)


def attn_backward(own, peer, w, qkv, *tables):
    images, patches, width = own.shape
    line, _, cols = w.shape
    hc = cols // 4
    rows = 2 * images * patches
    return pl.pallas_call(
        attn_backward_kernel,
        grid=(line,),
        in_specs=[resident(own.shape)] * 2
        + [by_line(w.shape[1:]), by_line(qkv.shape[1:])]
        + [resident(table.shape) for table in tables],
        out_specs=[by_line((rows, 3 * hc))]
        + [resident(own.shape)] * 2
        + [by_line((1, 3 * hc)), resident((2, hc))],
        out_shape=[jax.ShapeDtypeStruct((line, rows, 3 * hc), BF16)]
        + [jax.ShapeDtypeStruct(own.shape, BF16)] * 2
        + [jax.ShapeDtypeStruct((line, 1, 3 * hc), F32), jax.ShapeDtypeStruct((2, hc), F32)],
        scratch_shapes=[pltpu.VMEM((rows, width), BF16), pltpu.VMEM((rows, width), F32)],
        compiler_params=pltpu.CompilerParams(vmem_limit_bytes=50 << 20),
        cost_estimate=attn_cost(own, w, 5),
    )(own, peer, w, qkv, *tables)


def ffn_forward_kernel(
    own_ref, peer_ref, w_ref, b_ref, gu_ref, hidden_ref, x_all,
):
    ff = hidden_ref.shape[2]
    images, patches, width = own_ref.shape
    side = images * patches

    @pl.when(pl.program_id(0) == 0)
    def _():
        x_all[:side] = own_ref[...].reshape(side, width)
        x_all[side:] = peer_ref[...].reshape(side, width)

    made = dot_rows(x_all[...], w_ref[0]) + b_ref[0]
    gu_ref[0] = made.astype(BF16)
    gate, up = made[:, :ff], made[:, ff:]
    hidden_ref[0] = (gate * up / (1.0 + jnp.exp(-gate))).astype(BF16)


def ffn_forward(own, peer, w, b):
    images, patches, width = own.shape
    line, _, cols = w.shape
    rows = 2 * images * patches
    return pl.pallas_call(
        ffn_forward_kernel,
        grid=(line,),
        in_specs=[resident(own.shape)] * 2
        + [by_line(w.shape[1:]), by_line(b.shape[1:])],
        out_specs=[by_line((rows, cols)), by_line((rows, cols // 2))],
        out_shape=[
            jax.ShapeDtypeStruct((line, rows, cols), BF16),
            jax.ShapeDtypeStruct((line, rows, cols // 2), BF16),
        ],
        scratch_shapes=[pltpu.VMEM((rows, width), BF16)],
        compiler_params=pltpu.CompilerParams(vmem_limit_bytes=50 << 20),
        cost_estimate=pl.CostEstimate(
            flops=2 * rows * width * line * cols,
            bytes_accessed=2 * line * cols * (width + 2 * rows),
            transcendentals=line * rows * cols // 2,
        ),
    )(own, peer, w, b)


def ffn_backward_kernel(
    own_ref, peer_ref, down_ref, w_ref, gu_ref,
    d_gu_ref, own_out, peer_out, bias_ref, x_all, total,
):
    ff = down_ref.shape[2]
    images, patches, width = own_ref.shape
    side = images * patches
    at = pl.program_id(0)

    @pl.when(at == 0)
    def _():
        x_all[:side] = own_ref[...].reshape(side, width)
        x_all[side:] = peer_ref[...].reshape(side, width)

    d_hidden = dot_rows(x_all[...], down_ref[0])
    gate, up = gu_ref[0, :, :ff].astype(F32), gu_ref[0, :, ff:].astype(F32)
    sig = 1.0 / (1.0 + jnp.exp(-gate))
    silu = gate * sig
    d_up = d_hidden * silu
    d_gate = d_hidden * up * (sig + silu * (1.0 - sig))
    bias_ref[0, :, :ff] = jnp.sum(d_gate, axis=0, keepdims=True)
    bias_ref[0, :, ff:] = jnp.sum(d_up, axis=0, keepdims=True)
    d_gu_ref[0, :, :ff] = d_gate.astype(BF16)
    d_gu_ref[0, :, ff:] = d_up.astype(BF16)
    @pl.when(at == 0)
    def _():
        total[...] = dot_last(d_gu_ref[0], w_ref[0])

    @pl.when(at > 0)
    def _():
        total[...] += dot_last(d_gu_ref[0], w_ref[0])

    @pl.when(at == pl.num_programs(0) - 1)
    def _():
        own_out[...] = total[:side].reshape(images, patches, width).astype(BF16)
        peer_out[...] = total[side:].reshape(images, patches, width).astype(BF16)


def ffn_backward(own, peer, w_down, w_gu, gate_up):
    images, patches, width = own.shape
    line, rows, cols = gate_up.shape
    return pl.pallas_call(
        ffn_backward_kernel,
        grid=(line,),
        in_specs=[resident(own.shape)] * 2
        + [by_line(w_down.shape[1:]), by_line(w_gu.shape[1:]), by_line((rows, cols))],
        out_specs=[by_line((rows, cols))] + [resident(own.shape)] * 2 + [by_line((1, cols))],
        out_shape=[jax.ShapeDtypeStruct((line, rows, cols), BF16)]
        + [jax.ShapeDtypeStruct(own.shape, BF16)] * 2
        + [jax.ShapeDtypeStruct((line, 1, cols), F32)],
        scratch_shapes=[pltpu.VMEM((rows, width), BF16), pltpu.VMEM((rows, width), F32)],
        compiler_params=pltpu.CompilerParams(vmem_limit_bytes=50 << 20),
        cost_estimate=pl.CostEstimate(
            flops=3 * rows * width * line * cols,
            bytes_accessed=2 * line * cols * (2 * width + 2 * rows),
            transcendentals=line * rows * cols // 2,
        ),
    )(own, peer, w_down, w_gu, gate_up)


def after(values, *others):
    return lax.optimization_barrier((values, others))[0]


def axis_len(name):
    return lax.axis_size(name)


def swap(values, name, bit=1):
    count = axis_len(name)
    return lax.ppermute(values, name, [(i, i ^ bit) for i in range(count)])


def sum_by_swaps(values, name):
    count = axis_len(name)
    bit = 1
    while bit < count:
        values = values + swap(values, name, bit)
        bit *= 2
    return values


def place_kernel(half, spot_ref, own_ref, x_ref, y_ref, da_ref, db_ref, out_ref):
    at = pl.program_id(0)
    out_ref[0, spot_ref[0]] = own_ref[0]
    out_ref[0, spot_ref[1]] = x_ref[0]
    out_ref[0, spot_ref[2]] = y_ref[0]

    @pl.when(at < half)
    def _():
        out_ref[0, spot_ref[3]] = da_ref[0]

    @pl.when(at >= half)
    def _():
        out_ref[0, spot_ref[3]] = db_ref[0]


def place_parts(own, from_x, from_y, diag_a, diag_b):
    line, rows, cols = own.shape
    half = diag_a.shape[0]
    spots = lax.axis_index(CHIPS) ^ jnp.arange(4, dtype=jnp.int32)
    straight = pl.BlockSpec((1, rows, cols), lambda i: (i, 0, 0))
    early = pl.BlockSpec((1, rows, cols), lambda i: (jnp.minimum(i, half - 1), 0, 0))
    late = pl.BlockSpec((1, rows, cols), lambda i: (jnp.maximum(i - half, 0), 0, 0))
    return pl.pallas_call(
        functools.partial(place_kernel, half),
        grid=(line,),
        in_specs=[pl.BlockSpec(memory_space=pltpu.SMEM)] + [straight] * 3 + [early, late],
        out_specs=pl.BlockSpec((1, 4, rows, cols), lambda i: (i, 0, 0, 0)),
        out_shape=jax.ShapeDtypeStruct((line, 4, rows, cols), own.dtype),
        compiler_params=pltpu.CompilerParams(vmem_limit_bytes=40 << 20),
        cost_estimate=pl.CostEstimate(flops=0, bytes_accessed=16 * own.size, transcendentals=0),
    )(spots, own, from_x, from_y, diag_a, diag_b)


def to_whole(values):
    line = axis_len(LINE)
    images, patches, width = values.shape
    moved = values.reshape(line, images // line, patches, width)
    moved = lax.all_to_all(moved, LINE, 0, 0, tiled=True)
    return moved.transpose(1, 0, 2, 3).reshape(images // line, line * patches, width)


def to_parts(values):
    line = axis_len(LINE)
    images, patches, width = values.shape
    moved = values.reshape(images, line, patches // line, width).transpose(1, 0, 2, 3)
    moved = lax.all_to_all(moved, LINE, 0, 0, tiled=True)
    return moved.reshape(images * line, patches // line, width)


def gather_line(piece):
    return lax.all_gather(piece, LINE, axis=0)


def first_hop(held):
    if axis_len(CHIPS) != 4:
        return (held,)
    return swap(held, CHIPS, 1), swap(held, CHIPS, 2)


def second_hop(arrived):
    if len(arrived) == 1:
        return arrived, arrived
    half = arrived[0].shape[0] // 2
    low, high = arrived[0][:half], arrived[1][half:]
    return (low, high), (swap(low, CHIPS, 2), swap(high, CHIPS, 1))


def whole_weight(held, arrived, last):
    if len(arrived) == 1:
        return lax.all_gather(held, CHIPS, axis=1, tiled=True)[:, None]
    return place_parts(held, *arrived, *last)


def weight_product(lefts, right):
    left = jnp.concatenate(lefts, axis=0)
    return jnp.einsum("rd,zrn->zdn", left, right, preferred_element_type=F32).astype(BF16)


def grad_kernel(counts, spot_ref, *refs):
    lefts, refs = refs[: sum(counts)], refs[sum(counts) :]
    rights, refs = refs[: len(counts)], refs[len(counts) :]
    outs, scratch = refs[:5], refs[5:]
    plain, turned = scratch[0], scratch[1:]
    rows = outs[4].shape[1]
    half = rows // 2

    @pl.when(pl.program_id(0) == 0)
    def _():
        for pair, count in enumerate(counts):
            at = 0
            for left in lefts[sum(counts[:pair]) : sum(counts[:pair]) + count]:
                plain[:, at : at + left.shape[0]] = left[...].T
                at += left.shape[0]
            for place in range(4):
                turned[pair][place * rows : (place + 1) * rows] = plain[
                    pl.ds(pl.multiple_of(spot_ref[place] * rows, rows), rows)
                ]

    first = 0
    for pair, right in enumerate(rights):
        last = first + right.shape[-1]
        made = dot_rows(turned[pair][...], right[0]).astype(BF16)
        top = 0
        for out, count in zip(outs, (half, rows - half, rows, rows, rows)):
            out[0, :, first:last] = made[top : top + count]
            top += count
        first = last


def chip_products(pairs):
    line, total_rows, _ = pairs[0][1].shape
    width = pairs[0][0][0].shape[1]
    cols = sum(right.shape[-1] for _, right in pairs)
    rows = width // 4
    half = rows // 2
    spots = lax.axis_index(CHIPS) ^ jnp.array((3, 2, 1, 0), dtype=jnp.int32)
    lefts = [left for group, _ in pairs for left in group]
    rights = [right for _, right in pairs]
    cut = (half, rows - half, rows, rows, rows)
    return pl.pallas_call(
        functools.partial(grad_kernel, tuple(len(group) for group, _ in pairs)),
        grid=(line,),
        in_specs=[pl.BlockSpec(memory_space=pltpu.SMEM)]
        + [resident(left.shape) for left in lefts]
        + [by_line(right.shape[1:]) for right in rights],
        out_specs=[by_line((count, cols)) for count in cut],
        out_shape=[jax.ShapeDtypeStruct((line, count, cols), BF16) for count in cut],
        scratch_shapes=[pltpu.VMEM((width, total_rows), BF16)] * (1 + len(pairs)),
        compiler_params=pltpu.CompilerParams(vmem_limit_bytes=50 << 20),
        cost_estimate=pl.CostEstimate(
            flops=2 * line * width * total_rows * cols,
            bytes_accessed=2 * line * (width + total_rows) * cols,
            transcendentals=0,
        ),
    )(spots, *lefts, *rights)


def send_diagonal(pairs):
    if axis_len(CHIPS) != 4:
        grad = jnp.concatenate([weight_product(*pair) for pair in pairs], axis=-1)
        return (grad,), None
    parts = chip_products(pairs)
    return parts, (swap(parts[0], CHIPS, 1), swap(parts[1], CHIPS, 2))


def send_blocks(parts, got):
    if got is None:
        return parts, None
    _, _, to_y, to_x, _ = parts
    half = got[0].shape[1]
    to_y = jnp.concatenate((to_y[:, :half] + got[0], to_y[:, half:]), axis=1)
    to_x = jnp.concatenate((to_x[:, :half], to_x[:, half:] + got[1]), axis=1)
    return (to_y, to_x), (swap(to_y, CHIPS, 2), swap(to_x, CHIPS, 1))


def add_blocks(parts, got):
    if got is None:
        return lax.psum_scatter(parts[0], CHIPS, scatter_dimension=1, tiled=True)
    return (parts[4].astype(F32) + got[0].astype(F32) + got[1].astype(F32)).astype(BF16)


def scatter_line(part):
    return lax.psum_scatter(part, LINE, scatter_dimension=0, tiled=False)


def with_peer(values):
    return jnp.concatenate((values, swap(values, CORES)), axis=0)


def fold_peer(values):
    own = values.shape[0] // 2
    sent = swap(values[own:].astype(BF16), CORES)
    return values[:own] + sent.astype(F32)


def on_device(
    tokens,
    timesteps,
    labels,
    patch_cells,
    class_table,
    ada_weight,
    ada_bias,
    qkv_weight,
    qkv_bias,
    q_gain,
    k_gain,
    out_weight,
    out_bias,
    gate_up_weight,
    gate_up_bias,
    down_weight,
    down_bias,
    cotangent,
):
    core = lax.axis_index(CORES)
    line_at = lax.axis_index(LINE)
    line = axis_len(LINE)
    data = axis_len(CHIPS) * axis_len(CORES)
    devices = data * line
    images = tokens.shape[0]
    own_images = images // line
    width = class_table.shape[1]
    chunk = ada_weight.shape[2]
    highest = lax.Precision.HIGHEST

    rows_w = qkv_weight.shape[0]
    head_cols = qkv_weight.shape[2] // 2
    ff_cols = gate_up_weight.shape[2] // 2

    def column_halves(which):
        qkv_half = lax.dynamic_slice_in_dim(qkv_weight, which * head_cols, head_cols, 2)
        out_half = lax.dynamic_slice_in_dim(out_weight, which * head_cols, head_cols, 0)
        gu_half = lax.dynamic_slice_in_dim(gate_up_weight, which * ff_cols, ff_cols, 2)
        down_half = lax.dynamic_slice_in_dim(down_weight, which * ff_cols, ff_cols, 0)
        return jnp.concatenate(
            (
                qkv_half.reshape(rows_w, 3 * head_cols),
                out_half.T,
                gu_half.reshape(rows_w, 2 * ff_cols),
                down_half.T,
            ),
            axis=1,
        )

    kept = column_halves(core)
    got = swap(column_halves(1 - core), CORES)
    both = jnp.concatenate(
        (jnp.where(core == 0, kept, got), jnp.where(core == 0, got, kept)), axis=0
    )
    attn_cols = 4 * head_cols
    held_attn = gather_line(both[:, :attn_cols])
    held_gu = gather_line(both[:, attn_cols : attn_cols + 2 * ff_cols])
    down_piece = both[:, attn_cols + 2 * ff_cols :]
    held_down = gather_line(jnp.pad(down_piece, ((0, 0), (0, PAD))))

    small_in = jnp.stack((labels, timesteps))
    small_in = lax.all_to_all(
        jnp.broadcast_to(small_in, (data,) + small_in.shape), DATA, 0, 0, tiled=True
    )
    labels_all = small_in[:, 0].reshape(data * images)
    steps_all = small_in[:, 1].reshape(data * images)
    one_hot = (labels_all[:, None] == jnp.arange(CLASSES, dtype=jnp.int32)[None, :]).astype(BF16)
    cond = jnp.dot(one_hot, class_table, preferred_element_type=F32)
    cond = cond + wave_columns(steps_all, line_at * width, width)
    cond_low = jax.nn.silu(cond).astype(BF16)
    ada_flat = ada_weight.reshape(width, 6 * chunk)
    mod_part = jnp.dot(cond_low, ada_flat, preferred_element_type=F32)
    bias_in = jnp.concatenate((qkv_bias.reshape(-1), gate_up_bias.reshape(-1))).astype(F32)
    bias_len = bias_in.shape[0]
    share = -(-bias_len // data)
    bias_in = jnp.pad(bias_in, (0, share * data - bias_len)).reshape(data, share)
    data_at = lax.axis_index(CHIPS) * axis_len(CORES) + core
    bias_in = lax.dynamic_index_in_dim(bias_in, data_at, 0, keepdims=True)
    mod_part = mod_part.reshape(devices, own_images * 6 * chunk)
    mod_part = jnp.concatenate((mod_part, jnp.broadcast_to(bias_in, (devices, share))), axis=1)
    mod_part = lax.all_to_all(mod_part, EVERY, 0, 0, tiled=True)
    bias_all = mod_part[:, own_images * 6 * chunk :].reshape(data, line, share)
    bias_all = bias_all.transpose(1, 0, 2).reshape(line, data * share)[:, :bias_len]
    mod_part = mod_part[:, : own_images * 6 * chunk]
    mod = jnp.sum(mod_part.reshape(data, line, own_images, 6, chunk), axis=1)
    mod = mod.transpose(1, 2, 0, 3).reshape(own_images, 6, D) + ada_bias.astype(F32)
    shift_a, scale_a, gate_a, shift_f, scale_f, gate_f = (mod[:, k : k + 1] for k in range(6))

    cells = lax.dynamic_slice_in_dim(patch_cells, line_at * own_images, own_images, 0)
    repeat = head_cols // HEAD_DIM
    cosines, sines = rotary_tables(with_peer(cells), repeat)
    gains = jnp.tile(jnp.stack((q_gain, k_gain)).astype(F32)[:, None], (1, 1, repeat))
    same, turn = head_tables(head_cols)

    x_rows = to_whole(after(tokens, cond_low))
    qkv_b = bias_all[:, : 6 * head_cols].reshape(line, 3, 2, head_cols)
    qkv_b = lax.dynamic_index_in_dim(qkv_b, core, 2, keepdims=False).reshape(line, 1, 3 * head_cols)
    gu_b = bias_all[:, 6 * head_cols :].reshape(line, 2, 2, ff_cols)
    gu_b = lax.dynamic_index_in_dim(gu_b, core, 2, keepdims=False).reshape(line, 1, 2 * ff_cols)
    ready = (cosines, sines, qkv_b, gu_b)
    attn_arrived, ready = lax.optimization_barrier((first_hop(held_attn), ready))
    cosines, sines, qkv_b, gu_b = ready
    _, attn_last = second_hop(attn_arrived)
    x_rows = after(x_rows, attn_last).astype(F32)
    held_gu = after(held_gu, attn_last)
    gu_arrived = first_hop(held_gu)

    attn_own = modulate(x_rows, shift_a, scale_a).astype(BF16)
    attn_peer = swap(attn_own, CORES)
    w_attn = whole_weight(held_attn, attn_arrived, attn_last)
    w_attn = w_attn.reshape(line, D, attn_cols)
    patches = x_rows.shape[1]
    rows_all = 2 * own_images * patches
    tables = (gains, cosines.reshape(rows_all, -1), sines.reshape(rows_all, -1), same, turn)
    qkv, heads_out, part_own, part_peer = attn_forward(
        after(attn_own, held_gu), attn_peer, w_attn, qkv_b, *tables
    )
    part_peer = swap(part_peer, CORES)
    gu_passed, gu_last = second_hop(gu_arrived)
    part_own = after(part_own, gu_passed, held_down)
    held_down = after(held_down[:, :, :ff_cols], gu_last)
    down_arrived = first_hop(held_down)
    attn = part_own.astype(F32) + part_peer.astype(F32) + out_bias.astype(F32)

    def as_rows(*values):
        return [value.reshape(own_images * patches, D) for value in values]

    mid = x_rows + gate_a * attn
    ffn_own = modulate(mid, shift_f, scale_f).astype(BF16)
    ffn_peer = swap(ffn_own, CORES)
    grad_out = to_whole(after(cotangent, heads_out)).astype(F32)
    d_ffn_f = gate_f * grad_out
    d_ffn_own = d_ffn_f.astype(BF16)
    d_ffn_peer = swap(d_ffn_own, CORES)
    w_gu = whole_weight(held_gu, gu_arrived, gu_last).reshape(line, D, 2 * ff_cols)
    down_passed, down_last = second_hop(after(down_arrived, w_gu))
    gate_up, hidden = ffn_forward(after(ffn_own, down_passed), ffn_peer, w_gu, gu_b)
    w_down = whole_weight(held_down, down_arrived, down_last).reshape(line, D, ff_cols)
    d_gu, d_in_own, d_in_peer, gu_bias_part = ffn_backward(
        d_ffn_own, d_ffn_peer, w_down, w_gu, gate_up
    )
    d_in_peer = swap(d_in_peer, CORES)
    gu_parts, gu_got = send_diagonal(
        [(as_rows(ffn_own, ffn_peer), d_gu)]
    )
    down_parts, down_got = send_diagonal(
        [(as_rows(d_ffn_own, d_ffn_peer), after(hidden, gu_parts))]
    )
    ffn = jnp.einsum("zrf,zdf->rd", after(hidden, down_parts), w_down, preferred_element_type=F32)
    ffn = fold_peer(ffn.reshape(2 * own_images, patches, D)) + down_bias.astype(F32)
    output = to_parts((mid + gate_f * ffn).astype(BF16))

    down_bias_part = jnp.sum(d_ffn_f, axis=(0, 1))
    d_gate_f = jnp.sum(grad_out * ffn, axis=1, keepdims=True)
    d_ffn_in = after(d_in_own.astype(F32) + d_in_peer.astype(F32), gu_got)
    mid_grad, d_shift_f, d_scale_f = jax.vjp(modulate, mid, shift_f, scale_f)[1](d_ffn_in)
    d_mid = grad_out + mid_grad
    d_attn_f = gate_a * d_mid
    out_bias_part = jnp.sum(d_attn_f, axis=(0, 1))
    d_gate_a = jnp.sum(d_mid * attn, axis=1, keepdims=True)
    d_attn_own = d_attn_f.astype(BF16)
    d_attn_peer = swap(d_attn_own, CORES)
    gu_sent, gu_blocks = send_blocks(gu_parts, gu_got)
    down_sent, down_blocks = send_blocks(down_parts, after(down_got, gu_sent))
    d_qkv, d_in_own, d_in_peer, qkv_bias_part, gain_part = attn_backward(
        after(d_attn_own, gu_sent, down_sent), d_attn_peer, w_attn, qkv, *tables
    )
    d_in_peer = swap(d_in_peer, CORES)
    g_gu = add_blocks(gu_parts if gu_blocks is not None else gu_sent, after(gu_blocks, d_qkv))
    attn_parts, attn_got = send_diagonal(
        [
            (as_rows(attn_own, attn_peer), after(d_qkv, output, g_gu)),
            (as_rows(d_attn_own, d_attn_peer), heads_out),
        ]
    )
    g_gu = scatter_line(g_gu)
    qkv_bias_part, gain_part = after((qkv_bias_part, gain_part), attn_parts)
    gain_part = gain_part.reshape(2, repeat, HEAD_DIM).sum(axis=1)
    d_attn_in = d_in_own.astype(F32) + d_in_peer.astype(F32)
    row_grad, d_shift_a, d_scale_a = jax.vjp(modulate, x_rows, shift_a, scale_a)[1](d_attn_in)
    tokens_sent = (d_mid + row_grad).astype(BF16)

    g_down = add_blocks(down_parts if down_blocks is not None else down_sent, after(down_blocks, tokens_sent))
    attn_got = after(attn_got, g_down)
    g_down = scatter_line(g_down)
    attn_got = after(attn_got, g_gu, tokens_sent)
    tokens_grad = to_parts(tokens_sent)
    attn_sent, attn_blocks = send_blocks(attn_parts, attn_got)
    d_mod = jnp.concatenate(
        (d_shift_a, d_scale_a, d_gate_a, d_shift_f, d_scale_f, d_gate_f), axis=1
    )
    d_mod, tokens_grad = lax.optimization_barrier((after(d_mod, attn_sent), tokens_grad))
    ada_bias_part = jnp.sum(d_mod, axis=0)
    d_mod_low = d_mod.astype(BF16).reshape(own_images, 6, data, chunk).transpose(2, 0, 1, 3)
    d_mod_low = jnp.broadcast_to(
        d_mod_low[:, None], (data, line, own_images, 6, chunk)
    ).reshape(devices, own_images * 6 * chunk)
    d_mod_all = lax.all_to_all(d_mod_low, EVERY, 0, 0, tiled=True)
    d_mod_all = d_mod_all.reshape(data * images, 6 * chunk)
    g_ada = jnp.einsum("bc,be->ce", cond_low, d_mod_all, preferred_element_type=F32)
    g_ada = g_ada.reshape(width, 6, chunk)
    d_silu = jnp.einsum("be,ce->bc", d_mod_all, ada_flat, preferred_element_type=F32)
    d_cond = jax.vjp(jax.nn.silu, cond)[1](d_silu)[0]

    def by_core(part, groups, cols):
        spread = jnp.zeros((line, groups, 2, cols), F32)
        return lax.dynamic_update_slice(
            spread, part.reshape(line, groups, 1, cols), (0, 0, core, 0)
        )

    parts = (
        by_core(qkv_bias_part, 3, head_cols),
        by_core(gu_bias_part, 2, ff_cols),
        ada_bias_part,
        out_bias_part,
        down_bias_part,
        gain_part[0],
        gain_part[1],
    )
    flat = jnp.concatenate([part.reshape(-1) for part in parts])
    count = flat.shape[0]
    flat = jnp.concatenate((flat, d_cond.reshape(-1)))
    flat = sum_by_swaps(sum_by_swaps(flat, CORES), CHIPS)
    g_attn = add_blocks(attn_parts, attn_blocks)
    g_attn = after(g_attn, g_gu, g_down)
    g_attn = scatter_line(g_attn)
    d_cond = flat[count:].reshape(d_cond.shape)
    flat = sum_by_swaps(flat[:count], LINE)
    sums = []
    at = 0
    for part in parts:
        sums.append(flat[at : at + part.size].reshape(part.shape))
        at += part.size
    qkv_bias_grad = lax.dynamic_index_in_dim(sums[0], line_at, 0, keepdims=False)
    gu_bias_grad = lax.dynamic_index_in_dim(sums[1], line_at, 0, keepdims=False)
    tokens_grad = tokens_grad.astype(F32)
    table_grad = jnp.dot(one_hot.astype(F32).T, d_cond, precision=highest)

    def own_rows(part):
        kept = lax.dynamic_slice_in_dim(part, core * rows_w, rows_w, 0)
        got = swap(lax.dynamic_slice_in_dim(part, (1 - core) * rows_w, rows_w, 0), CORES)
        low_half = jnp.where(core == 0, kept, got).astype(F32)
        high_half = jnp.where(core == 0, got, kept).astype(F32)

        def joined(first, groups, cols):
            halves = [
                half[:, first : first + groups * cols].reshape(rows_w, groups, cols)
                for half in (low_half, high_half)
            ]
            return jnp.concatenate(halves, axis=2)

        return joined

    joined = own_rows(g_gu)
    g_gu = joined(0, 2, ff_cols)
    joined = own_rows(g_down)
    g_down = joined(0, 1, ff_cols)[:, 0].T
    joined = own_rows(g_attn)
    g_qkv = joined(0, 3, head_cols)
    g_out = joined(3 * head_cols, 1, head_cols)[:, 0].T
    return (
        output,
        tokens_grad,
        table_grad,
        g_ada,
        sums[2],
        g_qkv,
        qkv_bias_grad.reshape(qkv_bias.shape),
        sums[5],
        sums[6],
        g_out,
        sums[3],
        g_gu,
        gu_bias_grad.reshape(gate_up_bias.shape),
        g_down,
        sums[4],
    )


def solution(mesh):
    chips = mesh.shape["dp"] // 2
    finer = Mesh(mesh.devices.reshape(chips, 2, mesh.shape["tensor"]), EVERY)
    in_specs = (
        P(DATA, LINE, None),
        P(DATA),
        P(DATA),
        P(DATA, None),
        P(None, LINE),
        P(LINE, None, DATA),
        P(),
        P(DATA, None, LINE),
        P(None, LINE),
        P(),
        P(),
        P(LINE, DATA),
        P(),
        P(DATA, None, LINE),
        P(None, LINE),
        P(LINE, DATA),
        P(),
        P(DATA, LINE, None),
    )
    out_specs = (
        P(DATA, LINE, None),
        P(DATA, LINE, None),
        P(None, LINE),
        P(LINE, None, DATA),
        P(),
        P(DATA, None, LINE),
        P(None, LINE),
        P(),
        P(),
        P(LINE, DATA),
        P(),
        P(DATA, None, LINE),
        P(None, LINE),
        P(LINE, DATA),
        P(),
    )
    return jax.shard_map(
        on_device, mesh=finer, in_specs=in_specs, out_specs=out_specs, check_vma=False
    )
```

```python
import functools
import math

import jax
import jax.numpy as jnp
from jax import lax
from jax.experimental import pallas as pl
from jax.experimental.pallas import tpu as pltpu
from jax.sharding import Mesh
from jax.sharding import PartitionSpec as P

D = 1152
HEAD_DIM = 72
CLASSES = 1000
GRID = 16
F32 = jnp.float32
BF16 = jnp.bfloat16
INV_ROOT = 1.0 / math.sqrt(HEAD_DIM)
CHIPS = "p"
CORES = "c"
LINE = "t"
PAD = 128
EVERY = (CHIPS, CORES, LINE)
DATA = (CHIPS, CORES)


def rms_rows(values):
    return values * lax.rsqrt(jnp.mean(values * values, axis=-1, keepdims=True) + 1e-06)


def modulate(values, shift_rows, scale_rows):
    return rms_rows(values) * (1.0 + scale_rows) + shift_rows


def rotary_tables(patch_cells, repeat):
    entry = jnp.arange(repeat * HEAD_DIM, dtype=jnp.int32) % HEAD_DIM
    half = HEAD_DIM // 2
    step = (entry % half // 2).astype(F32)
    rates = 10000.0 ** (-4.0 * step / HEAD_DIM)
    cells = patch_cells[..., None]
    place = jnp.where(entry < half, cells // GRID, cells % GRID).astype(F32)
    angles = place * rates
    return jnp.cos(angles), jnp.sin(angles)


def wave_columns(timesteps, first, width):
    half_width = D // 2
    columns = first + jnp.arange(width, dtype=jnp.int32)
    is_cos = columns < half_width
    spot = jnp.where(is_cos, columns, columns - half_width).astype(F32)
    rates = jnp.exp(-math.log(10000.0) * spot / half_width)
    phases = timesteps.astype(F32)[:, None] * rates[None, :]
    return jnp.where(is_cos[None, :], jnp.cos(phases), jnp.sin(phases))


def dot_rows(a, b):
    return lax.dot_general(a, b, (((1,), (0,)), ((), ())), preferred_element_type=F32)


def dot_last(a, b):
    return lax.dot_general(a, b, (((1,), (1,)), ((), ())), preferred_element_type=F32)


def dot_first(a, b):
    return lax.dot_general(a, b, (((0,), (0,)), ((), ())), preferred_element_type=F32)


def head_tables(cols):
    lane = lax.broadcasted_iota(jnp.int32, (cols, cols), 0)
    other = lax.broadcasted_iota(jnp.int32, (cols, cols), 1)
    same = jnp.where(lane // HEAD_DIM == other // HEAD_DIM, 1.0, 0.0).astype(BF16)
    even = other % 2 == 0
    turn = jnp.where(even & (lane == other + 1), -1.0, 0.0)
    turn = jnp.where(jnp.logical_not(even) & (lane == other - 1), 1.0, turn).astype(BF16)
    return same, turn


def unit_heads(values, same):
    mean_sq = dot_rows((values * values).astype(BF16), same) * (1.0 / HEAD_DIM)
    scale = lax.rsqrt(mean_sq + 1e-06)
    return values * scale, scale


def turn_heads(values, cosines, sines, turn):
    return values * cosines + dot_rows(values.astype(BF16), turn) * sines


def head_masks(cols):
    lane = lax.broadcasted_iota(jnp.int32, (1, cols), 1)
    return [
        (lane >= h * HEAD_DIM) & (lane < (h + 1) * HEAD_DIM) for h in range(cols // HEAD_DIM)
    ]


def attn_forward_kernel(
    own_ref, peer_ref, w_ref, b_ref, g_ref, cos_ref, sin_ref, same_ref, turn_ref,
    qkv_ref, heads_ref, own_out, peer_out, x_all, total,
):
    hc = w_ref.shape[2] // 4
    images, patches, width = own_ref.shape
    side = images * patches
    same, turn = same_ref[...], turn_ref[...]
    masks = head_masks(hc)
    at = pl.program_id(0)

    @pl.when(at == 0)
    def _():
        x_all[:side] = own_ref[...].reshape(side, width)
        x_all[side:] = peer_ref[...].reshape(side, width)

    qkv = dot_rows(x_all[...], w_ref[0, :, : 3 * hc]) + b_ref[0]
    qkv_ref[0] = qkv.astype(BF16)
    tables = (cos_ref[...], sin_ref[...])
    q_rot = unit_heads(qkv[:, :hc], same)[0] * (g_ref[0] * INV_ROOT)
    q_rot = turn_heads(q_rot, *tables, turn).astype(BF16)
    k_rot = unit_heads(qkv[:, hc : 2 * hc], same)[0] * g_ref[1]
    k_rot = turn_heads(k_rot, *tables, turn).astype(BF16)
    v_all = qkv[:, 2 * hc :].astype(BF16)
    v_all = jnp.concatenate((v_all, jnp.ones((2 * side, 256 - hc), BF16)), axis=1)
    q_heads = [jnp.where(mine, q_rot, jnp.zeros_like(q_rot)) for mine in masks]
    outs = []
    for image in range(2 * images):
        rows_at = slice(image * patches, (image + 1) * patches)
        k, v = k_rot[rows_at], v_all[rows_at]
        heads = None
        for q, mine in zip(q_heads, masks):
            expo = jnp.exp(dot_last(q[rows_at], k)).astype(BF16)
            part = dot_rows(expo, v)
            part = part[:, :hc] * (1.0 / part[:, hc : hc + 1])
            heads = part if heads is None else jnp.where(mine, part, heads)
        outs.append(heads.astype(BF16))
    heads = jnp.concatenate(outs, axis=0)
    heads_ref[0] = heads
    @pl.when(at == 0)
    def _():
        total[...] = dot_last(heads, w_ref[0, :, 3 * hc :])

    @pl.when(at > 0)
    def _():
        total[...] += dot_last(heads, w_ref[0, :, 3 * hc :])

    @pl.when(at == pl.num_programs(0) - 1)
    def _():
        own_out[...] = total[:side].reshape(images, patches, width).astype(BF16)
        peer_out[...] = total[side:].reshape(images, patches, width).astype(BF16)


def attn_backward_kernel(
    own_ref, peer_ref, w_ref, qkv_in_ref, g_ref, cos_ref, sin_ref, same_ref, turn_ref,
    dqkv_ref, own_out, peer_out, bias_ref, gain_ref, x_all, total,
):
    hc = w_ref.shape[2] // 4
    images, patches, width = own_ref.shape
    side = images * patches
    same, turn = same_ref[...], turn_ref[...]
    masks = head_masks(hc)
    at = pl.program_id(0)

    @pl.when(at == 0)
    def _():
        gain_ref[...] = jnp.zeros_like(gain_ref)
        x_all[:side] = own_ref[...].reshape(side, width)
        x_all[side:] = peer_ref[...].reshape(side, width)

    tables = (cos_ref[...], sin_ref[...])
    d_heads_all = dot_rows(x_all[...], w_ref[0, :, 3 * hc :]).astype(BF16)
    qkv = qkv_in_ref[0]
    v_all = qkv[:, 2 * hc :]
    uq, rq = unit_heads(qkv[:, :hc].astype(F32), same)
    uk, rk = unit_heads(qkv[:, hc : 2 * hc].astype(F32), same)
    q_rot = turn_heads(uq * (g_ref[0] * INV_ROOT), *tables, turn).astype(BF16)
    k_rot = turn_heads(uk * g_ref[1], *tables, turn).astype(BF16)
    zero = jnp.zeros_like(q_rot)
    q_heads = [jnp.where(mine, q_rot, zero) for mine in masks]
    v_heads = [jnp.where(mine, v_all, zero) for mine in masks]
    grads = ([], [], [])
    for image in range(2 * images):
        rows_at = slice(image * patches, (image + 1) * patches)
        q, k, d_heads = q_rot[rows_at], k_rot[rows_at], d_heads_all[rows_at]
        here = [None, None, None]
        for head, mine in enumerate(masks):
            expo = jnp.exp(dot_last(k, q_heads[head][rows_at]))
            probs = expo * (1.0 / jnp.sum(expo, axis=0, keepdims=True))
            d_probs = dot_last(v_heads[head][rows_at], d_heads)
            mean = jnp.sum(d_probs * probs, axis=0, keepdims=True)
            d_scores = (probs * (d_probs - mean)).astype(BF16)
            parts = (
                dot_first(d_scores, k),
                dot_rows(d_scores, q),
                dot_rows(probs.astype(BF16), d_heads),
            )
            here = [
                new if old is None else jnp.where(mine, new, old)
                for new, old in zip(parts, here)
            ]
        for which in range(3):
            grads[which].append(here[which])
    d_q, d_k, d_v = (jnp.concatenate(part, axis=0) for part in grads)
    sides = []
    for which, (grad, unit, scale) in enumerate(((d_q * INV_ROOT, uq, rq), (d_k, uk, rk))):
        back = grad * tables[0] + dot_last((grad * tables[1]).astype(BF16), turn)
        gain_ref[which : which + 1] += jnp.sum(back * unit, axis=0, keepdims=True)
        back = back * g_ref[which]
        mean = dot_rows((back * unit).astype(BF16), same) * (1.0 / HEAD_DIM)
        sides.append((back - unit * mean) * scale)
    d_qkv = jnp.concatenate((sides[0], sides[1], d_v), axis=1)
    bias_ref[0] = jnp.sum(d_qkv, axis=0, keepdims=True)
    d_qkv = d_qkv.astype(BF16)
    dqkv_ref[0] = d_qkv
    @pl.when(at == 0)
    def _():
        total[...] = dot_last(d_qkv, w_ref[0, :, : 3 * hc])

    @pl.when(at > 0)
    def _():
        total[...] += dot_last(d_qkv, w_ref[0, :, : 3 * hc])

    @pl.when(at == pl.num_programs(0) - 1)
    def _():
        own_out[...] = total[:side].reshape(images, patches, width).astype(BF16)
        peer_out[...] = total[side:].reshape(images, patches, width).astype(BF16)


def resident(shape):
    return pl.BlockSpec(shape, lambda i: (0,) * len(shape))


def by_line(shape, first=0):
    return pl.BlockSpec((1,) + shape, lambda i: (i + first,) + (0,) * len(shape))


def attn_cost(x, w, products):
    images, patches, width = x.shape
    line, _, cols = w.shape
    pairs = 2 * images * line * (cols // (4 * HEAD_DIM)) * patches * patches
    return pl.CostEstimate(
        flops=4 * images * patches * width * line * cols + products * 2 * pairs * 256,
        bytes_accessed=w.size * 2 + x.size * 16,
        transcendentals=pairs,
    )


def attn_forward(own, peer, w, b, *tables):
    images, patches, width = own.shape
    line, _, cols = w.shape
    hc = cols // 4
    rows = 2 * images * patches
    return pl.pallas_call(
        attn_forward_kernel,
        grid=(line,),
        in_specs=[resident(own.shape)] * 2
        + [by_line(w.shape[1:]), by_line(b.shape[1:])]
        + [resident(table.shape) for table in tables],
        out_specs=[by_line((rows, 3 * hc)), by_line((rows, hc))]
        + [resident(own.shape)] * 2,
        out_shape=[
            jax.ShapeDtypeStruct((line, rows, 3 * hc), BF16),
            jax.ShapeDtypeStruct((line, rows, hc), BF16),
        ]
        + [jax.ShapeDtypeStruct(own.shape, BF16)] * 2,
        scratch_shapes=[pltpu.VMEM((rows, width), BF16), pltpu.VMEM((rows, width), F32)],
        compiler_params=pltpu.CompilerParams(vmem_limit_bytes=50 << 20),
        cost_estimate=attn_cost(own, w, 2),
    )(own, peer, w, b, *tables)


def attn_backward(own, peer, w, qkv, *tables):
    images, patches, width = own.shape
    line, _, cols = w.shape
    hc = cols // 4
    rows = 2 * images * patches
    return pl.pallas_call(
        attn_backward_kernel,
        grid=(line,),
        in_specs=[resident(own.shape)] * 2
        + [by_line(w.shape[1:]), by_line(qkv.shape[1:])]
        + [resident(table.shape) for table in tables],
        out_specs=[by_line((rows, 3 * hc))]
        + [resident(own.shape)] * 2
        + [by_line((1, 3 * hc)), resident((2, hc))],
        out_shape=[jax.ShapeDtypeStruct((line, rows, 3 * hc), BF16)]
        + [jax.ShapeDtypeStruct(own.shape, BF16)] * 2
        + [jax.ShapeDtypeStruct((line, 1, 3 * hc), F32), jax.ShapeDtypeStruct((2, hc), F32)],
        scratch_shapes=[pltpu.VMEM((rows, width), BF16), pltpu.VMEM((rows, width), F32)],
        compiler_params=pltpu.CompilerParams(vmem_limit_bytes=50 << 20),
        cost_estimate=attn_cost(own, w, 5),
    )(own, peer, w, qkv, *tables)


def ffn_forward_kernel(*refs):
    own_ref, peer_ref, w_ref, b_ref = refs[:4]
    gu_ref, hidden_ref, x_all = refs[-3:]
    ff = hidden_ref.shape[2]
    images, patches, width = own_ref.shape
    side = images * patches

    @pl.when(pl.program_id(0) == 0)
    def _():
        x_all[:side] = own_ref[...].reshape(side, width)
        x_all[side:] = peer_ref[...].reshape(side, width)

    made = dot_rows(x_all[...], w_ref[0]) + b_ref[0]
    gu_ref[0] = made.astype(BF16)
    gate, up = made[:, :ff], made[:, ff:]
    hidden_ref[0] = (gate * up / (1.0 + jnp.exp(-gate))).astype(BF16)


def ffn_forward(first, count, own, peer, w, b, *filled):
    images, patches, width = own.shape
    line, _, cols = w.shape
    rows = 2 * images * patches
    return pl.pallas_call(
        ffn_forward_kernel,
        grid=(count,),
        in_specs=[resident(own.shape)] * 2
        + [by_line(w.shape[1:], first), by_line(b.shape[1:], first)]
        + [pl.BlockSpec(memory_space=pl.ANY)] * len(filled),
        out_specs=[by_line((rows, cols), first), by_line((rows, cols // 2), first)],
        out_shape=[
            jax.ShapeDtypeStruct((line, rows, cols), BF16),
            jax.ShapeDtypeStruct((line, rows, cols // 2), BF16),
        ],
        scratch_shapes=[pltpu.VMEM((rows, width), BF16)],
        input_output_aliases={4: 0, 5: 1} if filled else {},
        compiler_params=pltpu.CompilerParams(vmem_limit_bytes=50 << 20),
        cost_estimate=pl.CostEstimate(
            flops=2 * rows * width * count * cols,
            bytes_accessed=2 * count * cols * (width + 2 * rows),
            transcendentals=count * rows * cols // 2,
        ),
    )(own, peer, w, b, *filled)


def ffn_backward_kernel(
    own_ref, peer_ref, down_ref, w_ref, gu_ref,
    d_gu_ref, own_out, peer_out, bias_ref, x_all, total,
):
    ff = down_ref.shape[2]
    images, patches, width = own_ref.shape
    side = images * patches
    at = pl.program_id(0)

    @pl.when(at == 0)
    def _():
        x_all[:side] = own_ref[...].reshape(side, width)
        x_all[side:] = peer_ref[...].reshape(side, width)

    d_hidden = dot_rows(x_all[...], down_ref[0])
    gate, up = gu_ref[0, :, :ff].astype(F32), gu_ref[0, :, ff:].astype(F32)
    sig = 1.0 / (1.0 + jnp.exp(-gate))
    silu = gate * sig
    d_up = d_hidden * silu
    d_gate = d_hidden * up * (sig + silu * (1.0 - sig))
    bias_ref[0, :, :ff] = jnp.sum(d_gate, axis=0, keepdims=True)
    bias_ref[0, :, ff:] = jnp.sum(d_up, axis=0, keepdims=True)
    d_gu_ref[0, :, :ff] = d_gate.astype(BF16)
    d_gu_ref[0, :, ff:] = d_up.astype(BF16)
    @pl.when(at == 0)
    def _():
        total[...] = dot_last(d_gu_ref[0], w_ref[0])

    @pl.when(at > 0)
    def _():
        total[...] += dot_last(d_gu_ref[0], w_ref[0])

    @pl.when(at == pl.num_programs(0) - 1)
    def _():
        own_out[...] = total[:side].reshape(images, patches, width).astype(BF16)
        peer_out[...] = total[side:].reshape(images, patches, width).astype(BF16)


def ffn_backward(own, peer, w_down, w_gu, gate_up):
    images, patches, width = own.shape
    line, rows, cols = gate_up.shape
    return pl.pallas_call(
        ffn_backward_kernel,
        grid=(line,),
        in_specs=[resident(own.shape)] * 2
        + [by_line(w_down.shape[1:]), by_line(w_gu.shape[1:]), by_line((rows, cols))],
        out_specs=[by_line((rows, cols))] + [resident(own.shape)] * 2 + [by_line((1, cols))],
        out_shape=[jax.ShapeDtypeStruct((line, rows, cols), BF16)]
        + [jax.ShapeDtypeStruct(own.shape, BF16)] * 2
        + [jax.ShapeDtypeStruct((line, 1, cols), F32)],
        scratch_shapes=[pltpu.VMEM((rows, width), BF16), pltpu.VMEM((rows, width), F32)],
        compiler_params=pltpu.CompilerParams(vmem_limit_bytes=50 << 20),
        cost_estimate=pl.CostEstimate(
            flops=3 * rows * width * line * cols,
            bytes_accessed=2 * line * cols * (2 * width + 2 * rows),
            transcendentals=line * rows * cols // 2,
        ),
    )(own, peer, w_down, w_gu, gate_up)


def after(values, *others):
    return lax.optimization_barrier((values, others))[0]


def axis_len(name):
    return lax.axis_size(name)


def swap(values, name, bit=1):
    count = axis_len(name)
    return lax.ppermute(values, name, [(i, i ^ bit) for i in range(count)])


def sum_by_swaps(values, name):
    count = axis_len(name)
    bit = 1
    while bit < count:
        values = values + swap(values, name, bit)
        bit *= 2
    return values


def place_kernel(half, spot_ref, own_ref, x_ref, y_ref, da_ref, db_ref, out_ref):
    at = pl.program_id(0)
    out_ref[0, spot_ref[0]] = own_ref[0]
    out_ref[0, spot_ref[1]] = x_ref[0]
    out_ref[0, spot_ref[2]] = y_ref[0]

    @pl.when(at < half)
    def _():
        out_ref[0, spot_ref[3]] = da_ref[0]

    @pl.when(at >= half)
    def _():
        out_ref[0, spot_ref[3]] = db_ref[0]


def place_parts(own, from_x, from_y, diag_a, diag_b):
    line, rows, cols = own.shape
    half = diag_a.shape[0]
    spots = lax.axis_index(CHIPS) ^ jnp.arange(4, dtype=jnp.int32)
    straight = pl.BlockSpec((1, rows, cols), lambda i: (i, 0, 0))
    early = pl.BlockSpec((1, rows, cols), lambda i: (jnp.minimum(i, half - 1), 0, 0))
    late = pl.BlockSpec((1, rows, cols), lambda i: (jnp.maximum(i - half, 0), 0, 0))
    return pl.pallas_call(
        functools.partial(place_kernel, half),
        grid=(line,),
        in_specs=[pl.BlockSpec(memory_space=pltpu.SMEM)] + [straight] * 3 + [early, late],
        out_specs=pl.BlockSpec((1, 4, rows, cols), lambda i: (i, 0, 0, 0)),
        out_shape=jax.ShapeDtypeStruct((line, 4, rows, cols), own.dtype),
        compiler_params=pltpu.CompilerParams(vmem_limit_bytes=40 << 20),
        cost_estimate=pl.CostEstimate(flops=0, bytes_accessed=16 * own.size, transcendentals=0),
    )(spots, own, from_x, from_y, diag_a, diag_b)


def to_whole(values):
    line = axis_len(LINE)
    images, patches, width = values.shape
    moved = values.reshape(line, images // line, patches, width)
    moved = lax.all_to_all(moved, LINE, 0, 0, tiled=True)
    return moved.transpose(1, 0, 2, 3).reshape(images // line, line * patches, width)


def to_parts(values):
    line = axis_len(LINE)
    images, patches, width = values.shape
    moved = values.reshape(images, line, patches // line, width).transpose(1, 0, 2, 3)
    moved = lax.all_to_all(moved, LINE, 0, 0, tiled=True)
    return moved.reshape(images * line, patches // line, width)


def gather_line(piece):
    return lax.all_gather(piece, LINE, axis=0)


def first_hop(held):
    if axis_len(CHIPS) != 4:
        return (held,)
    return swap(held, CHIPS, 1), swap(held, CHIPS, 2)


def second_hop(arrived):
    if len(arrived) == 1:
        return arrived, arrived
    half = arrived[0].shape[0] // 2
    low, high = arrived[0][:half], arrived[1][half:]
    return (low, high), (swap(low, CHIPS, 2), swap(high, CHIPS, 1))


def whole_weight(held, arrived, last):
    if len(arrived) == 1:
        return lax.all_gather(held, CHIPS, axis=1, tiled=True)[:, None]
    return place_parts(held, *arrived, *last)


def weight_product(lefts, right):
    left = jnp.concatenate(lefts, axis=0)
    return jnp.einsum("rd,zrn->zdn", left, right, preferred_element_type=F32).astype(BF16)


def grad_kernel(counts, spot_ref, *refs):
    lefts, refs = refs[: sum(counts)], refs[sum(counts) :]
    rights, refs = refs[: len(counts)], refs[len(counts) :]
    outs, scratch = refs[:5], refs[5:]
    plain, turned = scratch[0], scratch[1:]
    rows = outs[4].shape[1]
    half = rows // 2

    @pl.when(pl.program_id(0) == 0)
    def _():
        for pair, count in enumerate(counts):
            at = 0
            for left in lefts[sum(counts[:pair]) : sum(counts[:pair]) + count]:
                plain[:, at : at + left.shape[0]] = left[...].T
                at += left.shape[0]
            for place in range(4):
                turned[pair][place * rows : (place + 1) * rows] = plain[
                    pl.ds(pl.multiple_of(spot_ref[place] * rows, rows), rows)
                ]

    first = 0
    for pair, right in enumerate(rights):
        last = first + right.shape[-1]
        made = dot_rows(turned[pair][...], right[0]).astype(BF16)
        top = 0
        for out, count in zip(outs, (half, rows - half, rows, rows, rows)):
            out[0, :, first:last] = made[top : top + count]
            top += count
        first = last


def chip_products(pairs):
    line, total_rows, _ = pairs[0][1].shape
    width = pairs[0][0][0].shape[1]
    cols = sum(right.shape[-1] for _, right in pairs)
    rows = width // 4
    half = rows // 2
    spots = lax.axis_index(CHIPS) ^ jnp.array((3, 2, 1, 0), dtype=jnp.int32)
    lefts = [left for group, _ in pairs for left in group]
    rights = [right for _, right in pairs]
    cut = (half, rows - half, rows, rows, rows)
    return pl.pallas_call(
        functools.partial(grad_kernel, tuple(len(group) for group, _ in pairs)),
        grid=(line,),
        in_specs=[pl.BlockSpec(memory_space=pltpu.SMEM)]
        + [resident(left.shape) for left in lefts]
        + [by_line(right.shape[1:]) for right in rights],
        out_specs=[by_line((count, cols)) for count in cut],
        out_shape=[jax.ShapeDtypeStruct((line, count, cols), BF16) for count in cut],
        scratch_shapes=[pltpu.VMEM((width, total_rows), BF16)] * (1 + len(pairs)),
        compiler_params=pltpu.CompilerParams(vmem_limit_bytes=50 << 20),
        cost_estimate=pl.CostEstimate(
            flops=line * width * total_rows * cols // 4,
            bytes_accessed=2 * line * (width + total_rows) * cols,
            transcendentals=0,
        ),
    )(spots, *lefts, *rights)


def send_diagonal(pairs):
    if axis_len(CHIPS) != 4:
        grad = jnp.concatenate([weight_product(*pair) for pair in pairs], axis=-1)
        return (grad,), None
    parts = chip_products(pairs)
    return parts, (swap(parts[0], CHIPS, 1), swap(parts[1], CHIPS, 2))


def send_blocks(parts, got):
    if got is None:
        return parts, None
    _, _, to_y, to_x, _ = parts
    half = got[0].shape[1]
    to_y = jnp.concatenate((to_y[:, :half] + got[0], to_y[:, half:]), axis=1)
    to_x = jnp.concatenate((to_x[:, :half], to_x[:, half:] + got[1]), axis=1)
    return (to_y, to_x), (swap(to_y, CHIPS, 2), swap(to_x, CHIPS, 1))


def add_blocks(parts, got):
    if got is None:
        return lax.psum_scatter(parts[0], CHIPS, scatter_dimension=1, tiled=True)
    return (parts[4].astype(F32) + got[0].astype(F32) + got[1].astype(F32)).astype(BF16)


def scatter_line(part):
    return lax.psum_scatter(part, LINE, scatter_dimension=0, tiled=False)


def with_peer(values):
    return jnp.concatenate((values, swap(values, CORES)), axis=0)


def fold_peer(values):
    own = values.shape[0] // 2
    sent = swap(values[own:].astype(BF16), CORES)
    return values[:own] + sent.astype(F32)


def on_device(
    tokens,
    timesteps,
    labels,
    patch_cells,
    class_table,
    ada_weight,
    ada_bias,
    qkv_weight,
    qkv_bias,
    q_gain,
    k_gain,
    out_weight,
    out_bias,
    gate_up_weight,
    gate_up_bias,
    down_weight,
    down_bias,
    cotangent,
):
    core = lax.axis_index(CORES)
    line_at = lax.axis_index(LINE)
    line = axis_len(LINE)
    data = axis_len(CHIPS) * axis_len(CORES)
    devices = data * line
    images = tokens.shape[0]
    own_images = images // line
    width = class_table.shape[1]
    chunk = ada_weight.shape[2]
    highest = lax.Precision.HIGHEST

    rows_w = qkv_weight.shape[0]
    head_cols = qkv_weight.shape[2] // 2
    ff_cols = gate_up_weight.shape[2] // 2

    def column_halves(which):
        qkv_half = lax.dynamic_slice_in_dim(qkv_weight, which * head_cols, head_cols, 2)
        out_half = lax.dynamic_slice_in_dim(out_weight, which * head_cols, head_cols, 0)
        gu_half = lax.dynamic_slice_in_dim(gate_up_weight, which * ff_cols, ff_cols, 2)
        down_half = lax.dynamic_slice_in_dim(down_weight, which * ff_cols, ff_cols, 0)
        return jnp.concatenate(
            (
                qkv_half.reshape(rows_w, 3 * head_cols),
                out_half.T,
                gu_half.reshape(rows_w, 2 * ff_cols),
                down_half.T,
            ),
            axis=1,
        )

    kept = column_halves(core)
    got = swap(column_halves(1 - core), CORES)
    both = jnp.concatenate(
        (jnp.where(core == 0, kept, got), jnp.where(core == 0, got, kept)), axis=0
    )
    attn_cols = 4 * head_cols
    held_attn = gather_line(both[:, :attn_cols])
    held_gu = gather_line(both[:, attn_cols : attn_cols + 2 * ff_cols])
    down_piece = both[:, attn_cols + 2 * ff_cols :]
    held_down = gather_line(jnp.pad(down_piece, ((0, 0), (0, PAD))))

    small_in = jnp.stack((labels, timesteps))
    small_in = lax.all_to_all(
        jnp.broadcast_to(small_in, (data,) + small_in.shape), DATA, 0, 0, tiled=True
    )
    labels_all = small_in[:, 0].reshape(data * images)
    steps_all = small_in[:, 1].reshape(data * images)
    one_hot = (labels_all[:, None] == jnp.arange(CLASSES, dtype=jnp.int32)[None, :]).astype(BF16)
    cond = jnp.dot(one_hot, class_table, preferred_element_type=F32)
    cond = cond + wave_columns(steps_all, line_at * width, width)
    cond_low = jax.nn.silu(cond).astype(BF16)
    ada_flat = ada_weight.reshape(width, 6 * chunk)
    mod_part = jnp.dot(cond_low, ada_flat, preferred_element_type=F32)
    bias_in = jnp.concatenate((qkv_bias.reshape(-1), gate_up_bias.reshape(-1))).astype(F32)
    bias_len = bias_in.shape[0]
    share = -(-bias_len // data)
    bias_in = jnp.pad(bias_in, (0, share * data - bias_len)).reshape(data, share)
    data_at = lax.axis_index(CHIPS) * axis_len(CORES) + core
    bias_in = lax.dynamic_index_in_dim(bias_in, data_at, 0, keepdims=True)
    mod_part = mod_part.reshape(devices, own_images * 6 * chunk)
    mod_part = jnp.concatenate((mod_part, jnp.broadcast_to(bias_in, (devices, share))), axis=1)
    mod_part = lax.all_to_all(mod_part, EVERY, 0, 0, tiled=True)
    bias_all = mod_part[:, own_images * 6 * chunk :].reshape(data, line, share)
    bias_all = bias_all.transpose(1, 0, 2).reshape(line, data * share)[:, :bias_len]
    mod_part = mod_part[:, : own_images * 6 * chunk]
    mod = jnp.sum(mod_part.reshape(data, line, own_images, 6, chunk), axis=1)
    mod = mod.transpose(1, 2, 0, 3).reshape(own_images, 6, D) + ada_bias.astype(F32)
    shift_a, scale_a, gate_a, shift_f, scale_f, gate_f = (mod[:, k : k + 1] for k in range(6))

    cells = lax.dynamic_slice_in_dim(patch_cells, line_at * own_images, own_images, 0)
    repeat = head_cols // HEAD_DIM
    cosines, sines = rotary_tables(with_peer(cells), repeat)
    gains = jnp.tile(jnp.stack((q_gain, k_gain)).astype(F32)[:, None], (1, 1, repeat))
    same, turn = head_tables(head_cols)

    x_rows = to_whole(after(tokens, cond_low))
    qkv_b = bias_all[:, : 6 * head_cols].reshape(line, 3, 2, head_cols)
    qkv_b = lax.dynamic_index_in_dim(qkv_b, core, 2, keepdims=False).reshape(line, 1, 3 * head_cols)
    gu_b = bias_all[:, 6 * head_cols :].reshape(line, 2, 2, ff_cols)
    gu_b = lax.dynamic_index_in_dim(gu_b, core, 2, keepdims=False).reshape(line, 1, 2 * ff_cols)
    ready = (cosines, sines, qkv_b, gu_b)
    attn_arrived, ready = lax.optimization_barrier((first_hop(held_attn), ready))
    cosines, sines, qkv_b, gu_b = ready
    _, attn_last = second_hop(attn_arrived)
    x_rows = after(x_rows, attn_last).astype(F32)
    held_gu = after(held_gu, attn_last)
    gu_arrived = first_hop(held_gu)

    attn_own = modulate(x_rows, shift_a, scale_a).astype(BF16)
    attn_peer = swap(attn_own, CORES)
    w_attn = whole_weight(held_attn, attn_arrived, attn_last)
    w_attn = w_attn.reshape(line, D, attn_cols)
    patches = x_rows.shape[1]
    rows_all = 2 * own_images * patches
    tables = (gains, cosines.reshape(rows_all, -1), sines.reshape(rows_all, -1), same, turn)
    qkv, heads_out, part_own, part_peer = attn_forward(
        after(attn_own, held_gu), attn_peer, w_attn, qkv_b, *tables
    )
    part_peer = swap(part_peer, CORES)
    gu_passed, gu_last = second_hop(gu_arrived)
    part_own = after(part_own, gu_passed, held_down)
    held_down = after(held_down[:, :, :ff_cols], gu_last)
    down_arrived = first_hop(held_down)
    attn = part_own.astype(F32) + part_peer.astype(F32) + out_bias.astype(F32)

    def as_rows(*values):
        return [value.reshape(own_images * patches, D) for value in values]

    mid = x_rows + gate_a * attn
    ffn_own = modulate(mid, shift_f, scale_f).astype(BF16)
    ffn_peer = swap(ffn_own, CORES)
    grad_out = to_whole(after(cotangent, heads_out)).astype(F32)
    d_ffn_f = gate_f * grad_out
    d_ffn_own = d_ffn_f.astype(BF16)
    d_ffn_peer = swap(d_ffn_own, CORES)
    w_gu = whole_weight(held_gu, gu_arrived, gu_last).reshape(line, D, 2 * ff_cols)
    early = line // 2
    begun = ffn_forward(0, early, ffn_own, ffn_peer, w_gu, gu_b)
    down_passed, down_last = second_hop(after(down_arrived, begun))
    gate_up, hidden = ffn_forward(
        early, line - early, after(ffn_own, down_passed), ffn_peer, w_gu, gu_b, *begun
    )
    w_down = whole_weight(held_down, down_arrived, down_last).reshape(line, D, ff_cols)
    d_gu, d_in_own, d_in_peer, gu_bias_part = ffn_backward(
        d_ffn_own, d_ffn_peer, w_down, w_gu, gate_up
    )
    d_in_peer = swap(d_in_peer, CORES)
    gu_parts, gu_got = send_diagonal(
        [(as_rows(ffn_own, ffn_peer), d_gu)]
    )
    down_parts, down_got = send_diagonal(
        [(as_rows(d_ffn_own, d_ffn_peer), after(hidden, gu_parts))]
    )
    ffn = jnp.einsum("zrf,zdf->rd", after(hidden, down_parts), w_down, preferred_element_type=F32)
    ffn = fold_peer(ffn.reshape(2 * own_images, patches, D)) + down_bias.astype(F32)
    output = to_parts((mid + gate_f * ffn).astype(BF16))

    down_bias_part = jnp.sum(d_ffn_f, axis=(0, 1))
    d_gate_f = jnp.sum(grad_out * ffn, axis=1, keepdims=True)
    d_ffn_in = after(d_in_own.astype(F32) + d_in_peer.astype(F32), gu_got)
    mid_grad, d_shift_f, d_scale_f = jax.vjp(modulate, mid, shift_f, scale_f)[1](d_ffn_in)
    d_mid = grad_out + mid_grad
    d_attn_f = gate_a * d_mid
    out_bias_part = jnp.sum(d_attn_f, axis=(0, 1))
    d_gate_a = jnp.sum(d_mid * attn, axis=1, keepdims=True)
    d_attn_own = d_attn_f.astype(BF16)
    d_attn_peer = swap(d_attn_own, CORES)
    gu_sent, gu_blocks = send_blocks(gu_parts, gu_got)
    down_sent, down_blocks = send_blocks(down_parts, after(down_got, gu_sent))
    d_qkv, d_in_own, d_in_peer, qkv_bias_part, gain_part = attn_backward(
        after(d_attn_own, gu_sent, down_sent), d_attn_peer, w_attn, qkv, *tables
    )
    d_in_peer = swap(d_in_peer, CORES)
    g_gu = add_blocks(gu_parts if gu_blocks is not None else gu_sent, after(gu_blocks, d_qkv))
    attn_parts, attn_got = send_diagonal(
        [
            (as_rows(attn_own, attn_peer), after(d_qkv, output, g_gu)),
            (as_rows(d_attn_own, d_attn_peer), heads_out),
        ]
    )
    g_gu = scatter_line(g_gu)
    qkv_bias_part, gain_part = after((qkv_bias_part, gain_part), attn_parts)
    gain_part = gain_part.reshape(2, repeat, HEAD_DIM).sum(axis=1)
    d_attn_in = d_in_own.astype(F32) + d_in_peer.astype(F32)
    row_grad, d_shift_a, d_scale_a = jax.vjp(modulate, x_rows, shift_a, scale_a)[1](d_attn_in)
    tokens_sent = (d_mid + row_grad).astype(BF16)

    g_down = add_blocks(down_parts if down_blocks is not None else down_sent, after(down_blocks, tokens_sent))
    attn_got = after(attn_got, g_down)
    g_down = scatter_line(g_down)
    attn_got = after(attn_got, g_gu, tokens_sent)
    tokens_grad = to_parts(tokens_sent)
    attn_sent, attn_blocks = send_blocks(attn_parts, attn_got)
    d_mod = jnp.concatenate(
        (d_shift_a, d_scale_a, d_gate_a, d_shift_f, d_scale_f, d_gate_f), axis=1
    )
    d_mod, tokens_grad = lax.optimization_barrier((after(d_mod, attn_sent), tokens_grad))
    ada_bias_part = jnp.sum(d_mod, axis=0)
    d_mod_low = d_mod.astype(BF16).reshape(own_images, 6, data, chunk).transpose(2, 0, 1, 3)
    d_mod_low = jnp.broadcast_to(
        d_mod_low[:, None], (data, line, own_images, 6, chunk)
    ).reshape(devices, own_images * 6 * chunk)
    d_mod_all = lax.all_to_all(d_mod_low, EVERY, 0, 0, tiled=True)
    d_mod_all = d_mod_all.reshape(data * images, 6 * chunk)
    g_ada = jnp.einsum("bc,be->ce", cond_low, d_mod_all, preferred_element_type=F32)
    g_ada = g_ada.reshape(width, 6, chunk)
    d_silu = jnp.einsum("be,ce->bc", d_mod_all, ada_flat, preferred_element_type=F32)
    d_cond = jax.vjp(jax.nn.silu, cond)[1](d_silu)[0]

    def by_core(part, groups, cols):
        spread = jnp.zeros((line, groups, 2, cols), F32)
        return lax.dynamic_update_slice(
            spread, part.reshape(line, groups, 1, cols), (0, 0, core, 0)
        )

    parts = (
        by_core(qkv_bias_part, 3, head_cols),
        by_core(gu_bias_part, 2, ff_cols),
        ada_bias_part,
        out_bias_part,
        down_bias_part,
        gain_part[0],
        gain_part[1],
    )
    flat = jnp.concatenate([part.reshape(-1) for part in parts])
    count = flat.shape[0]
    flat = jnp.concatenate((flat, d_cond.reshape(-1)))
    flat = sum_by_swaps(sum_by_swaps(flat, CORES), CHIPS)
    g_attn = add_blocks(attn_parts, attn_blocks)
    g_attn = after(g_attn, g_gu, g_down)
    g_attn = scatter_line(g_attn)
    d_cond = flat[count:].reshape(d_cond.shape)
    flat = sum_by_swaps(flat[:count], LINE)
    sums = []
    at = 0
    for part in parts:
        sums.append(flat[at : at + part.size].reshape(part.shape))
        at += part.size
    qkv_bias_grad = lax.dynamic_index_in_dim(sums[0], line_at, 0, keepdims=False)
    gu_bias_grad = lax.dynamic_index_in_dim(sums[1], line_at, 0, keepdims=False)
    tokens_grad = tokens_grad.astype(F32)
    table_grad = jnp.dot(one_hot.astype(F32).T, d_cond, precision=highest)

    def own_rows(part):
        kept = lax.dynamic_slice_in_dim(part, core * rows_w, rows_w, 0)
        got = swap(lax.dynamic_slice_in_dim(part, (1 - core) * rows_w, rows_w, 0), CORES)
        low_half = jnp.where(core == 0, kept, got).astype(F32)
        high_half = jnp.where(core == 0, got, kept).astype(F32)

        def joined(first, groups, cols):
            halves = [
                half[:, first : first + groups * cols].reshape(rows_w, groups, cols)
                for half in (low_half, high_half)
            ]
            return jnp.concatenate(halves, axis=2)

        return joined

    joined = own_rows(g_gu)
    g_gu = joined(0, 2, ff_cols)
    joined = own_rows(g_down)
    g_down = joined(0, 1, ff_cols)[:, 0].T
    joined = own_rows(g_attn)
    g_qkv = joined(0, 3, head_cols)
    g_out = joined(3 * head_cols, 1, head_cols)[:, 0].T
    return (
        output,
        tokens_grad,
        table_grad,
        g_ada,
        sums[2],
        g_qkv,
        qkv_bias_grad.reshape(qkv_bias.shape),
        sums[5],
        sums[6],
        g_out,
        sums[3],
        g_gu,
        gu_bias_grad.reshape(gate_up_bias.shape),
        g_down,
        sums[4],
    )


def solution(mesh):
    chips = mesh.shape["dp"] // 2
    finer = Mesh(mesh.devices.reshape(chips, 2, mesh.shape["tensor"]), EVERY)
    in_specs = (
        P(DATA, LINE, None),
        P(DATA),
        P(DATA),
        P(DATA, None),
        P(None, LINE),
        P(LINE, None, DATA),
        P(),
        P(DATA, None, LINE),
        P(None, LINE),
        P(),
        P(),
        P(LINE, DATA),
        P(),
        P(DATA, None, LINE),
        P(None, LINE),
        P(LINE, DATA),
        P(),
        P(DATA, LINE, None),
    )
    out_specs = (
        P(DATA, LINE, None),
        P(DATA, LINE, None),
        P(None, LINE),
        P(LINE, None, DATA),
        P(),
        P(DATA, None, LINE),
        P(None, LINE),
        P(),
        P(),
        P(LINE, DATA),
        P(),
        P(DATA, None, LINE),
        P(None, LINE),
        P(LINE, DATA),
        P(),
    )
    return jax.shard_map(
        on_device, mesh=finer, in_specs=in_specs, out_specs=out_specs, check_vma=False
    )
```

```python
import functools
import math

import jax
import jax.numpy as jnp
from jax import lax
from jax.experimental import pallas as pl
from jax.experimental.pallas import tpu as pltpu
from jax.sharding import Mesh
from jax.sharding import PartitionSpec as P

D = 1152
HEAD_DIM = 72
CLASSES = 1000
GRID = 16
F32 = jnp.float32
BF16 = jnp.bfloat16
INV_ROOT = 1.0 / math.sqrt(HEAD_DIM)
CHIPS = "p"
CORES = "c"
LINE = "t"
PAD = 128
EVERY = (CHIPS, CORES, LINE)
DATA = (CHIPS, CORES)


def rms_rows(values):
    return values * lax.rsqrt(jnp.mean(values * values, axis=-1, keepdims=True) + 1e-06)


def modulate(values, shift_rows, scale_rows):
    return rms_rows(values) * (1.0 + scale_rows) + shift_rows


def rotary_tables(patch_cells, repeat):
    entry = jnp.arange(repeat * HEAD_DIM, dtype=jnp.int32) % HEAD_DIM
    half = HEAD_DIM // 2
    step = (entry % half // 2).astype(F32)
    rates = 10000.0 ** (-4.0 * step / HEAD_DIM)
    cells = patch_cells[..., None]
    place = jnp.where(entry < half, cells // GRID, cells % GRID).astype(F32)
    angles = place * rates
    return jnp.cos(angles), jnp.sin(angles)


def wave_columns(timesteps, first, width):
    half_width = D // 2
    columns = first + jnp.arange(width, dtype=jnp.int32)
    is_cos = columns < half_width
    spot = jnp.where(is_cos, columns, columns - half_width).astype(F32)
    rates = jnp.exp(-math.log(10000.0) * spot / half_width)
    phases = timesteps.astype(F32)[:, None] * rates[None, :]
    return jnp.where(is_cos[None, :], jnp.cos(phases), jnp.sin(phases))


def dot_rows(a, b):
    return lax.dot_general(a, b, (((1,), (0,)), ((), ())), preferred_element_type=F32)


def dot_last(a, b):
    return lax.dot_general(a, b, (((1,), (1,)), ((), ())), preferred_element_type=F32)


def dot_first(a, b):
    return lax.dot_general(a, b, (((0,), (0,)), ((), ())), preferred_element_type=F32)


def head_tables(cols):
    lane = lax.broadcasted_iota(jnp.int32, (cols, cols), 0)
    other = lax.broadcasted_iota(jnp.int32, (cols, cols), 1)
    same = jnp.where(lane // HEAD_DIM == other // HEAD_DIM, 1.0, 0.0).astype(BF16)
    even = other % 2 == 0
    turn = jnp.where(even & (lane == other + 1), -1.0, 0.0)
    turn = jnp.where(jnp.logical_not(even) & (lane == other - 1), 1.0, turn).astype(BF16)
    return same, turn


def unit_heads(values, same):
    mean_sq = dot_rows((values * values).astype(BF16), same) * (1.0 / HEAD_DIM)
    scale = lax.rsqrt(mean_sq + 1e-06)
    return values * scale, scale


def turn_heads(values, cosines, sines, turn):
    return values * cosines + dot_rows(values.astype(BF16), turn) * sines


def head_masks(cols):
    lane = lax.broadcasted_iota(jnp.int32, (1, cols), 1)
    return [
        (lane >= h * HEAD_DIM) & (lane < (h + 1) * HEAD_DIM) for h in range(cols // HEAD_DIM)
    ]


def attn_forward_kernel(
    own_ref, peer_ref, w_ref, b_ref, g_ref, cos_ref, sin_ref, same_ref, turn_ref,
    qkv_ref, heads_ref, own_out, peer_out, x_all, total,
):
    hc = w_ref.shape[2] // 4
    images, patches, width = own_ref.shape
    side = images * patches
    same, turn = same_ref[...], turn_ref[...]
    masks = head_masks(hc)
    at = pl.program_id(0)

    @pl.when(at == 0)
    def _():
        x_all[:side] = own_ref[...].reshape(side, width)
        x_all[side:] = peer_ref[...].reshape(side, width)

    qkv = dot_rows(x_all[...], w_ref[0, :, : 3 * hc]) + b_ref[0]
    qkv_ref[0] = qkv.astype(BF16)
    tables = (cos_ref[...], sin_ref[...])
    q_rot = unit_heads(qkv[:, :hc], same)[0] * (g_ref[0] * INV_ROOT)
    q_rot = turn_heads(q_rot, *tables, turn).astype(BF16)
    k_rot = unit_heads(qkv[:, hc : 2 * hc], same)[0] * g_ref[1]
    k_rot = turn_heads(k_rot, *tables, turn).astype(BF16)
    v_all = qkv[:, 2 * hc :].astype(BF16)
    v_all = jnp.concatenate((v_all, jnp.ones((2 * side, 256 - hc), BF16)), axis=1)
    q_heads = [jnp.where(mine, q_rot, jnp.zeros_like(q_rot)) for mine in masks]
    outs = []
    for image in range(2 * images):
        rows_at = slice(image * patches, (image + 1) * patches)
        k, v = k_rot[rows_at], v_all[rows_at]
        heads = None
        for q, mine in zip(q_heads, masks):
            expo = jnp.exp(dot_last(q[rows_at], k)).astype(BF16)
            part = dot_rows(expo, v)
            part = part[:, :hc] * (1.0 / part[:, hc : hc + 1])
            heads = part if heads is None else jnp.where(mine, part, heads)
        outs.append(heads.astype(BF16))
    heads = jnp.concatenate(outs, axis=0)
    heads_ref[0] = heads
    @pl.when(at == 0)
    def _():
        total[...] = dot_last(heads, w_ref[0, :, 3 * hc :])

    @pl.when(at > 0)
    def _():
        total[...] += dot_last(heads, w_ref[0, :, 3 * hc :])

    @pl.when(at == pl.num_programs(0) - 1)
    def _():
        own_out[...] = total[:side].reshape(images, patches, width).astype(BF16)
        peer_out[...] = total[side:].reshape(images, patches, width).astype(BF16)


def attn_backward_kernel(
    own_ref, peer_ref, w_ref, qkv_in_ref, g_ref, cos_ref, sin_ref, same_ref, turn_ref,
    dqkv_ref, own_out, peer_out, bias_ref, gain_ref, x_all, total,
):
    hc = w_ref.shape[2] // 4
    images, patches, width = own_ref.shape
    side = images * patches
    same, turn = same_ref[...], turn_ref[...]
    masks = head_masks(hc)
    at = pl.program_id(0)

    @pl.when(at == 0)
    def _():
        gain_ref[...] = jnp.zeros_like(gain_ref)
        x_all[:side] = own_ref[...].reshape(side, width)
        x_all[side:] = peer_ref[...].reshape(side, width)

    tables = (cos_ref[...], sin_ref[...])
    d_heads_all = dot_rows(x_all[...], w_ref[0, :, 3 * hc :]).astype(BF16)
    qkv = qkv_in_ref[0]
    v_all = qkv[:, 2 * hc :]
    uq, rq = unit_heads(qkv[:, :hc].astype(F32), same)
    uk, rk = unit_heads(qkv[:, hc : 2 * hc].astype(F32), same)
    q_rot = turn_heads(uq * (g_ref[0] * INV_ROOT), *tables, turn).astype(BF16)
    k_rot = turn_heads(uk * g_ref[1], *tables, turn).astype(BF16)
    zero = jnp.zeros_like(q_rot)
    q_heads = [jnp.where(mine, q_rot, zero) for mine in masks]
    v_heads = [jnp.where(mine, v_all, zero) for mine in masks]
    grads = ([], [], [])
    for image in range(2 * images):
        rows_at = slice(image * patches, (image + 1) * patches)
        q, k, d_heads = q_rot[rows_at], k_rot[rows_at], d_heads_all[rows_at]
        here = [None, None, None]
        for head, mine in enumerate(masks):
            expo = jnp.exp(dot_last(k, q_heads[head][rows_at]))
            probs = expo * (1.0 / jnp.sum(expo, axis=0, keepdims=True))
            d_probs = dot_last(v_heads[head][rows_at], d_heads)
            mean = jnp.sum(d_probs * probs, axis=0, keepdims=True)
            d_scores = (probs * (d_probs - mean)).astype(BF16)
            parts = (
                dot_first(d_scores, k),
                dot_rows(d_scores, q),
                dot_rows(probs.astype(BF16), d_heads),
            )
            here = [
                new if old is None else jnp.where(mine, new, old)
                for new, old in zip(parts, here)
            ]
        for which in range(3):
            grads[which].append(here[which])
    d_q, d_k, d_v = (jnp.concatenate(part, axis=0) for part in grads)
    sides = []
    for which, (grad, unit, scale) in enumerate(((d_q * INV_ROOT, uq, rq), (d_k, uk, rk))):
        back = grad * tables[0] + dot_last((grad * tables[1]).astype(BF16), turn)
        gain_ref[which : which + 1] += jnp.sum(back * unit, axis=0, keepdims=True)
        back = back * g_ref[which]
        mean = dot_rows((back * unit).astype(BF16), same) * (1.0 / HEAD_DIM)
        sides.append((back - unit * mean) * scale)
    d_qkv = jnp.concatenate((sides[0], sides[1], d_v), axis=1)
    bias_ref[0] = jnp.sum(d_qkv, axis=0, keepdims=True)
    d_qkv = d_qkv.astype(BF16)
    dqkv_ref[0] = d_qkv
    @pl.when(at == 0)
    def _():
        total[...] = dot_last(d_qkv, w_ref[0, :, : 3 * hc])

    @pl.when(at > 0)
    def _():
        total[...] += dot_last(d_qkv, w_ref[0, :, : 3 * hc])

    @pl.when(at == pl.num_programs(0) - 1)
    def _():
        own_out[...] = total[:side].reshape(images, patches, width).astype(BF16)
        peer_out[...] = total[side:].reshape(images, patches, width).astype(BF16)


def resident(shape):
    return pl.BlockSpec(shape, lambda i: (0,) * len(shape))


def by_line(shape, first=0):
    return pl.BlockSpec((1,) + shape, lambda i: (i + first,) + (0,) * len(shape))


def attn_cost(x, w, products):
    images, patches, width = x.shape
    line, _, cols = w.shape
    pairs = 2 * images * line * (cols // (4 * HEAD_DIM)) * patches * patches
    return pl.CostEstimate(
        flops=4 * images * patches * width * line * cols + products * 2 * pairs * 256,
        bytes_accessed=w.size * 2 + x.size * 16,
        transcendentals=pairs,
    )


def attn_forward(own, peer, w, b, *tables):
    images, patches, width = own.shape
    line, _, cols = w.shape
    hc = cols // 4
    rows = 2 * images * patches
    return pl.pallas_call(
        attn_forward_kernel,
        grid=(line,),
        in_specs=[resident(own.shape)] * 2
        + [by_line(w.shape[1:]), by_line(b.shape[1:])]
        + [resident(table.shape) for table in tables],
        out_specs=[by_line((rows, 3 * hc)), by_line((rows, hc))]
        + [resident(own.shape)] * 2,
        out_shape=[
            jax.ShapeDtypeStruct((line, rows, 3 * hc), BF16),
            jax.ShapeDtypeStruct((line, rows, hc), BF16),
        ]
        + [jax.ShapeDtypeStruct(own.shape, BF16)] * 2,
        scratch_shapes=[pltpu.VMEM((rows, width), BF16), pltpu.VMEM((rows, width), F32)],
        compiler_params=pltpu.CompilerParams(vmem_limit_bytes=50 << 20),
        cost_estimate=attn_cost(own, w, 2),
    )(own, peer, w, b, *tables)


def attn_backward(own, peer, w, qkv, *tables):
    images, patches, width = own.shape
    line, _, cols = w.shape
    hc = cols // 4
    rows = 2 * images * patches
    return pl.pallas_call(
        attn_backward_kernel,
        grid=(line,),
        in_specs=[resident(own.shape)] * 2
        + [by_line(w.shape[1:]), by_line(qkv.shape[1:])]
        + [resident(table.shape) for table in tables],
        out_specs=[by_line((rows, 3 * hc))]
        + [resident(own.shape)] * 2
        + [by_line((1, 3 * hc)), resident((2, hc))],
        out_shape=[jax.ShapeDtypeStruct((line, rows, 3 * hc), BF16)]
        + [jax.ShapeDtypeStruct(own.shape, BF16)] * 2
        + [jax.ShapeDtypeStruct((line, 1, 3 * hc), F32), jax.ShapeDtypeStruct((2, hc), F32)],
        scratch_shapes=[pltpu.VMEM((rows, width), BF16), pltpu.VMEM((rows, width), F32)],
        compiler_params=pltpu.CompilerParams(vmem_limit_bytes=50 << 20),
        cost_estimate=attn_cost(own, w, 5),
    )(own, peer, w, qkv, *tables)


def ffn_forward_kernel(*refs):
    own_ref, peer_ref, w_ref, b_ref = refs[:4]
    gu_ref, hidden_ref, x_all = refs[-3:]
    ff = hidden_ref.shape[2]
    images, patches, width = own_ref.shape
    side = images * patches

    @pl.when(pl.program_id(0) == 0)
    def _():
        x_all[:side] = own_ref[...].reshape(side, width)
        x_all[side:] = peer_ref[...].reshape(side, width)

    made = dot_rows(x_all[...], w_ref[0]) + b_ref[0]
    gu_ref[0] = made.astype(BF16)
    gate, up = made[:, :ff], made[:, ff:]
    hidden_ref[0] = (gate * up / (1.0 + jnp.exp(-gate))).astype(BF16)


def ffn_forward(first, count, own, peer, w, b, *filled):
    images, patches, width = own.shape
    line, _, cols = w.shape
    rows = 2 * images * patches
    return pl.pallas_call(
        ffn_forward_kernel,
        grid=(count,),
        in_specs=[resident(own.shape)] * 2
        + [by_line(w.shape[1:], first), by_line(b.shape[1:], first)]
        + [pl.BlockSpec(memory_space=pl.ANY)] * len(filled),
        out_specs=[by_line((rows, cols), first), by_line((rows, cols // 2), first)],
        out_shape=[
            jax.ShapeDtypeStruct((line, rows, cols), BF16),
            jax.ShapeDtypeStruct((line, rows, cols // 2), BF16),
        ],
        scratch_shapes=[pltpu.VMEM((rows, width), BF16)],
        input_output_aliases={4: 0, 5: 1} if filled else {},
        compiler_params=pltpu.CompilerParams(vmem_limit_bytes=50 << 20),
        cost_estimate=pl.CostEstimate(
            flops=2 * rows * width * count * cols,
            bytes_accessed=2 * count * cols * (width + 2 * rows),
            transcendentals=count * rows * cols // 2,
        ),
    )(own, peer, w, b, *filled)


def ffn_backward_kernel(
    own_ref, peer_ref, down_ref, w_ref, gu_ref,
    d_gu_ref, own_out, peer_out, bias_ref, x_all, total,
):
    ff = down_ref.shape[2]
    images, patches, width = own_ref.shape
    side = images * patches
    at = pl.program_id(0)

    @pl.when(at == 0)
    def _():
        x_all[:side] = own_ref[...].reshape(side, width)
        x_all[side:] = peer_ref[...].reshape(side, width)

    d_hidden = dot_rows(x_all[...], down_ref[0])
    gate, up = gu_ref[0, :, :ff].astype(F32), gu_ref[0, :, ff:].astype(F32)
    sig = 1.0 / (1.0 + jnp.exp(-gate))
    silu = gate * sig
    d_up = d_hidden * silu
    d_gate = d_hidden * up * (sig + silu * (1.0 - sig))
    bias_ref[0, :, :ff] = jnp.sum(d_gate, axis=0, keepdims=True)
    bias_ref[0, :, ff:] = jnp.sum(d_up, axis=0, keepdims=True)
    d_gu_ref[0, :, :ff] = d_gate.astype(BF16)
    d_gu_ref[0, :, ff:] = d_up.astype(BF16)
    @pl.when(at == 0)
    def _():
        total[...] = dot_last(d_gu_ref[0], w_ref[0])

    @pl.when(at > 0)
    def _():
        total[...] += dot_last(d_gu_ref[0], w_ref[0])

    @pl.when(at == pl.num_programs(0) - 1)
    def _():
        own_out[...] = total[:side].reshape(images, patches, width).astype(BF16)
        peer_out[...] = total[side:].reshape(images, patches, width).astype(BF16)


def ffn_backward(own, peer, w_down, w_gu, gate_up):
    images, patches, width = own.shape
    line, rows, cols = gate_up.shape
    return pl.pallas_call(
        ffn_backward_kernel,
        grid=(line,),
        in_specs=[resident(own.shape)] * 2
        + [by_line(w_down.shape[1:]), by_line(w_gu.shape[1:]), by_line((rows, cols))],
        out_specs=[by_line((rows, cols))] + [resident(own.shape)] * 2 + [by_line((1, cols))],
        out_shape=[jax.ShapeDtypeStruct((line, rows, cols), BF16)]
        + [jax.ShapeDtypeStruct(own.shape, BF16)] * 2
        + [jax.ShapeDtypeStruct((line, 1, cols), F32)],
        scratch_shapes=[pltpu.VMEM((rows, width), BF16), pltpu.VMEM((rows, width), F32)],
        compiler_params=pltpu.CompilerParams(vmem_limit_bytes=50 << 20),
        cost_estimate=pl.CostEstimate(
            flops=3 * rows * width * line * cols,
            bytes_accessed=2 * line * cols * (2 * width + 2 * rows),
            transcendentals=line * rows * cols // 2,
        ),
    )(own, peer, w_down, w_gu, gate_up)


def after(values, *others):
    return lax.optimization_barrier((values, others))[0]


def axis_len(name):
    return lax.axis_size(name)


def swap(values, name, bit=1):
    count = axis_len(name)
    return lax.ppermute(values, name, [(i, i ^ bit) for i in range(count)])


def sum_by_swaps(values, name):
    count = axis_len(name)
    bit = 1
    while bit < count:
        values = values + swap(values, name, bit)
        bit *= 2
    return values


def place_kernel(half, spot_ref, own_ref, x_ref, y_ref, da_ref, db_ref, out_ref):
    at = pl.program_id(0)
    out_ref[0, spot_ref[0]] = own_ref[0]
    out_ref[0, spot_ref[1]] = x_ref[0]
    out_ref[0, spot_ref[2]] = y_ref[0]

    @pl.when(at < half)
    def _():
        out_ref[0, spot_ref[3]] = da_ref[0]

    @pl.when(at >= half)
    def _():
        out_ref[0, spot_ref[3]] = db_ref[0]


def place_parts(own, from_x, from_y, diag_a, diag_b):
    line, rows, cols = own.shape
    half = diag_a.shape[0]
    spots = lax.axis_index(CHIPS) ^ jnp.arange(4, dtype=jnp.int32)
    straight = pl.BlockSpec((1, rows, cols), lambda i: (i, 0, 0))
    early = pl.BlockSpec((1, rows, cols), lambda i: (jnp.minimum(i, half - 1), 0, 0))
    late = pl.BlockSpec((1, rows, cols), lambda i: (jnp.maximum(i - half, 0), 0, 0))
    return pl.pallas_call(
        functools.partial(place_kernel, half),
        grid=(line,),
        in_specs=[pl.BlockSpec(memory_space=pltpu.SMEM)] + [straight] * 3 + [early, late],
        out_specs=pl.BlockSpec((1, 4, rows, cols), lambda i: (i, 0, 0, 0)),
        out_shape=jax.ShapeDtypeStruct((line, 4, rows, cols), own.dtype),
        compiler_params=pltpu.CompilerParams(vmem_limit_bytes=40 << 20),
        cost_estimate=pl.CostEstimate(flops=0, bytes_accessed=16 * own.size, transcendentals=0),
    )(spots, own, from_x, from_y, diag_a, diag_b)


def to_whole(values):
    line = axis_len(LINE)
    images, patches, width = values.shape
    moved = values.reshape(line, images // line, patches, width)
    moved = lax.all_to_all(moved, LINE, 0, 0, tiled=True)
    return moved.transpose(1, 0, 2, 3).reshape(images // line, line * patches, width)


def to_parts(values):
    line = axis_len(LINE)
    images, patches, width = values.shape
    moved = values.reshape(images, line, patches // line, width).transpose(1, 0, 2, 3)
    moved = lax.all_to_all(moved, LINE, 0, 0, tiled=True)
    return moved.reshape(images * line, patches // line, width)


def gather_line(piece):
    return lax.all_gather(piece, LINE, axis=0)


def first_hop(held):
    if axis_len(CHIPS) != 4:
        return (held,)
    return swap(held, CHIPS, 1), swap(held, CHIPS, 2)


def second_hop(arrived):
    if len(arrived) == 1:
        return arrived, arrived
    half = arrived[0].shape[0] // 2
    low, high = arrived[0][:half], arrived[1][half:]
    return (low, high), (swap(low, CHIPS, 2), swap(high, CHIPS, 1))


def whole_weight(held, arrived, last):
    if len(arrived) == 1:
        return lax.all_gather(held, CHIPS, axis=1, tiled=True)[:, None]
    return place_parts(held, *arrived, *last)


def weight_product(lefts, right):
    left = jnp.concatenate(lefts, axis=0)
    return jnp.einsum("rd,zrn->zdn", left, right, preferred_element_type=F32).astype(BF16)


def grad_kernel(counts, spot_ref, *refs):
    lefts, refs = refs[: sum(counts)], refs[sum(counts) :]
    rights, refs = refs[: len(counts)], refs[len(counts) :]
    outs, scratch = refs[:5], refs[5:]
    plain, turned = scratch[0], scratch[1:]
    rows = outs[4].shape[1]
    half = rows // 2

    @pl.when(pl.program_id(0) == 0)
    def _():
        for pair, count in enumerate(counts):
            at = 0
            for left in lefts[sum(counts[:pair]) : sum(counts[:pair]) + count]:
                plain[:, at : at + left.shape[0]] = left[...].T
                at += left.shape[0]
            for place in range(4):
                turned[pair][place * rows : (place + 1) * rows] = plain[
                    pl.ds(pl.multiple_of(spot_ref[place] * rows, rows), rows)
                ]

    first = 0
    for pair, right in enumerate(rights):
        last = first + right.shape[-1]
        made = dot_rows(turned[pair][...], right[0]).astype(BF16)
        top = 0
        for out, count in zip(outs, (half, rows - half, rows, rows, rows)):
            out[0, :, first:last] = made[top : top + count]
            top += count
        first = last


def chip_products(pairs):
    line, total_rows, _ = pairs[0][1].shape
    width = pairs[0][0][0].shape[1]
    cols = sum(right.shape[-1] for _, right in pairs)
    rows = width // 4
    half = rows // 2
    spots = lax.axis_index(CHIPS) ^ jnp.array((3, 2, 1, 0), dtype=jnp.int32)
    lefts = [left for group, _ in pairs for left in group]
    rights = [right for _, right in pairs]
    cut = (half, rows - half, rows, rows, rows)
    return pl.pallas_call(
        functools.partial(grad_kernel, tuple(len(group) for group, _ in pairs)),
        grid=(line,),
        in_specs=[pl.BlockSpec(memory_space=pltpu.SMEM)]
        + [resident(left.shape) for left in lefts]
        + [by_line(right.shape[1:]) for right in rights],
        out_specs=[by_line((count, cols)) for count in cut],
        out_shape=[jax.ShapeDtypeStruct((line, count, cols), BF16) for count in cut],
        scratch_shapes=[pltpu.VMEM((width, total_rows), BF16)] * (1 + len(pairs)),
        compiler_params=pltpu.CompilerParams(vmem_limit_bytes=50 << 20),
        cost_estimate=pl.CostEstimate(
            flops=line * width * total_rows * cols // 4,
            bytes_accessed=2 * line * (width + total_rows) * cols,
            transcendentals=0,
        ),
    )(spots, *lefts, *rights)


def send_diagonal(pairs):
    if axis_len(CHIPS) != 4:
        grad = jnp.concatenate([weight_product(*pair) for pair in pairs], axis=-1)
        return (grad,), None
    parts = chip_products(pairs)
    return parts, (swap(parts[0], CHIPS, 1), swap(parts[1], CHIPS, 2))


def send_blocks(parts, got):
    if got is None:
        return parts, None
    _, _, to_y, to_x, _ = parts
    half = got[0].shape[1]
    to_y = jnp.concatenate((to_y[:, :half] + got[0], to_y[:, half:]), axis=1)
    to_x = jnp.concatenate((to_x[:, :half], to_x[:, half:] + got[1]), axis=1)
    return (to_y, to_x), (swap(to_y, CHIPS, 2), swap(to_x, CHIPS, 1))


def add_blocks(parts, got):
    if got is None:
        return lax.psum_scatter(parts[0], CHIPS, scatter_dimension=1, tiled=True)
    return (parts[4].astype(F32) + got[0].astype(F32) + got[1].astype(F32)).astype(BF16)


def scatter_line(part):
    return lax.psum_scatter(part, LINE, scatter_dimension=0, tiled=False)


def with_peer(values):
    return jnp.concatenate((values, swap(values, CORES)), axis=0)


def fold_peer(values):
    own = values.shape[0] // 2
    sent = swap(values[own:].astype(BF16), CORES)
    return values[:own] + sent.astype(F32)


def on_device(
    tokens,
    timesteps,
    labels,
    patch_cells,
    class_table,
    ada_weight,
    ada_bias,
    qkv_weight,
    qkv_bias,
    q_gain,
    k_gain,
    out_weight,
    out_bias,
    gate_up_weight,
    gate_up_bias,
    down_weight,
    down_bias,
    cotangent,
):
    core = lax.axis_index(CORES)
    line_at = lax.axis_index(LINE)
    line = axis_len(LINE)
    data = axis_len(CHIPS) * axis_len(CORES)
    devices = data * line
    images = tokens.shape[0]
    own_images = images // line
    width = class_table.shape[1]
    chunk = ada_weight.shape[2]
    highest = lax.Precision.HIGHEST

    rows_w = qkv_weight.shape[0]
    head_cols = qkv_weight.shape[2] // 2
    ff_cols = gate_up_weight.shape[2] // 2

    def column_halves(which):
        qkv_half = lax.dynamic_slice_in_dim(qkv_weight, which * head_cols, head_cols, 2)
        out_half = lax.dynamic_slice_in_dim(out_weight, which * head_cols, head_cols, 0)
        gu_half = lax.dynamic_slice_in_dim(gate_up_weight, which * ff_cols, ff_cols, 2)
        down_half = lax.dynamic_slice_in_dim(down_weight, which * ff_cols, ff_cols, 0)
        return jnp.concatenate(
            (
                qkv_half.reshape(rows_w, 3 * head_cols),
                out_half.T,
                gu_half.reshape(rows_w, 2 * ff_cols),
                down_half.T,
            ),
            axis=1,
        )

    kept = column_halves(core)
    got = swap(column_halves(1 - core), CORES)
    both = jnp.concatenate(
        (jnp.where(core == 0, kept, got), jnp.where(core == 0, got, kept)), axis=0
    )
    attn_cols = 4 * head_cols
    held_attn = gather_line(both[:, :attn_cols])
    held_gu = gather_line(both[:, attn_cols : attn_cols + 2 * ff_cols])
    down_piece = both[:, attn_cols + 2 * ff_cols :]
    held_down = gather_line(jnp.pad(down_piece, ((0, 0), (0, PAD))))

    small_in = jnp.stack((labels, timesteps))
    small_in = lax.all_to_all(
        jnp.broadcast_to(small_in, (data,) + small_in.shape), DATA, 0, 0, tiled=True
    )
    labels_all = small_in[:, 0].reshape(data * images)
    steps_all = small_in[:, 1].reshape(data * images)
    one_hot = (labels_all[:, None] == jnp.arange(CLASSES, dtype=jnp.int32)[None, :]).astype(BF16)
    cond = jnp.dot(one_hot, class_table, preferred_element_type=F32)
    cond = cond + wave_columns(steps_all, line_at * width, width)
    cond_low = jax.nn.silu(cond).astype(BF16)
    ada_flat = ada_weight.reshape(width, 6 * chunk)
    mod_part = jnp.dot(cond_low, ada_flat, preferred_element_type=F32)
    bias_in = jnp.concatenate((qkv_bias.reshape(-1), gate_up_bias.reshape(-1))).astype(F32)
    bias_len = bias_in.shape[0]
    share = -(-bias_len // data)
    bias_in = jnp.pad(bias_in, (0, share * data - bias_len)).reshape(data, share)
    data_at = lax.axis_index(CHIPS) * axis_len(CORES) + core
    bias_in = lax.dynamic_index_in_dim(bias_in, data_at, 0, keepdims=True)
    mod_part = mod_part.reshape(devices, own_images * 6 * chunk)
    mod_part = jnp.concatenate((mod_part, jnp.broadcast_to(bias_in, (devices, share))), axis=1)
    mod_part = lax.all_to_all(mod_part, EVERY, 0, 0, tiled=True)
    bias_all = mod_part[:, own_images * 6 * chunk :].reshape(data, line, share)
    bias_all = bias_all.transpose(1, 0, 2).reshape(line, data * share)[:, :bias_len]
    mod_part = mod_part[:, : own_images * 6 * chunk]
    mod = jnp.sum(mod_part.reshape(data, line, own_images, 6, chunk), axis=1)
    mod = mod.transpose(1, 2, 0, 3).reshape(own_images, 6, D) + ada_bias.astype(F32)
    shift_a, scale_a, gate_a, shift_f, scale_f, gate_f = (mod[:, k : k + 1] for k in range(6))

    cells = lax.dynamic_slice_in_dim(patch_cells, line_at * own_images, own_images, 0)
    repeat = head_cols // HEAD_DIM
    cosines, sines = rotary_tables(with_peer(cells), repeat)
    gains = jnp.tile(jnp.stack((q_gain, k_gain)).astype(F32)[:, None], (1, 1, repeat))
    same, turn = head_tables(head_cols)

    x_rows = to_whole(after(tokens, cond_low))
    qkv_b = bias_all[:, : 6 * head_cols].reshape(line, 3, 2, head_cols)
    qkv_b = lax.dynamic_index_in_dim(qkv_b, core, 2, keepdims=False).reshape(line, 1, 3 * head_cols)
    gu_b = bias_all[:, 6 * head_cols :].reshape(line, 2, 2, ff_cols)
    gu_b = lax.dynamic_index_in_dim(gu_b, core, 2, keepdims=False).reshape(line, 1, 2 * ff_cols)
    ready = (cosines, sines, qkv_b, gu_b)
    attn_arrived, ready = lax.optimization_barrier((first_hop(held_attn), ready))
    cosines, sines, qkv_b, gu_b = ready
    _, attn_last = second_hop(attn_arrived)
    x_rows = after(x_rows, attn_last).astype(F32)
    held_gu = after(held_gu, attn_last)
    gu_arrived = first_hop(held_gu)

    attn_own = modulate(x_rows, shift_a, scale_a).astype(BF16)
    attn_peer = swap(attn_own, CORES)
    w_attn = whole_weight(held_attn, attn_arrived, attn_last)
    w_attn = w_attn.reshape(line, D, attn_cols)
    patches = x_rows.shape[1]
    rows_all = 2 * own_images * patches
    tables = (gains, cosines.reshape(rows_all, -1), sines.reshape(rows_all, -1), same, turn)
    qkv, heads_out, part_own, part_peer = attn_forward(
        after(attn_own, held_gu), attn_peer, w_attn, qkv_b, *tables
    )
    part_peer = swap(part_peer, CORES)
    gu_passed, gu_last = second_hop(gu_arrived)
    part_own = after(part_own, gu_passed, held_down)
    held_down = after(held_down[:, :, :ff_cols], gu_last)
    down_arrived = first_hop(held_down)
    attn = part_own.astype(F32) + part_peer.astype(F32) + out_bias.astype(F32)

    def as_rows(*values):
        return [value.reshape(own_images * patches, D) for value in values]

    mid = x_rows + gate_a * attn
    ffn_own = modulate(mid, shift_f, scale_f).astype(BF16)
    ffn_peer = swap(ffn_own, CORES)
    grad_out = to_whole(after(cotangent, heads_out)).astype(F32)
    d_ffn_f = gate_f * grad_out
    d_ffn_own = d_ffn_f.astype(BF16)
    d_ffn_peer = swap(d_ffn_own, CORES)
    w_gu = whole_weight(held_gu, gu_arrived, gu_last).reshape(line, D, 2 * ff_cols)
    early = line // 2
    begun = ffn_forward(0, early, ffn_own, ffn_peer, w_gu, gu_b)
    down_passed, down_last = second_hop(after(down_arrived, begun))
    gate_up, hidden = ffn_forward(
        early, line - early, after(ffn_own, down_passed), ffn_peer, w_gu, gu_b, *begun
    )
    w_down = whole_weight(held_down, down_arrived, down_last).reshape(line, D, ff_cols)
    d_gu, d_in_own, d_in_peer, gu_bias_part = ffn_backward(
        d_ffn_own, d_ffn_peer, w_down, w_gu, gate_up
    )
    d_in_peer = swap(d_in_peer, CORES)
    gu_parts, gu_got = send_diagonal(
        [(as_rows(ffn_own, ffn_peer), d_gu)]
    )
    down_parts, down_got = send_diagonal(
        [(as_rows(d_ffn_own, d_ffn_peer), after(hidden, gu_parts))]
    )
    ffn = jnp.einsum("zrf,zdf->rd", after(hidden, down_parts), w_down, preferred_element_type=F32)
    ffn = fold_peer(ffn.reshape(2 * own_images, patches, D)) + down_bias.astype(F32)
    output = to_parts((mid + gate_f * ffn).astype(BF16))

    down_bias_part = jnp.sum(d_ffn_f, axis=(0, 1))
    d_gate_f = jnp.sum(grad_out * ffn, axis=1, keepdims=True)
    d_ffn_in = after(d_in_own.astype(F32) + d_in_peer.astype(F32), gu_got)
    mid_grad, d_shift_f, d_scale_f = jax.vjp(modulate, mid, shift_f, scale_f)[1](d_ffn_in)
    d_mid = grad_out + mid_grad
    d_attn_f = gate_a * d_mid
    out_bias_part = jnp.sum(d_attn_f, axis=(0, 1))
    d_gate_a = jnp.sum(d_mid * attn, axis=1, keepdims=True)
    d_attn_own = d_attn_f.astype(BF16)
    d_attn_peer = swap(d_attn_own, CORES)
    gu_sent, gu_blocks = send_blocks(gu_parts, gu_got)
    down_sent, down_blocks = send_blocks(down_parts, after(down_got, gu_sent))
    d_qkv, d_in_own, d_in_peer, qkv_bias_part, gain_part = attn_backward(
        after(d_attn_own, gu_sent, down_sent), d_attn_peer, w_attn, qkv, *tables
    )
    d_in_peer = swap(d_in_peer, CORES)
    g_gu = add_blocks(gu_parts if gu_blocks is not None else gu_sent, after(gu_blocks, d_qkv))
    attn_parts, attn_got = send_diagonal(
        [
            (as_rows(attn_own, attn_peer), after(d_qkv, output, g_gu)),
            (as_rows(d_attn_own, d_attn_peer), heads_out),
        ]
    )
    g_gu = scatter_line(g_gu)
    qkv_bias_part, gain_part = after((qkv_bias_part, gain_part), attn_parts)
    gain_part = gain_part.reshape(2, repeat, HEAD_DIM).sum(axis=1)
    d_attn_in = d_in_own.astype(F32) + d_in_peer.astype(F32)
    row_grad, d_shift_a, d_scale_a = jax.vjp(modulate, x_rows, shift_a, scale_a)[1](d_attn_in)
    tokens_sent = (d_mid + row_grad).astype(BF16)

    g_down = add_blocks(down_parts if down_blocks is not None else down_sent, after(down_blocks, tokens_sent))
    attn_got = after(attn_got, g_down)
    g_down = scatter_line(g_down)
    attn_got = after(attn_got, g_gu, tokens_sent)
    tokens_grad = to_parts(tokens_sent)
    attn_sent, attn_blocks = send_blocks(attn_parts, attn_got)
    d_mod = jnp.concatenate(
        (d_shift_a, d_scale_a, d_gate_a, d_shift_f, d_scale_f, d_gate_f), axis=1
    )
    d_mod, tokens_grad = lax.optimization_barrier((after(d_mod, attn_sent), tokens_grad))
    ada_bias_part = jnp.sum(d_mod, axis=0)
    d_mod_low = d_mod.astype(BF16).reshape(own_images, 6, data, chunk).transpose(2, 0, 1, 3)
    d_mod_low = jnp.broadcast_to(
        d_mod_low[:, None], (data, line, own_images, 6, chunk)
    ).reshape(devices, own_images * 6 * chunk)
    d_mod_all = lax.all_to_all(d_mod_low, EVERY, 0, 0, tiled=True)
    d_mod_all = d_mod_all.reshape(data * images, 6 * chunk)
    g_ada = jnp.einsum("bc,be->ce", cond_low, d_mod_all, preferred_element_type=F32)
    g_ada = g_ada.reshape(width, 6, chunk)
    d_silu = jnp.einsum("be,ce->bc", d_mod_all, ada_flat, preferred_element_type=F32)
    d_cond = jax.vjp(jax.nn.silu, cond)[1](d_silu)[0]

    def by_core(part, groups, cols):
        spread = jnp.zeros((line, groups, 2, cols), F32)
        return lax.dynamic_update_slice(
            spread, part.reshape(line, groups, 1, cols), (0, 0, core, 0)
        )

    parts = (
        by_core(qkv_bias_part, 3, head_cols),
        by_core(gu_bias_part, 2, ff_cols),
        ada_bias_part,
        out_bias_part,
        down_bias_part,
        gain_part[0],
        gain_part[1],
    )
    flat = jnp.concatenate([part.reshape(-1) for part in parts])
    count = flat.shape[0]
    flat = jnp.concatenate((flat, d_cond.reshape(-1)))
    flat = sum_by_swaps(sum_by_swaps(flat, CORES), CHIPS)
    g_attn = add_blocks(attn_parts, attn_blocks)
    g_attn = after(g_attn, g_gu, g_down)
    g_attn = scatter_line(g_attn)
    d_cond = flat[count:].reshape(d_cond.shape)
    flat = sum_by_swaps(flat[:count], LINE)
    sums = []
    at = 0
    for part in parts:
        sums.append(flat[at : at + part.size].reshape(part.shape))
        at += part.size
    qkv_bias_grad = lax.dynamic_index_in_dim(sums[0], line_at, 0, keepdims=False)
    gu_bias_grad = lax.dynamic_index_in_dim(sums[1], line_at, 0, keepdims=False)
    tokens_grad = tokens_grad.astype(F32)
    table_grad = jnp.dot(one_hot.astype(F32).T, d_cond, precision=highest)

    def own_rows(part):
        kept = lax.dynamic_slice_in_dim(part, core * rows_w, rows_w, 0)
        got = swap(lax.dynamic_slice_in_dim(part, (1 - core) * rows_w, rows_w, 0), CORES)
        low_half = jnp.where(core == 0, kept, got).astype(F32)
        high_half = jnp.where(core == 0, got, kept).astype(F32)

        def joined(first, groups, cols):
            halves = [
                half[:, first : first + groups * cols].reshape(rows_w, groups, cols)
                for half in (low_half, high_half)
            ]
            return jnp.concatenate(halves, axis=2)

        return joined

    joined = own_rows(g_gu)
    g_gu = joined(0, 2, ff_cols)
    joined = own_rows(g_down)
    g_down = joined(0, 1, ff_cols)[:, 0].T
    joined = own_rows(g_attn)
    g_qkv = jnp.stack([joined(k * head_cols, 1, head_cols)[:, 0] for k in range(3)], axis=1)
    g_out = joined(3 * head_cols, 1, head_cols)[:, 0].T
    return (
        output,
        tokens_grad,
        table_grad,
        g_ada,
        sums[2],
        g_qkv,
        qkv_bias_grad.reshape(qkv_bias.shape),
        sums[5],
        sums[6],
        g_out,
        sums[3],
        g_gu,
        gu_bias_grad.reshape(gate_up_bias.shape),
        g_down,
        sums[4],
    )


def solution(mesh):
    chips = mesh.shape["dp"] // 2
    finer = Mesh(mesh.devices.reshape(chips, 2, mesh.shape["tensor"]), EVERY)
    in_specs = (
        P(DATA, LINE, None),
        P(DATA),
        P(DATA),
        P(DATA, None),
        P(None, LINE),
        P(LINE, None, DATA),
        P(),
        P(DATA, None, LINE),
        P(None, LINE),
        P(),
        P(),
        P(LINE, DATA),
        P(),
        P(DATA, None, LINE),
        P(None, LINE),
        P(LINE, DATA),
        P(),
        P(DATA, LINE, None),
    )
    out_specs = (
        P(DATA, LINE, None),
        P(DATA, LINE, None),
        P(None, LINE),
        P(LINE, None, DATA),
        P(),
        P(DATA, None, LINE),
        P(None, LINE),
        P(),
        P(),
        P(LINE, DATA),
        P(),
        P(DATA, None, LINE),
        P(None, LINE),
        P(LINE, DATA),
        P(),
    )
    return jax.shard_map(
        on_device, mesh=finer, in_specs=in_specs, out_specs=out_specs, check_vma=False
    )
```
